128 devices in a mesh: dp: 8 (over x, core), seq: 16 (over y, z).
Axes of the slice: x: 4, y: 4, z: 4, core: 2. Of those that a mesh axis runs over, the one named last changes fastest.
Arguments:
- events: bfloat16 [8, 4096, 1024], P('dp', 'seq'), may hold values from -6 to 6
- cotangent: bfloat16 [8, 4096, 1024], P('dp', 'seq'), may hold values from -6 to 6
- hist_lengths: int32 [8, 8], P('dp'), may hold values from 1 to 1024, 4096 in all within a row
- w_in: bfloat16 [1024, 4096], replicated, may hold values from -0.1875 to 0.1875
- w_out: bfloat16 [1024, 1024], replicated, may hold values from -0.1875 to 0.1875
Outputs:
- grad_events: bfloat16 [8, 4096, 1024], P('dp', 'seq')
- grad_w_in: bfloat16 [1024, 4096], P(('dp', 'seq'))
- grad_w_out: bfloat16 [1024, 1024], P(('dp', 'seq'))
The draws below stay inside these ranges and needn't reach their ends.
Inputs may be any that keep to these rules, and one draw needn't show every extreme that they name: `hist_lengths`: each row sums to 4096; some history in each row has exactly 1024 events.
All inputs are finite; a program needn't handle non-finite values.
Results may differ from the reference program's by a relative error of at most 0.014.
Values may be sent and summed in bfloat16 or wider, within the bound.
No kernel may reach another device: no remote copies, remote signals or barrier semaphores. Data moves between devices by JAX's collectives and lax.ppermute only.
A program may use at most 128 MiB of HBM per device.

```python
import math
import jax
import jax.numpy as jnp
import numpy as np
from jax import lax

D = 1024
HEADS = 8
ROWS_DEV = 256
SPAN = 4
LONGEST = 1024
GROUP = 4096
USERS = 8
N_DP = 8
N_SEQ = 16


def strengthened(entries, rng, source, target, blocks, factor):
    owner, partner = [(jnp.arange(entries.shape[axis_at]) // (entries.shape[axis_at] // blocks)).reshape([-1 if axis == axis_at else 1 for axis in range(entries.ndim)]) for axis_at in (source, target)]
    chosen = jax.random.permutation(rng, blocks)[partner]
    strong = (owner == chosen) | (owner == (partner + blocks // 2) % blocks)
    return jnp.where(strong, factor * entries, entries)


def shard_levels(stream_key, shape, shards, smallest, high):
    factor_of, own = 1.0, jax.random.fold_in(stream_key, 6)
    for position, blocks in shards:
        steps = jnp.exp(jax.random.uniform(jax.random.fold_in(own, position), (blocks,), jnp.float32, smallest / len(shards), high / len(shards)))
        factor_of = factor_of * jnp.repeat(steps, shape[position] // blocks).reshape([-1 if axis == position else 1 for axis in range(len(shape))])
    return factor_of


def length_profile(number_of, total, most, slope):
    portions = [(1 << 20) // math.isqrt(rank ** slope) + 1 for rank in range(2, number_of + 1)]
    rest, counts = total - most - (number_of - 1), [1] * (number_of - 1)
    while rest > 0:
        free = [i for i in range(number_of - 1) if counts[i] < most]
        pool, left = sum([portions[i] for i in free]), rest
        for i in free:
            more = min(most - counts[i], max(1, left * portions[i] // pool), rest)
            counts[i] = counts[i] + more
            rest = rest - more
    return np.array([most] + counts)


def ragged(stream_key, amount, total, limit, lean):
    if amount == 2:
        one = jax.random.randint(stream_key, (), max(1, total - limit), min(limit, total - 1) + 1)
        return jnp.stack([one, total - one])
    sizes = jnp.asarray(length_profile(amount, total, limit, lean), jnp.int32)
    pairs = (amount - 1) // 2
    giver, receiver = sizes[1:1 + 2 * pairs:2], sizes[2:2 + 2 * pairs:2]
    slack = jnp.minimum(giver - 1, limit - receiver)
    shifted = jax.random.randint(jax.random.fold_in(stream_key, 1), (pairs,), 0, 1 << 20) % (slack + 1)
    sizes = sizes.at[1:1 + 2 * pairs:2].set(giver - shifted).at[2:2 + 2 * pairs:2].set(receiver + shifted)
    return sizes[jax.random.permutation(jax.random.fold_in(stream_key, 2), amount)]


def bell_draw(stream_key, extent, deviation, reach, shards=(), held_as=jnp.bfloat16):
    result = deviation * jax.random.normal(stream_key, extent, jnp.float32)
    if shards:
        result = result * shard_levels(stream_key, extent, shards, -0.22, 0.18)
    return jnp.clip(result, -reach, reach).astype(held_as)


def heavy_noise(stream_key, extent, scale, limit, pieces, heavy, kind=jnp.bfloat16):
    result = scale * jax.random.normal(stream_key, extent, jnp.float32)
    if pieces:
        result = result * shard_levels(stream_key, extent, pieces, -0.22, 0.18)
    return jnp.clip(strengthened(result, jax.random.fold_in(stream_key, 3), *heavy), -limit, limit).astype(kind)


def setup_inputs(seed: int = 0) -> dict:
    key_list = jax.random.split(jax.random.key(seed), 6)
    events = heavy_noise(key_list[0], (N_DP, GROUP, D), 1.0, 6.0, ((0, 8), (1, 16)), (1, 2, 16, 2.0))
    cotangent = bell_draw(key_list[1], (N_DP, GROUP, D), 1.0, 6.0, ((0, 8), (1, 16)))
    hist_lengths = jax.vmap(lambda own: ragged(own, USERS, GROUP, LONGEST, 2))(jax.random.split(key_list[2], N_DP)).reshape((N_DP, USERS)).astype(jnp.int32)
    w_in = bell_draw(key_list[3], (D, 4 * D), D ** -0.5, 0.1875)
    w_out = bell_draw(key_list[4], (D, D), D ** -0.5, 0.1875)
    return dict(events=events, cotangent=cotangent, hist_lengths=hist_lengths, w_in=w_in, w_out=w_out)


def segment_ids(positions, doc_ends):
    return lax.optimization_barrier(jnp.sum((positions[:, None] >= doc_ends[None, :]).astype(jnp.int32), axis=1)).astype(jnp.int32)

def pair_keep(query_pos, key_pos, doc_ends):
    same = segment_ids(query_pos, doc_ends)[:, None] == segment_ids(key_pos, doc_ends)[None, :]
    keep = same & (key_pos[None, :] <= query_pos[:, None]) & (key_pos[None, :] >= 0)
    return keep.astype(jnp.float32)[None]

def pair_output(query_rows, key_rows, value_rows, query_pos, key_pos, doc_ends):
    keep = pair_keep(query_pos, key_pos, doc_ends)
    scores = jnp.einsum('qhd,khd->hqk', query_rows.astype(jnp.float32), key_rows.astype(jnp.float32))
    weights_bf = (scores * jax.nn.sigmoid(scores) * keep / ROWS_DEV).astype(jnp.bfloat16)
    return jnp.einsum('hqk,khd->qhd', weights_bf.astype(jnp.float32), value_rows.astype(jnp.float32))

def pair_grads(query_rows, grad_rows, key_rows, value_rows, query_pos, key_pos, doc_ends):
    keep = pair_keep(query_pos, key_pos, doc_ends)
    scores = jnp.einsum('qhd,khd->hqk', query_rows.astype(jnp.float32), key_rows.astype(jnp.float32))
    sigma = jax.nn.sigmoid(scores)
    weights_bf = (scores * sigma * keep / ROWS_DEV).astype(jnp.bfloat16).astype(jnp.float32)
    grad_weights = jnp.einsum('qhd,khd->hqk', grad_rows.astype(jnp.float32), value_rows.astype(jnp.float32))
    grad_scores = (grad_weights * sigma * (1.0 + scores * (1.0 - sigma)) * keep / ROWS_DEV).astype(jnp.bfloat16).astype(jnp.float32)
    grad_query = jnp.einsum('hqk,khd->qhd', grad_scores, key_rows.astype(jnp.float32))
    grad_key = jnp.einsum('hqk,qhd->khd', grad_scores, query_rows.astype(jnp.float32))
    grad_value = jnp.einsum('hqk,qhd->khd', weights_bf, grad_rows.astype(jnp.float32))
    return (grad_query, grad_key, grad_value)

def group_backward(tokens, upstream, lengths_row, w_in, w_out):
    head_dim = D // HEADS
    padding = SPAN * ROWS_DEV
    window = padding + ROWS_DEV
    doc_ends = jnp.cumsum(lengths_row).astype(jnp.int32)
    proj = jnp.dot(tokens, w_in, preferred_element_type=jnp.float32)
    sigma_proj = jax.nn.sigmoid(proj)
    act_bf = (proj * sigma_proj).astype(jnp.bfloat16)
    parts = act_bf.reshape(GROUP, 4, HEADS, head_dim)
    gate_rows = parts[:, 0].reshape(GROUP, D).astype(jnp.float32)
    value_rows = parts[:, 1]
    query_rows = parts[:, 2]
    key_rows = parts[:, 3]
    blank_rows = jnp.zeros((padding, HEADS, head_dim), jnp.bfloat16)
    key_padded = jnp.concatenate([blank_rows, key_rows], axis=0)
    value_padded = jnp.concatenate([blank_rows, value_rows], axis=0)

    def window_rows(first_row):
        query_pos = (first_row + jnp.arange(ROWS_DEV, dtype=jnp.int32)).astype(jnp.int32)
        key_pos = (first_row - padding + jnp.arange(window, dtype=jnp.int32)).astype(jnp.int32)
        query_blk = lax.dynamic_slice_in_dim(query_rows, first_row, ROWS_DEV, 0)
        key_blk = lax.dynamic_slice_in_dim(key_padded, first_row, window, 0)
        value_blk = lax.dynamic_slice_in_dim(value_padded, first_row, window, 0)
        return (query_blk, key_blk, value_blk, query_pos, key_pos)

    def forward_block(shard_index):
        first_row = (shard_index * ROWS_DEV).astype(jnp.int32)
        query_blk, key_blk, value_blk, query_pos, key_pos = window_rows(first_row)
        return pair_output(query_blk, key_blk, value_blk, query_pos, key_pos, doc_ends)
    attended = lax.map(forward_block, jnp.arange(N_SEQ, dtype=jnp.int32)).reshape(GROUP, D)
    center = attended - lax.optimization_barrier(jnp.mean(attended, axis=1, keepdims=True))
    inv_std = lax.rsqrt(lax.optimization_barrier(jnp.mean(center * center, axis=1, keepdims=True)) + 1e-06)
    normed = center * inv_std
    gated_bf = (normed * gate_rows).astype(jnp.bfloat16)
    grad_wout = jnp.dot(gated_bf.T, upstream, preferred_element_type=jnp.float32)
    grad_gated = jnp.dot(upstream, w_out.T, preferred_element_type=jnp.float32)
    grad_gate = grad_gated * normed
    grad_normed = grad_gated * gate_rows
    grad_att = inv_std * (grad_normed - lax.optimization_barrier(jnp.mean(grad_normed, axis=1, keepdims=True)) - normed * lax.optimization_barrier(jnp.mean(grad_normed * normed, axis=1, keepdims=True)))
    grad_att_bf = grad_att.astype(jnp.bfloat16).reshape(GROUP, HEADS, head_dim)

    def backward_block(shard_index, carry):
        grad_q_all, grad_k_pad, grad_v_pad = carry
        first_row = (shard_index * ROWS_DEV).astype(jnp.int32)
        query_blk, key_blk, value_blk, query_pos, key_pos = window_rows(first_row)
        grad_blk = lax.dynamic_slice_in_dim(grad_att_bf, first_row, ROWS_DEV, 0)
        part_q, part_k, part_v = pair_grads(query_blk, grad_blk, key_blk, value_blk, query_pos, key_pos, doc_ends)
        grad_q_all = lax.dynamic_update_slice_in_dim(grad_q_all, part_q, first_row, 0)
        grad_k_pad = lax.dynamic_update_slice_in_dim(grad_k_pad, lax.dynamic_slice_in_dim(grad_k_pad, first_row, window, 0) + part_k, first_row, 0)
        grad_v_pad = lax.dynamic_update_slice_in_dim(grad_v_pad, lax.dynamic_slice_in_dim(grad_v_pad, first_row, window, 0) + part_v, first_row, 0)
        return (grad_q_all, grad_k_pad, grad_v_pad)
    start_carry = (jnp.zeros((GROUP, HEADS, head_dim), jnp.float32), jnp.zeros((padding + GROUP, HEADS, head_dim), jnp.float32), jnp.zeros((padding + GROUP, HEADS, head_dim), jnp.float32))
    grad_q_all, grad_k_pad, grad_v_pad = lax.fori_loop(0, N_SEQ, backward_block, start_carry)
    grad_query = grad_q_all.reshape(GROUP, D)
    grad_key = grad_k_pad[padding:].reshape(GROUP, D)
    grad_value = grad_v_pad[padding:].reshape(GROUP, D)
    grad_act = jnp.concatenate([grad_gate, grad_value, grad_query, grad_key], axis=1)
    grad_proj_bf = (grad_act * sigma_proj * (1.0 + proj * (1.0 - sigma_proj))).astype(jnp.bfloat16)
    grad_win = jnp.dot(tokens.T, grad_proj_bf, preferred_element_type=jnp.float32)
    grad_tokens = (jnp.dot(grad_proj_bf, w_in.T, preferred_element_type=jnp.float32) + upstream.astype(jnp.float32)).astype(jnp.bfloat16)
    return (grad_tokens, grad_win, grad_wout)

def reference(events, cotangent, hist_lengths, w_in, w_out):

    def step(carry, item):
        tokens, upstream, lengths_row = item
        grad_tokens, grad_win, grad_wout = group_backward(tokens, upstream, lengths_row, w_in, w_out)
        return ((carry[0] + grad_win, carry[1] + grad_wout), grad_tokens)
    start = (jnp.zeros((D, 4 * D), jnp.float32), jnp.zeros((D, D), jnp.float32))
    totals, grad_events = lax.scan(step, start, (events, cotangent, hist_lengths))
    return (grad_events, totals[0].astype(jnp.bfloat16), totals[1].astype(jnp.bfloat16))
```

```python
import jax
import jax.numpy as jnp
from jax import lax
from jax.experimental import pallas as pl
from jax.experimental.pallas import tpu as pltpu
from jax.sharding import Mesh
from jax.sharding import PartitionSpec as P

BLK = 256
NB = 4
DH = 128
GRP = NB * BLK
D = 1024
F32 = jnp.float32
BF16 = jnp.bfloat16
SCALE = 1.0 / 256.0
VMEM = pl.BlockSpec(memory_space=pltpu.VMEM)
SMEM = pl.BlockSpec(memory_space=pltpu.SMEM)


def call(body, outs, n_in, flops, nbytes, scratch=()):
    return pl.pallas_call(
        body,
        out_shape=outs,
        in_specs=[SMEM] + [VMEM] * n_in,
        out_specs=jax.tree.map(lambda _: VMEM, outs),
        scratch_shapes=scratch,
        compiler_params=pltpu.CompilerParams(vmem_limit_bytes=48 * 1024 * 1024),
        cost_estimate=pl.CostEstimate(flops=flops, bytes_accessed=nbytes, transcendentals=0),
    )


def nt(a, b):
    return lax.dot_general(a, b, (((1,), (1,)), ((), ())), preferred_element_type=F32)


def nn(a, b):
    return lax.dot_general(a, b, (((1,), (0,)), ((), ())), preferred_element_type=F32)


def tn(a, b):
    return lax.dot_general(a, b, (((0,), (0,)), ((), ())), preferred_element_type=F32)


def history_ends(info):
    ends, total = [], jnp.int32(0)
    for k in range(8):
        total = total + info[k]
        ends.append(total)
    return ends


def start_of(pos, ends):
    start = jnp.zeros_like(pos)
    for e in ends:
        start = jnp.where(pos >= e, e, start)
    return start


def end_of(pos, ends):
    end = ends[-1]
    for e in reversed(ends):
        end = jnp.where(e > pos, e, end)
    return end


def rows(i):
    return pl.ds(pl.multiple_of(i * BLK, BLK), BLK)


def head(h, base=0):
    return slice(base + h * DH, base + (h + 1) * DH)


def project_body(info, ev, wk, wv, wq, wg, kv, q, g, dsig):
    x = ev[...]
    for p, w in enumerate((wg, wv, wq, wk)):
        proj = nn(x, w[...])
        sig = 0.5 + 0.5 * jnp.tanh(0.5 * proj)
        act = (proj * sig).astype(BF16)
        if p == 0:
            g[...] = act
        elif p == 1:
            kv[:, BLK:] = act
        elif p == 2:
            q[...] = (0.5 * act.astype(F32)).astype(BF16)
        else:
            kv[:, :BLK] = act
        dsig[:, p * BLK : (p + 1) * BLK] = (sig * (1.0 + proj * (1.0 - sig))).astype(BF16)


def keep_rows(qpos, kpos, ends):
    r = qpos + lax.broadcasted_iota(jnp.int32, (BLK, 1), 0)
    c = kpos + lax.broadcasted_iota(jnp.int32, (1, BLK), 1)
    return jnp.where((c >= start_of(r, ends)) & (c <= r), SCALE, 0.0)


def keep_cols(qpos, kpos, ends):
    r = qpos + lax.broadcasted_iota(jnp.int32, (1, BLK), 1)
    c = kpos + lax.broadcasted_iota(jnp.int32, (BLK, 1), 0)
    return jnp.where((c >= start_of(r, ends)) & (c <= r), SCALE, 0.0)


def attend(q, kv, att, i, j, keep):
    for h in range(2):
        u = nt(q[rows(i), head(h)], kv[rows(j), head(h)])
        w = (u * (1.0 + jnp.tanh(u)) * keep).astype(BF16)
        att[rows(i), head(h)] += nn(w, kv[rows(j), head(h, BLK)])


def forward_local_body(info, *refs):
    q_in, kv_in = refs[0:4], refs[4:8]
    q, kv, att = refs[8:]
    ends = history_ends(info)
    base = info[8] * GRP
    for k in range(NB):
        at = rows(lax.rem(info[9] + k, NB))
        q[at, :] = q_in[k][...]
        kv[at, :] = kv_in[k][...]
    att[...] = jnp.zeros_like(att)

    def over_i(i, _):
        qpos = base + i * BLK
        first = jnp.maximum(start_of(qpos, ends) - base, 0) // BLK

        def over_j(j, _):
            attend(q, kv, att, i, j, keep_rows(qpos, base + j * BLK, ends))
            return 0

        return lax.fori_loop(first, i + 1, over_j, 0)

    lax.fori_loop(0, NB, over_i, 0)


def halo_first(i, qpos, prev, ends):
    start = start_of(qpos, ends)
    return jnp.where(start >= prev + GRP, NB, jnp.maximum((start - prev) // BLK, i))


def forward_halo_body(info, *refs):
    q, att_in, wout = refs[0:3]
    kv_in, cot, gate_in = refs[3:7], refs[7:11], refs[11:15]
    att, kv, gg, gate, stats = refs[15:20]
    ends = history_ends(info)
    base = info[8] * GRP
    prev = base - GRP
    att[...] = att_in[...]
    for k in range(NB):
        at = rows(lax.rem(info[9] + k, NB))
        kv[at, :] = kv_in[k][...]
        gate[at, :] = gate_in[k][...]
        gg[at, :] = nt(cot[k][...], wout[...])

    def over_i(i, _):
        qpos = base + i * BLK

        def over_j(j, _):
            attend(q, kv, att, i, j, keep_rows(qpos, prev + j * BLK, ends))
            return 0

        return lax.fori_loop(halo_first(i, qpos, prev, ends), NB, over_j, 0)

    lax.fori_loop(0, NB, over_i, 0)
    a = att[...]
    gn = gg[...] * gate[...].astype(F32)
    mean = jnp.sum(a, axis=1, keepdims=True) / BLK
    cent = a - mean
    m2 = jnp.sum(cent * cent, axis=1, keepdims=True)
    g1 = jnp.sum(gn, axis=1, keepdims=True)
    ga = jnp.sum(gn * cent, axis=1, keepdims=True)
    lane = lax.broadcasted_iota(jnp.int32, (GRP, DH), 1)
    packed = jnp.where(lane == 0, mean, jnp.where(lane == 1, m2, jnp.where(lane == 2, g1, ga)))
    stats[...] = packed.T[:8, :]


def norm_body(info, *refs):
    att, gg, gate = refs[0:3]
    stats, dsig = refs[3:7], refs[7:11]
    gatt, gated, gp, table = refs[11:15]
    parts = [s[...] for s in stats]
    mean = (parts[0][0:1] + parts[1][0:1] + parts[2][0:1] + parts[3][0:1]) * 0.25
    m2 = jnp.zeros_like(mean)
    g1 = jnp.zeros_like(mean)
    ga = jnp.zeros_like(mean)
    for p in parts:
        off = p[0:1] - mean
        m2 = m2 + p[1:2] + BLK * off * off
        g1 = g1 + p[2:3]
        ga = ga + p[3:4] + off * p[2:3]
    inv = lax.rsqrt(m2 / D + 1e-6)
    row = lax.broadcasted_iota(jnp.int32, (DH, GRP), 0)
    cols = jnp.where(row == 0, mean, jnp.where(row == 1, inv, jnp.where(row == 2, g1 / D, ga * inv / D)))
    table[...] = cols.T
    for k in range(NB):
        at = rows(lax.rem(info[9] + k, NB))
        t = table[at, :]
        mean_c, inv_c, g1_c, ga_c = (t[:, n : n + 1] for n in range(4))
        normed = (att[at, :] - mean_c) * inv_c
        g = gate[at, :].astype(F32)
        grad_gated = gg[at, :]
        gatt[at, :] = (inv_c * (grad_gated * g - g1_c - normed * ga_c)).astype(BF16)
        gated[at, :] = (normed * g).astype(BF16)
        gp[at, :] = (grad_gated * normed * dsig[k][:, 0:BLK].astype(F32)).astype(BF16)


def early_weights_body(info, *refs):
    ev, cot = refs[0:4], refs[4:8]
    gated, gp = refs[8:10]
    send, keep, acc_in, acc_out = refs[10:14]
    for k in range(NB):
        at = rows(lax.rem(info[9] + k, NB))
        part_in = tn(ev[k][...], gp[at, :])
        part_out = tn(gated[at, :], cot[k][...])
        if k:
            part_in += acc_in[...]
            part_out += acc_out[...]
        acc_in[...] = part_in
        acc_out[...] = part_out
    for x in range(4):
        for out, c, kind in ((send, 1 - info[10], BF16), (keep, info[10], F32)):
            big = pl.multiple_of((x * 2 + c) * 128, 128)
            small = pl.multiple_of((x * 2 + c) * 32, 32)
            out[x, 0:128, :] = acc_in[pl.ds(big, 128), :].astype(kind)
            for n in range(4):
                out[x, 128 + 32 * n : 160 + 32 * n, :] = acc_out[
                    pl.ds(small, 32), n * BLK : (n + 1) * BLK
                ].astype(kind)


def late_weights_body(info, *refs):
    ev = refs[0:4]
    gp_q, gp_kv = refs[4:6]
    send, keep, acc = refs[6:9]
    for k in range(NB):
        at = rows(lax.rem(info[9] + k, NB))
        x = ev[k][...]
        for n, gp, lanes in ((0, gp_kv, slice(BLK, 2 * BLK)), (1, gp_q, slice(0, BLK)), (2, gp_kv, slice(0, BLK))):
            part = tn(x, gp[at, lanes])
            cols = slice(n * BLK, (n + 1) * BLK)
            acc[:, cols] = part if k == 0 else acc[:, cols] + part
    for x in range(4):
        for out, c, kind in ((send, 1 - info[10], BF16), (keep, info[10], F32)):
            at = pl.multiple_of((x * 2 + c) * 128, 128)
            out[x, :, :] = acc[pl.ds(at, 128), :].astype(kind)


def silu_parts(u):
    t = jnp.tanh(u)
    a = 1.0 + t
    ut = u * t
    return u + ut, a * ((1.0 + u) - ut)


def key_side(q, g, kv, dkv, dq, i, j, keep):
    half = keep * 0.5
    for h in range(2):
        qi, gi = q[rows(i), head(h)], g[rows(i), head(h)]
        kj, vj = kv[rows(j), head(h)], kv[rows(j), head(h, BLK)]
        silu, slope = silu_parts(nt(kj, qi))
        w = (silu * keep).astype(BF16)
        ds = (nt(vj, gi) * slope * half).astype(BF16)
        dkv[rows(j), head(h, BLK)] += nn(w, gi)
        dkv[rows(j), head(h)] += nn(ds, qi)
        if dq is not None:
            dq[rows(i), head(h)] += tn(ds, kj)


def query_side(q, g, kv, dq, i, j, keep):
    half = keep * 0.5
    for h in range(2):
        kj, vj = kv[rows(j), head(h)], kv[rows(j), head(h, BLK)]
        slope = silu_parts(nt(q[rows(i), head(h)], kj))[1]
        ds = (nt(g[rows(i), head(h)], vj) * slope * half).astype(BF16)
        dq[rows(i), head(h)] += nn(ds, kj)


def backward_local_body(info, *refs):
    q, g, kv, kv_prev = refs[0:4]
    dsig = refs[4:8]
    gp_q, dkv, dq = refs[8:11]
    ends = history_ends(info)
    base = info[8] * GRP
    prev = base - GRP
    dq[...] = jnp.zeros_like(dq)
    dkv[...] = jnp.zeros_like(dkv)

    def over_j(j, _):
        kpos = base + j * BLK
        last = jnp.minimum((end_of(kpos + BLK - 1, ends) - 1 - base) // BLK, NB - 1)

        def over_i(i, _):
            key_side(q, g, kv, dkv, dq, i, j, keep_cols(base + i * BLK, kpos, ends))
            return 0

        return lax.fori_loop(j, last + 1, over_i, 0)

    lax.fori_loop(0, NB, over_j, 0)

    def halo_i(i, _):
        qpos = base + i * BLK

        def halo_j(j, _):
            query_side(q, g, kv_prev, dq, i, j, keep_rows(qpos, prev + j * BLK, ends))
            return 0

        return lax.fori_loop(halo_first(i, qpos, prev, ends), NB, halo_j, 0)

    lax.fori_loop(0, NB, halo_i, 0)
    for k in range(NB):
        at = rows(lax.rem(info[9] + k, NB))
        gp_q[at, :] = (dq[at, :] * dsig[k][:, 2 * BLK : 3 * BLK].astype(F32)).astype(BF16)


def backward_later_body(info, *refs):
    q, g, kv, dkv_in = refs[0:4]
    dsig = refs[4:8]
    gp_kv, dkv = refs[8:10]
    ends = history_ends(info)
    base = info[8] * GRP
    later = base + GRP
    dkv[...] = dkv_in[...]

    def over_j(j, _):
        kpos = base + j * BLK
        end = end_of(kpos + BLK - 1, ends)
        count = jnp.where(end > later, jnp.minimum((end - 1 - later) // BLK, j) + 1, 0)

        def over_i(i, _):
            key_side(q, g, kv, dkv, None, i, j, keep_cols(later + i * BLK, kpos, ends))
            return 0

        return lax.fori_loop(0, count, over_i, 0)

    lax.fori_loop(0, NB, over_j, 0)
    for k in range(NB):
        at = rows(lax.rem(info[9] + k, NB))
        dk = 2.0 * dkv[at, 0:BLK]
        gp_kv[at, 0:BLK] = (dk * dsig[k][:, 3 * BLK :].astype(F32)).astype(BF16)
        gp_kv[at, BLK:] = (dkv[at, BLK:] * dsig[k][:, BLK : 2 * BLK].astype(F32)).astype(BF16)


def input_early_body(gp_g, gp_q, w_g, w_q, cot, out):
    part = nt(gp_g[0], w_g[...]) + nt(gp_q[0], w_q[...])

    @pl.when(pl.program_id(0) == 0)
    def _():
        out[...] = part + cot[...].astype(F32)

    @pl.when(pl.program_id(0) > 0)
    def _():
        out[...] += part


def input_late_body(gp_kv, w_k, w_v, early, out, acc):
    part = nt(gp_kv[0, :, :BLK], w_k[...]) + nt(gp_kv[0, :, BLK:], w_v[...])

    @pl.when(pl.program_id(0) == 0)
    def _():
        acc[...] = part + early[...]

    @pl.when(pl.program_id(0) > 0)
    def _():
        acc[...] += part

    @pl.when(pl.program_id(0) == 3)
    def _():
        out[...] = acc[...].astype(BF16)


def along(x, axis, d):
    return lax.ppermute(x, axis, [(i, (i + d) % 4) for i in range(4)])


def swap(x):
    return lax.ppermute(x, "c", [(0, 1), (1, 0)])


def gather_z(x):
    return [x, along(x, "z", -1), along(x, "z", 2), along(x, "z", 1)]


def to_owner(x):
    route = []
    for xc in range(8):
        for y in range(4):
            for z in range(4):
                src = (xc * 4 + y) * 4 + z
                dst = ((2 * z + xc // 4) * 4 + xc % 4) * 4 + y
                route.append((src, dst))
    return lax.ppermute(x, ("x", "c", "y", "z"), route)


def f32(shape):
    return jax.ShapeDtypeStruct(shape, F32)


def bf16(shape):
    return jax.ShapeDtypeStruct(shape, BF16)


def reduce_xc(send, keep):
    summed = (keep + swap(send).astype(F32)).astype(BF16)
    got = lax.all_to_all(summed, "x", 0, 0)
    return jnp.sum(got.astype(F32), axis=0)


def body(events, cotangent, hist, w_in, w_out):
    z = lax.axis_index("z")
    info = jnp.concatenate(
        [hist[0], jnp.stack([lax.axis_index("y"), z, lax.axis_index("c")]).astype(jnp.int32)]
    )
    ev, cot = events[0], cotangent[0]
    evs = gather_z(ev)
    wg, wv, wq, wk = (lax.dynamic_slice(w_in, (0, p * D + z * BLK), (D, BLK)) for p in range(4))
    wout = lax.dynamic_slice(w_out, (z * BLK, 0), (BLK, D))
    kvs, qs, gs, dsigs, kv_prevs = [], [], [], [], []
    for k in range(NB):
        kv, q, g, dsig = call(
            project_body,
            (bf16((BLK, 2 * BLK)), bf16((BLK, BLK)), bf16((BLK, BLK)), bf16((BLK, 4 * BLK))),
            5, 2 * BLK * D * D, 4 << 20,
        )(info, evs[k], wk, wv, wq, wg)
        kvs.append(kv)
        qs.append(q)
        gs.append(g)
        dsigs.append(dsig)
        kv_prevs.append(along(kv, "y", 1))
    cots = gather_z(cot)
    q, kv, att = call(
        forward_local_body, (bf16((GRP, BLK)), bf16((GRP, 2 * BLK)), f32((GRP, BLK))), 8, 5 << 30, 4 << 20
    )(info, *qs, *kvs)
    q_next = along(q, "y", -1)
    att, kv_prev, gg, gate, stats = call(
        forward_halo_body,
        (f32((GRP, BLK)), bf16((GRP, 2 * BLK)), f32((GRP, BLK)), bf16((GRP, BLK)), f32((8, GRP))),
        15, 5 << 30, 4 << 20,
    )(info, q, att, wout, *kv_prevs, *cots, *gs)
    gatt, gated, gp_g = call(
        norm_body, (bf16((GRP, BLK)),) * 3, 11, 1 << 30, 4 << 20, [pltpu.VMEM((GRP, DH), F32)]
    )(info, att, gg, gate, *gather_z(stats), *dsigs)
    g_next = along(gatt, "y", -1)
    send_1, keep_1 = call(
        early_weights_body,
        (bf16((4, BLK, BLK)), f32((4, BLK, BLK))), 10, 1 << 30, 4 << 20,
        [pltpu.VMEM((D, BLK), F32), pltpu.VMEM((BLK, D), F32)],
    )(info, *evs, *cots, gated, gp_g)
    gp_q, dkv = call(
        backward_local_body, (bf16((GRP, BLK)), f32((GRP, 2 * BLK))), 8, 10 << 30, 4 << 20,
        [pltpu.VMEM((GRP, BLK), F32)],
    )(info, q, gatt, kv, kv_prev, *dsigs)
    gp_kv = call(
        backward_later_body, bf16((GRP, 2 * BLK)), 8, 5 << 30, 4 << 20, [pltpu.VMEM((GRP, 2 * BLK), F32)]
    )(info, q_next, g_next, kv, dkv, *dsigs)
    send_2, keep_2 = call(
        late_weights_body,
        (bf16((4, 128, 768)), f32((4, 128, 768))), 6, 2 << 30, 4 << 20,
        [pltpu.VMEM((D, 768), F32)],
    )(info, *evs, gp_q, gp_kv)

    rows_g = lax.all_to_all(gp_g.reshape(NB, BLK, BLK), "z", 0, 0)
    rows_q = lax.all_to_all(gp_q.reshape(NB, BLK, BLK), "z", 0, 0)
    rows_kv = lax.all_to_all(gp_kv.reshape(NB, BLK, 2 * BLK), "z", 0, 0)
    early = pl.pallas_call(
        input_early_body,
        grid=(4,),
        out_shape=f32((BLK, D)),
        in_specs=[
            pl.BlockSpec((1, BLK, BLK), lambda s: (s, 0, 0)),
            pl.BlockSpec((1, BLK, BLK), lambda s: (s, 0, 0)),
            pl.BlockSpec((D, BLK), lambda s: (0, s)),
            pl.BlockSpec((D, BLK), lambda s: (0, 8 + s)),
            pl.BlockSpec((BLK, D), lambda s: (0, 0)),
        ],
        out_specs=pl.BlockSpec((BLK, D), lambda s: (0, 0)),
        cost_estimate=pl.CostEstimate(flops=1 << 30, bytes_accessed=6 << 20, transcendentals=0),
    )(rows_g, rows_q, w_in, w_in, cot)
    grad_events = pl.pallas_call(
        input_late_body,
        grid=(4,),
        out_shape=bf16((BLK, D)),
        in_specs=[
            pl.BlockSpec((1, BLK, 2 * BLK), lambda s: (s, 0, 0)),
            pl.BlockSpec((D, BLK), lambda s: (0, 12 + s)),
            pl.BlockSpec((D, BLK), lambda s: (0, 4 + s)),
            pl.BlockSpec((BLK, D), lambda s: (0, 0)),
        ],
        out_specs=pl.BlockSpec((BLK, D), lambda s: (0, 0)),
        scratch_shapes=[pltpu.VMEM((BLK, D), F32)],
        cost_estimate=pl.CostEstimate(flops=1 << 30, bytes_accessed=6 << 20, transcendentals=0),
    )(rows_kv, w_in, w_in, early)

    first = reduce_xc(send_1, keep_1)
    out_rows = first[128:].reshape(4, 32, BLK).transpose(1, 0, 2).reshape(4, 8, D).astype(BF16)
    out_rows = jnp.sum(lax.all_to_all(out_rows, "y", 0, 0).astype(F32), axis=0)
    grad_w_out = to_owner(out_rows.astype(BF16))

    def reduce_yz(part):
        chunks = part.astype(BF16).reshape(16, 8, part.shape[1])
        got = lax.all_to_all(chunks, ("y", "z"), 0, 0)
        return jnp.sum(got.reshape(4, 4, 8, part.shape[1]).astype(F32), axis=0)

    gate_part = reduce_yz(first[:128])
    late = reduce_yz(reduce_xc(send_2, keep_2))
    pieces = [gate_part] + [late[:, :, n * BLK : (n + 1) * BLK] for n in range(3)]
    grad_w_in = jnp.stack(pieces).transpose(2, 0, 1, 3).reshape(8, 4 * D).astype(BF16)
    return grad_events[None], grad_w_in, grad_w_out


def solution(mesh):
    axes = ("x", "c", "y", "z")
    split = Mesh(mesh.devices.reshape(4, 2, 4, 4), axes)
    dp, seq = ("x", "c"), ("y", "z")
    return jax.shard_map(
        body,
        mesh=split,
        in_specs=(P(dp, seq, None), P(dp, seq, None), P(dp, None), P(), P()),
        out_specs=(P(dp, seq, None), P(axes, None), P(axes, None)),
        check_vma=False,
    )
```

```python
import jax
import jax.numpy as jnp
from jax import lax
from jax.experimental import pallas as pl
from jax.experimental.pallas import tpu as pltpu
from jax.sharding import Mesh
from jax.sharding import PartitionSpec as P

BLK = 256
NB = 4
DH = 128
GRP = NB * BLK
D = 1024
F32 = jnp.float32
BF16 = jnp.bfloat16
SCALE = 1.0 / 256.0
VMEM = pl.BlockSpec(memory_space=pltpu.VMEM)
SMEM = pl.BlockSpec(memory_space=pltpu.SMEM)


def call(body, outs, n_in, flops, nbytes, scratch=()):
    return pl.pallas_call(
        body,
        out_shape=outs,
        in_specs=[SMEM] + [VMEM] * n_in,
        out_specs=jax.tree.map(lambda _: VMEM, outs),
        scratch_shapes=scratch,
        compiler_params=pltpu.CompilerParams(vmem_limit_bytes=20 * 1024 * 1024),
        cost_estimate=pl.CostEstimate(flops=flops, bytes_accessed=nbytes, transcendentals=0),
    )


def nt(a, b):
    return lax.dot_general(a, b, (((1,), (1,)), ((), ())), preferred_element_type=F32)


def nn(a, b):
    return lax.dot_general(a, b, (((1,), (0,)), ((), ())), preferred_element_type=F32)


def tn(a, b):
    return lax.dot_general(a, b, (((0,), (0,)), ((), ())), preferred_element_type=F32)


def history_ends(info):
    ends, total = [], jnp.int32(0)
    for k in range(8):
        total = total + info[k]
        ends.append(total)
    return ends


def start_of(pos, ends):
    start = jnp.zeros_like(pos)
    for e in ends:
        start = jnp.where(pos >= e, e, start)
    return start


def end_of(pos, ends):
    end = ends[-1]
    for e in reversed(ends):
        end = jnp.where(e > pos, e, end)
    return end


def rows(i):
    return pl.ds(pl.multiple_of(i * BLK, BLK), BLK)


def head(h, base=0):
    return slice(base + h * DH, base + (h + 1) * DH)


def project_body(info, ev, wk, wv, wq, wg, kv, q, g, dsig):
    x = ev[...]
    for p, w in enumerate((wg, wv, wq, wk)):
        proj = nn(x, w[...])
        sig = 0.5 + 0.5 * jnp.tanh(0.5 * proj)
        act = (proj * sig).astype(BF16)
        if p == 0:
            g[...] = act
        elif p == 1:
            kv[:, BLK:] = act
        elif p == 2:
            q[...] = (0.5 * act.astype(F32)).astype(BF16)
        else:
            kv[:, :BLK] = act
        dsig[:, p * BLK : (p + 1) * BLK] = (sig * (1.0 + proj * (1.0 - sig))).astype(BF16)


def keep_rows(qpos, kpos, ends):
    r = qpos + lax.broadcasted_iota(jnp.int32, (BLK, 1), 0)
    c = kpos + lax.broadcasted_iota(jnp.int32, (1, BLK), 1)
    return jnp.where((c >= start_of(r, ends)) & (c <= r), SCALE, 0.0)


def keep_cols(qpos, kpos, ends):
    r = qpos + lax.broadcasted_iota(jnp.int32, (1, BLK), 1)
    c = kpos + lax.broadcasted_iota(jnp.int32, (BLK, 1), 0)
    return jnp.where((c >= start_of(r, ends)) & (c <= r), SCALE, 0.0)


def attend(q, kv, att, i, j, keep):
    for h in range(2):
        u = nt(q[rows(i), head(h)], kv[rows(j), head(h)])
        w = (u * (1.0 + jnp.tanh(u)) * keep).astype(BF16)
        att[rows(i), head(h)] += nn(w, kv[rows(j), head(h, BLK)])


def forward_local_body(info, *refs):
    q_in, kv_in = refs[0:4], refs[4:8]
    q, kv, att = refs[8:]
    ends = history_ends(info)
    base = info[8] * GRP
    for k in range(NB):
        at = rows(lax.rem(info[9] + k, NB))
        q[at, :] = q_in[k][...]
        kv[at, :] = kv_in[k][...]
    att[...] = jnp.zeros_like(att)

    def over_i(i, _):
        qpos = base + i * BLK
        first = jnp.maximum(start_of(qpos, ends) - base, 0) // BLK

        def over_j(j, _):
            attend(q, kv, att, i, j, keep_rows(qpos, base + j * BLK, ends))
            return 0

        return lax.fori_loop(first, i + 1, over_j, 0)

    lax.fori_loop(0, NB, over_i, 0)


def halo_first(i, qpos, prev, ends):
    start = start_of(qpos, ends)
    return jnp.where(start >= prev + GRP, NB, jnp.maximum((start - prev) // BLK, i))


def forward_halo_body(info, *refs):
    q, att_in, wout = refs[0:3]
    kv_in, cot, gate_in = refs[3:7], refs[7:11], refs[11:15]
    att, kv, gg, gate, stats = refs[15:20]
    ends = history_ends(info)
    base = info[8] * GRP
    prev = base - GRP
    att[...] = att_in[...]
    for k in range(NB):
        at = rows(lax.rem(info[9] + k, NB))
        kv[at, :] = kv_in[k][...]
        gate[at, :] = gate_in[k][...]
        gg[at, :] = nt(cot[k][...], wout[...])

    def over_i(i, _):
        qpos = base + i * BLK

        def over_j(j, _):
            attend(q, kv, att, i, j, keep_rows(qpos, prev + j * BLK, ends))
            return 0

        return lax.fori_loop(halo_first(i, qpos, prev, ends), NB, over_j, 0)

    lax.fori_loop(0, NB, over_i, 0)
    a = att[...]
    gn = gg[...] * gate[...].astype(F32)
    mean = jnp.sum(a, axis=1, keepdims=True) / BLK
    cent = a - mean
    m2 = jnp.sum(cent * cent, axis=1, keepdims=True)
    g1 = jnp.sum(gn, axis=1, keepdims=True)
    ga = jnp.sum(gn * cent, axis=1, keepdims=True)
    lane = lax.broadcasted_iota(jnp.int32, (GRP, DH), 1)
    packed = jnp.where(lane == 0, mean, jnp.where(lane == 1, m2, jnp.where(lane == 2, g1, ga)))
    stats[...] = packed.T[:8, :]


def norm_body(info, *refs):
    att, gg, gate = refs[0:3]
    stats, dsig = refs[3:7], refs[7:11]
    gatt, gated, gp, table = refs[11:15]
    parts = [s[...] for s in stats]
    mean = (parts[0][0:1] + parts[1][0:1] + parts[2][0:1] + parts[3][0:1]) * 0.25
    m2 = jnp.zeros_like(mean)
    g1 = jnp.zeros_like(mean)
    ga = jnp.zeros_like(mean)
    for p in parts:
        off = p[0:1] - mean
        m2 = m2 + p[1:2] + BLK * off * off
        g1 = g1 + p[2:3]
        ga = ga + p[3:4] + off * p[2:3]
    inv = lax.rsqrt(m2 / D + 1e-6)
    row = lax.broadcasted_iota(jnp.int32, (DH, GRP), 0)
    cols = jnp.where(row == 0, mean, jnp.where(row == 1, inv, jnp.where(row == 2, g1 / D, ga * inv / D)))
    table[...] = cols.T
    for k in range(NB):
        at = rows(lax.rem(info[9] + k, NB))
        t = table[at, :]
        mean_c, inv_c, g1_c, ga_c = (t[:, n : n + 1] for n in range(4))
        normed = (att[at, :] - mean_c) * inv_c
        g = gate[at, :].astype(F32)
        grad_gated = gg[at, :]
        gatt[at, :] = (inv_c * (grad_gated * g - g1_c - normed * ga_c)).astype(BF16)
        gated[at, :] = (normed * g).astype(BF16)
        gp[at, :] = (grad_gated * normed * dsig[k][:, 0:BLK].astype(F32)).astype(BF16)


def early_weights_body(info, *refs):
    ev, cot, gp = refs[0:4], refs[4:8], refs[8:12]
    gated, send, keep, acc_in, acc_out = refs[12:17]
    for k in range(NB):
        part_in = tn(ev[k][...], gp[k][...])
        part_out = tn(gated[rows(lax.rem(info[9] + k, NB)), :], cot[k][...])
        if k:
            part_in += acc_in[...]
            part_out += acc_out[...]
        acc_in[...] = part_in
        acc_out[...] = part_out
    for x in range(4):
        for out, c, kind in ((send, 1 - info[10], BF16), (keep, info[10], F32)):
            big = pl.multiple_of((x * 2 + c) * 128, 128)
            small = pl.multiple_of((x * 2 + c) * 32, 32)
            out[x, :, 0:512] = acc_in[pl.ds(big, 128), :].astype(kind)
            for n in range(4):
                out[x, 32 * n : 32 * n + 32, 512:768] = acc_out[
                    pl.ds(small, 32), n * BLK : (n + 1) * BLK
                ].astype(kind)


def late_weights_body(info, *refs):
    ev, gp = refs[0:4], refs[4:8]
    send, keep, acc = refs[8:11]
    for k in range(NB):
        part = tn(ev[k][...], gp[k][...])
        if k:
            part += acc[...]
        acc[...] = part
    for x in range(4):
        for out, c, kind in ((send, 1 - info[10], BF16), (keep, info[10], F32)):
            at = pl.multiple_of((x * 2 + c) * 128, 128)
            out[x, :, :] = acc[pl.ds(at, 128), :].astype(kind)


def add_core_body(info, keep, got, to_1, to_2, to_3, own):
    own[...] = keep[info[11]] + got[info[11]].astype(F32)
    for d, out in ((1, to_1), (2, to_2), (3, to_3)):
        at = lax.rem(info[11] + d, 4)
        out[...] = (keep[at] + got[at].astype(F32)).astype(BF16)


def add_early_body(info, own, got_1, got_2, got_3, part_in, part_out):
    total = own[...] + got_1[...].astype(F32) + got_2[...].astype(F32) + got_3[...].astype(F32)
    part_in[...] = total[:, 0:512].astype(BF16)
    part_out[...] = total[:, 512:768]


def add_late_body(info, own, got_1, got_2, got_3, early, part_in):
    total = own[...] + got_1[...].astype(F32) + got_2[...].astype(F32) + got_3[...].astype(F32)
    part_in[:, 0:512] = early[...]
    part_in[:, 512:1024] = total.astype(BF16)


def silu_parts(u):
    t = jnp.tanh(u)
    a = 1.0 + t
    ut = u * t
    return u + ut, a * ((1.0 + u) - ut)


def key_side(q, g, kv, dkv, dq, i, j, keep):
    half = keep * 0.5
    for h in range(2):
        qi, gi = q[rows(i), head(h)], g[rows(i), head(h)]
        kj, vj = kv[rows(j), head(h)], kv[rows(j), head(h, BLK)]
        silu, slope = silu_parts(nt(kj, qi))
        w = (silu * keep).astype(BF16)
        ds = (nt(vj, gi) * slope * half).astype(BF16)
        dkv[rows(j), head(h, BLK)] += nn(w, gi)
        dkv[rows(j), head(h)] += nn(ds, qi)
        if dq is not None:
            dq[rows(i), head(h)] += tn(ds, kj)


def query_side(q, g, kv, dq, i, j, keep):
    half = keep * 0.5
    for h in range(2):
        kj, vj = kv[rows(j), head(h)], kv[rows(j), head(h, BLK)]
        slope = silu_parts(nt(q[rows(i), head(h)], kj))[1]
        ds = (nt(g[rows(i), head(h)], vj) * slope * half).astype(BF16)
        dq[rows(i), head(h)] += nn(ds, kj)


def backward_local_body(info, *refs):
    q, g, kv, kv_prev, gp_g = refs[0:5]
    dsig, gp = refs[5:9], refs[9:13]
    dkv, dq = refs[13:15]
    ends = history_ends(info)
    base = info[8] * GRP
    prev = base - GRP
    dq[...] = jnp.zeros_like(dq)
    dkv[...] = jnp.zeros_like(dkv)

    def over_j(j, _):
        kpos = base + j * BLK
        last = jnp.minimum((end_of(kpos + BLK - 1, ends) - 1 - base) // BLK, NB - 1)

        def over_i(i, _):
            key_side(q, g, kv, dkv, dq, i, j, keep_cols(base + i * BLK, kpos, ends))
            return 0

        return lax.fori_loop(j, last + 1, over_i, 0)

    lax.fori_loop(0, NB, over_j, 0)

    def halo_i(i, _):
        qpos = base + i * BLK

        def halo_j(j, _):
            query_side(q, g, kv_prev, dq, i, j, keep_rows(qpos, prev + j * BLK, ends))
            return 0

        return lax.fori_loop(halo_first(i, qpos, prev, ends), NB, halo_j, 0)

    lax.fori_loop(0, NB, halo_i, 0)
    for k in range(NB):
        at = rows(lax.rem(info[9] + k, NB))
        gp[k][:, :BLK] = gp_g[at, :]
        gp[k][:, BLK:] = (dq[at, :] * dsig[k][:, 2 * BLK : 3 * BLK].astype(F32)).astype(BF16)


def backward_later_body(info, *refs):
    q, g, kv, dkv_in = refs[0:4]
    dsig, gp = refs[4:8], refs[8:12]
    dkv = refs[12]
    ends = history_ends(info)
    base = info[8] * GRP
    later = base + GRP
    dkv[...] = dkv_in[...]

    def over_j(j, _):
        kpos = base + j * BLK
        end = end_of(kpos + BLK - 1, ends)
        count = jnp.where(end > later, jnp.minimum((end - 1 - later) // BLK, j) + 1, 0)

        def over_i(i, _):
            key_side(q, g, kv, dkv, None, i, j, keep_cols(later + i * BLK, kpos, ends))
            return 0

        return lax.fori_loop(0, count, over_i, 0)

    lax.fori_loop(0, NB, over_j, 0)
    for k in range(NB):
        at = rows(lax.rem(info[9] + k, NB))
        dk = 2.0 * dkv[at, 0:BLK]
        gp[k][:, :BLK] = (dkv[at, BLK:] * dsig[k][:, BLK : 2 * BLK].astype(F32)).astype(BF16)
        gp[k][:, BLK:] = (dk * dsig[k][:, 3 * BLK :].astype(F32)).astype(BF16)


def input_rows(info, gp, w, parts, total):
    for d in range(NB):
        owner = lax.rem(info[9] + NB - d, NB)
        for n, part in enumerate(parts):
            lanes = pl.ds(pl.multiple_of(part * D + owner * BLK, BLK), BLK)
            total = total + nt(gp[d][:, n * BLK : (n + 1) * BLK], w[:, lanes])
    return total


def input_early_body(info, *refs):
    gp, (w, cot, out) = refs[0:4], refs[4:7]
    out[...] = input_rows(info, gp, w, (0, 2), cot[...].astype(F32))


def input_late_body(info, *refs):
    gp, (w, early, out) = refs[0:4], refs[4:7]
    out[...] = input_rows(info, gp, w, (1, 3), early[...]).astype(BF16)


def along(x, axis, d):
    return lax.ppermute(x, axis, [(i, (i + d) % 4) for i in range(4)])


def swap(x):
    return lax.ppermute(x, "c", [(0, 1), (1, 0)])


def gather_z(x):
    return [x, along(x, "z", -1), along(x, "z", 2), along(x, "z", 1)]


def to_owners(pieces, y):
    got = []
    for step in range(4):
        route = []
        for xc in range(8):
            for ys in range(4):
                for z in range(4):
                    src = (xc * 4 + ys) * 4 + z
                    dst = ((2 * z + xc // 4) * 4 + xc % 4) * 4 + (ys + step) % 4
                    route.append((src, dst))
        piece = lax.dynamic_index_in_dim(pieces, lax.rem(y + step, 4), 0, keepdims=False)
        got.append(lax.ppermute(piece, ("x", "c", "y", "z"), route).astype(F32))
    return got[0] + got[1] + got[2] + got[3]


def exchange(parts, axis):
    return [parts[0]] + [along(parts[d], axis, d) for d in (1, 2, 3)]


def f32(shape):
    return jax.ShapeDtypeStruct(shape, F32)


def bf16(shape):
    return jax.ShapeDtypeStruct(shape, BF16)


def body(events, cotangent, hist, w_in, w_out):
    z = lax.axis_index("z")
    info = jnp.concatenate(
        [hist[0], jnp.stack([lax.axis_index("y"), z, lax.axis_index("c"), lax.axis_index("x")]).astype(jnp.int32)]
    )
    ev, cot = events[0], cotangent[0]
    evs = gather_z(ev)
    wg, wv, wq, wk = (lax.dynamic_slice(w_in, (0, p * D + z * BLK), (D, BLK)) for p in range(4))
    wout = lax.dynamic_slice(w_out, (z * BLK, 0), (BLK, D))
    kvs, qs, gs, dsigs, kv_prevs = [], [], [], [], []
    for k in range(NB):
        kv, q, g, dsig = call(
            project_body,
            (bf16((BLK, 2 * BLK)), bf16((BLK, BLK)), bf16((BLK, BLK)), bf16((BLK, 4 * BLK))),
            5, 2 * BLK * D * D, 4 << 20,
        )(info, evs[k], wk, wv, wq, wg)
        kvs.append(kv)
        qs.append(q)
        gs.append(g)
        dsigs.append(dsig)
        kv_prevs.append(along(kv, "y", 1))
    cots = gather_z(cot)
    q, kv, att = call(
        forward_local_body, (bf16((GRP, BLK)), bf16((GRP, 2 * BLK)), f32((GRP, BLK))), 8, 5 << 30, 4 << 20
    )(info, *qs, *kvs)
    q_next = along(q, "y", -1)
    att, kv_prev, gg, gate, stats = call(
        forward_halo_body,
        (f32((GRP, BLK)), bf16((GRP, 2 * BLK)), f32((GRP, BLK)), bf16((GRP, BLK)), f32((8, GRP))),
        15, 5 << 30, 4 << 20,
    )(info, q, att, wout, *kv_prevs, *cots, *gs)
    gatt, gated, gp_g = call(
        norm_body, (bf16((GRP, BLK)),) * 3, 11, 1 << 30, 4 << 20, [pltpu.VMEM((GRP, DH), F32)]
    )(info, att, gg, gate, *gather_z(stats), *dsigs)
    g_next = along(gatt, "y", -1)
    *gp_gq, dkv = call(
        backward_local_body, (bf16((BLK, 2 * BLK)),) * 4 + (f32((GRP, 2 * BLK)),), 9, 10 << 30, 4 << 20,
        [pltpu.VMEM((GRP, BLK), F32)],
    )(info, q, gatt, kv, kv_prev, gp_g, *dsigs)
    rows_gq = exchange(gp_gq, "z")
    send_1, keep_1 = call(
        early_weights_body,
        (bf16((4, 128, 768)), f32((4, 128, 768))), 13, 2 << 30, 4 << 20,
        [pltpu.VMEM((D, 2 * BLK), F32), pltpu.VMEM((BLK, D), F32)],
    )(info, *evs, *cots, *gp_gq, gated)
    got_1 = swap(send_1)
    q_next, g_next, keep_1 = lax.optimization_barrier((q_next, g_next, keep_1))
    gp_vk = call(
        backward_later_body, (bf16((BLK, 2 * BLK)),) * 4, 8, 5 << 30, 4 << 20, [pltpu.VMEM((GRP, 2 * BLK), F32)]
    )(info, q_next, g_next, kv, dkv, *dsigs)
    rows_vk = exchange(gp_vk, "z")
    send_2, keep_2 = call(
        late_weights_body,
        (bf16((4, 128, 512)), f32((4, 128, 512))), 8, 1 << 30, 4 << 20,
        [pltpu.VMEM((D, 2 * BLK), F32)],
    )(info, *evs, *gp_vk)
    got_2 = swap(send_2)

    def add_core(keep, got):
        n = keep.shape[2]
        *away, own = call(
            add_core_body, (bf16((128, n)),) * 3 + (f32((128, n)),), 2, 1 << 20, 4 << 20
        )(info, keep, got)
        return exchange([own] + away, "x")

    first = add_core(keep_1, got_1)
    second = add_core(keep_2, got_2)
    part_gq, part_out = call(add_early_body, (bf16((128, 512)), f32((128, BLK))), 4, 1 << 20, 1 << 20)(info, *first)
    pieces = part_out.reshape(4, 4, 8, BLK).transpose(1, 2, 0, 3).reshape(4, 8, D).astype(BF16)
    grad_w_out = to_owners(pieces, lax.axis_index("y")).astype(BF16)
    early = call(input_early_body, f32((BLK, D)), 6, 1 << 30, 8 << 20)(info, *rows_gq, w_in, cot)
    part_in = call(add_late_body, bf16((128, D)), 5, 1 << 20, 1 << 20)(info, *second, part_gq)
    got = lax.all_to_all(part_in.reshape(16, 8, D), ("y", "z"), 0, 0)
    grad_events = call(input_late_body, bf16((BLK, D)), 6, 1 << 30, 8 << 20)(info, *rows_vk, w_in, early)
    got = jnp.sum(got.reshape(4, 4, 8, 4, BLK).astype(F32), axis=0)
    got = got.transpose(1, 2, 0, 3)
    got = jnp.stack([got[:, 0], got[:, 2], got[:, 1], got[:, 3]], axis=1)
    return grad_events[None], got.reshape(8, 4 * D).astype(BF16), grad_w_out


def solution(mesh):
    axes = ("x", "c", "y", "z")
    split = Mesh(mesh.devices.reshape(4, 2, 4, 4), axes)
    dp, seq = ("x", "c"), ("y", "z")
    return jax.shard_map(
        body,
        mesh=split,
        in_specs=(P(dp, seq, None), P(dp, seq, None), P(dp, None), P(), P()),
        out_specs=(P(dp, seq, None), P(axes, None), P(axes, None)),
        check_vma=False,
    )
```

```python
import jax
import jax.numpy as jnp
from jax import lax
from jax.experimental import pallas as pl
from jax.experimental.pallas import tpu as pltpu
from jax.sharding import Mesh
from jax.sharding import PartitionSpec as P

BLK = 256
NB = 4
DH = 128
GRP = NB * BLK
D = 1024
F32 = jnp.float32
BF16 = jnp.bfloat16
SCALE = 1.0 / 256.0
VMEM = pl.BlockSpec(memory_space=pltpu.VMEM)
SMEM = pl.BlockSpec(memory_space=pltpu.SMEM)


def call(body, outs, n_in, flops, nbytes, scratch=()):
    return pl.pallas_call(
        body,
        out_shape=outs,
        in_specs=[SMEM] + [VMEM] * n_in,
        out_specs=jax.tree.map(lambda _: VMEM, outs),
        scratch_shapes=scratch,
        compiler_params=pltpu.CompilerParams(vmem_limit_bytes=20 * 1024 * 1024),
        cost_estimate=pl.CostEstimate(flops=flops, bytes_accessed=nbytes, transcendentals=0),
    )


def nt(a, b):
    return lax.dot_general(a, b, (((1,), (1,)), ((), ())), preferred_element_type=F32)


def nn(a, b):
    return lax.dot_general(a, b, (((1,), (0,)), ((), ())), preferred_element_type=F32)


def tn(a, b):
    return lax.dot_general(a, b, (((0,), (0,)), ((), ())), preferred_element_type=F32)


def history_ends(info):
    ends, total = [], jnp.int32(0)
    for k in range(8):
        total = total + info[k]
        ends.append(total)
    return ends


def start_of(pos, ends):
    start = jnp.zeros_like(pos)
    for e in ends:
        start = jnp.where(pos >= e, e, start)
    return start


def end_of(pos, ends):
    end = ends[-1]
    for e in reversed(ends):
        end = jnp.where(e > pos, e, end)
    return end


def rows(i):
    return pl.ds(pl.multiple_of(i * BLK, BLK), BLK)


def head(h, base=0):
    return slice(base + h * DH, base + (h + 1) * DH)


def project_body(info, *refs):
    n = (len(refs) - 4) // 2
    ev, (w, kv, q, g), dsig = refs[:n], refs[n : n + 4], refs[n + 4 :]
    for b in range(n):
        x, at = ev[b][...], slice(b * BLK, (b + 1) * BLK)
        for p in range(4):
            lanes = pl.ds(pl.multiple_of(p * D + info[9] * BLK, BLK), BLK)
            proj = nn(x, w[:, lanes])
            sig = 0.5 + 0.5 * jnp.tanh(0.5 * proj)
            act = (proj * sig).astype(BF16)
            if p == 0:
                g[at, :] = act
            elif p == 1:
                kv[at, BLK:] = act
            elif p == 2:
                q[at, :] = (0.5 * act.astype(F32)).astype(BF16)
            else:
                kv[at, :BLK] = act
            dsig[b][:, p * BLK : (p + 1) * BLK] = (sig * (1.0 + proj * (1.0 - sig))).astype(BF16)


def grad_gated_body(info, cot, w, *outs):
    for d in range(NB):
        out_rows = rows(lax.rem(info[9] + d, NB))
        outs[d][...] = nt(cot[...], w[out_rows, :]).astype(BF16)


def keep_rows(qpos, kpos, ends):
    r = qpos + lax.broadcasted_iota(jnp.int32, (BLK, 1), 0)
    c = kpos + lax.broadcasted_iota(jnp.int32, (1, BLK), 1)
    return jnp.where((c >= start_of(r, ends)) & (c <= r), SCALE, 0.0)


def keep_cols(qpos, kpos, ends):
    r = qpos + lax.broadcasted_iota(jnp.int32, (1, BLK), 1)
    c = kpos + lax.broadcasted_iota(jnp.int32, (BLK, 1), 0)
    return jnp.where((c >= start_of(r, ends)) & (c <= r), SCALE, 0.0)


def attend(q, kv, att, i, j, keep):
    for h in range(2):
        u = nt(q[rows(i), head(h)], kv[rows(j), head(h)])
        w = (u * (1.0 + jnp.tanh(u)) * keep).astype(BF16)
        att[rows(i), head(h)] += nn(w, kv[rows(j), head(h, BLK)])


def block_of(parts, k):
    part, at = ((0, 0), (1, 0), (2, 0), (1, BLK))[k]
    return parts[part][at : at + BLK, :]


def forward_local_body(info, *refs):
    q_in, kv_in = refs[0:3], refs[3:6]
    q, kv, att = refs[6:]
    ends = history_ends(info)
    base = info[8] * GRP
    for k in range(NB):
        at = rows(lax.rem(info[9] + k, NB))
        q[at, :] = block_of(q_in, k)
        kv[at, :] = block_of(kv_in, k)
    att[...] = jnp.zeros_like(att)

    def over_i(i, _):
        qpos = base + i * BLK
        first = jnp.maximum(start_of(qpos, ends) - base, 0) // BLK

        def over_j(j, _):
            attend(q, kv, att, i, j, keep_rows(qpos, base + j * BLK, ends))
            return 0

        return lax.fori_loop(first, i + 1, over_j, 0)

    lax.fori_loop(0, NB, over_i, 0)


def halo_first(i, qpos, prev, ends):
    start = start_of(qpos, ends)
    return jnp.where(start >= prev + GRP, NB, jnp.maximum((start - prev) // BLK, i))


def forward_halo_body(info, *refs):
    q, att_in = refs[0:2]
    kv_in, gg_in, gate_in = refs[2:5], refs[5:9], refs[9:12]
    att, kv, gg, gate, stats = refs[12:17]
    ends = history_ends(info)
    base = info[8] * GRP
    prev = base - GRP
    att[...] = att_in[...]
    for k in range(NB):
        at = rows(lax.rem(info[9] + k, NB))
        kv[at, :] = block_of(kv_in, k)
        gate[at, :] = block_of(gate_in, k)
        gg[at, :] = gg_in[(4 - k) % 4][...]

    def over_i(i, _):
        qpos = base + i * BLK

        def over_j(j, _):
            attend(q, kv, att, i, j, keep_rows(qpos, prev + j * BLK, ends))
            return 0

        return lax.fori_loop(halo_first(i, qpos, prev, ends), NB, over_j, 0)

    lax.fori_loop(0, NB, over_i, 0)
    a = att[...]
    gn = gg[...].astype(F32) * gate[...].astype(F32)
    mean = jnp.sum(a, axis=1, keepdims=True) / BLK
    cent = a - mean
    m2 = jnp.sum(cent * cent, axis=1, keepdims=True)
    g1 = jnp.sum(gn, axis=1, keepdims=True)
    ga = jnp.sum(gn * cent, axis=1, keepdims=True)
    lane = lax.broadcasted_iota(jnp.int32, (GRP, DH), 1)
    packed = jnp.where(lane == 0, mean, jnp.where(lane == 1, m2, jnp.where(lane == 2, g1, ga)))
    stats[...] = packed.T[:8, :]


def norm_body(info, *refs):
    att, gg, gate = refs[0:3]
    stats, dsig = refs[3:7], refs[7:11]
    gatt, gated, gp, table = refs[11:15]
    parts = [s[...] for s in stats]
    mean = (parts[0][0:1] + parts[1][0:1] + parts[2][0:1] + parts[3][0:1]) * 0.25
    m2 = jnp.zeros_like(mean)
    g1 = jnp.zeros_like(mean)
    ga = jnp.zeros_like(mean)
    for p in parts:
        off = p[0:1] - mean
        m2 = m2 + p[1:2] + BLK * off * off
        g1 = g1 + p[2:3]
        ga = ga + p[3:4] + off * p[2:3]
    inv = lax.rsqrt(m2 / D + 1e-6)
    row = lax.broadcasted_iota(jnp.int32, (DH, GRP), 0)
    cols = jnp.where(row == 0, mean, jnp.where(row == 1, inv, jnp.where(row == 2, g1 / D, ga * inv / D)))
    table[...] = cols.T
    for k in range(NB):
        at = rows(lax.rem(info[9] + k, NB))
        t = table[at, :]
        mean_c, inv_c, g1_c, ga_c = (t[:, n : n + 1] for n in range(4))
        normed = (att[at, :] - mean_c) * inv_c
        g = gate[at, :].astype(F32)
        grad_gated = gg[at, :].astype(F32)
        gatt[at, :] = (inv_c * (grad_gated * g - g1_c - normed * ga_c)).astype(BF16)
        gated[at, :] = (normed * g).astype(BF16)
        gp[at, :] = (grad_gated * normed * dsig[k][:, 0:BLK].astype(F32)).astype(BF16)


def early_weights_body(info, *refs):
    ev, cot = refs[0:4], refs[4:8]
    gated, gp, out, acc_in, acc_out = refs[8:13]
    for k in range(NB):
        at = rows(lax.rem(info[9] + k, NB))
        part_in = tn(ev[k][...], gp[at, :])
        part_out = tn(gated[at, :], cot[k][...])
        if k:
            part_in += acc_in[...]
            part_out += acc_out[...]
        acc_in[...] = part_in
        acc_out[...] = part_out
    for n in range(8):
        out[n, :, :BLK] = acc_in[n * 128 : (n + 1) * 128, :]
        for m in range(4):
            out[n, 32 * m : 32 * m + 32, BLK:] = acc_out[n * 32 : (n + 1) * 32, m * BLK : (m + 1) * BLK]


def late_weights_body(info, *refs):
    ev, gq, vk = refs[0:4], refs[4:8], refs[8:12]
    send, keep, acc = refs[12:15]
    for k in range(NB):
        x = ev[k][...]
        for lanes, gp in ((slice(0, BLK), gq[k][:, BLK:]), (slice(BLK, 3 * BLK), vk[k][...])):
            part = tn(x, gp)
            acc[:, lanes] = part if k == 0 else acc[:, lanes] + part
    for x in range(4):
        for out, c, kind in ((send, 1 - info[10], BF16), (keep, info[10], F32)):
            at = pl.multiple_of((x * 2 + c) * 128, 128)
            out[x, :, :] = acc[pl.ds(at, 128), :].astype(kind)


def add_core_body(info, keep, got, to_1, to_2, to_3, own):
    own[...] = keep[info[11]] + got[info[11]].astype(F32)
    for d, out in ((1, to_1), (2, to_2), (3, to_3)):
        at = lax.rem(info[11] + d, 4)
        out[...] = (keep[at] + got[at].astype(F32)).astype(BF16)


def add_x_body(info, own, got_1, got_2, got_3, early, part_in, *pieces):
    total = own[...] + got_1[...].astype(F32) + got_2[...].astype(F32) + got_3[...].astype(F32)
    part_in[:, :BLK] = early[:, :BLK].astype(BF16)
    part_in[:, BLK:] = total.astype(BF16)
    for step in range(4):
        p = lax.rem(info[8] + step, 4)
        for n in range(4):
            at = pl.ds(pl.multiple_of(n * 32 + p * 8, 8), 8)
            pieces[step][:, n * BLK : (n + 1) * BLK] = early[at, BLK:]


def silu_parts(u):
    t = jnp.tanh(u)
    a = 1.0 + t
    ut = u * t
    return u + ut, a * ((1.0 + u) - ut)


def key_side(q, g, kv, dkv, dq, i, j, keep):
    half = keep * 0.5
    for h in range(2):
        qi, gi = q[rows(i), head(h)], g[rows(i), head(h)]
        kj, vj = kv[rows(j), head(h)], kv[rows(j), head(h, BLK)]
        silu, slope = silu_parts(nt(kj, qi))
        w = (silu * keep).astype(BF16)
        ds = (nt(vj, gi) * slope * half).astype(BF16)
        dkv[rows(j), head(h, BLK)] += nn(w, gi)
        dkv[rows(j), head(h)] += nn(ds, qi)
        if dq is not None:
            dq[rows(i), head(h)] += tn(ds, kj)


def query_side(q, g, kv, dq, i, j, keep):
    half = keep * 0.5
    for h in range(2):
        kj, vj = kv[rows(j), head(h)], kv[rows(j), head(h, BLK)]
        slope = silu_parts(nt(q[rows(i), head(h)], kj))[1]
        ds = (nt(g[rows(i), head(h)], vj) * slope * half).astype(BF16)
        dq[rows(i), head(h)] += nn(ds, kj)


def backward_local_body(info, *refs):
    q, g, kv, kv_prev, gp_g = refs[0:5]
    dsig, gp = refs[5:9], refs[9:13]
    dkv, dq = refs[13:15]
    ends = history_ends(info)
    base = info[8] * GRP
    prev = base - GRP
    dq[...] = jnp.zeros_like(dq)
    dkv[...] = jnp.zeros_like(dkv)

    def over_j(j, _):
        kpos = base + j * BLK
        last = jnp.minimum((end_of(kpos + BLK - 1, ends) - 1 - base) // BLK, NB - 1)

        def over_i(i, _):
            key_side(q, g, kv, dkv, dq, i, j, keep_cols(base + i * BLK, kpos, ends))
            return 0

        return lax.fori_loop(j, last + 1, over_i, 0)

    lax.fori_loop(0, NB, over_j, 0)

    def halo_i(i, _):
        qpos = base + i * BLK

        def halo_j(j, _):
            query_side(q, g, kv_prev, dq, i, j, keep_rows(qpos, prev + j * BLK, ends))
            return 0

        return lax.fori_loop(halo_first(i, qpos, prev, ends), NB, halo_j, 0)

    lax.fori_loop(0, NB, halo_i, 0)
    for k in range(NB):
        at = rows(lax.rem(info[9] + k, NB))
        gp[k][:, :BLK] = gp_g[at, :]
        gp[k][:, BLK:] = (dq[at, :] * dsig[k][:, 2 * BLK : 3 * BLK].astype(F32)).astype(BF16)


def backward_later_body(info, *refs):
    q, g, kv, dkv_in = refs[0:4]
    dsig, gp = refs[4:8], refs[8:12]
    dkv = refs[12]
    ends = history_ends(info)
    base = info[8] * GRP
    later = base + GRP
    dkv[...] = dkv_in[...]

    def over_j(j, _):
        kpos = base + j * BLK
        end = end_of(kpos + BLK - 1, ends)
        count = jnp.where(end > later, jnp.minimum((end - 1 - later) // BLK, j) + 1, 0)

        def over_i(i, _):
            key_side(q, g, kv, dkv, None, i, j, keep_cols(later + i * BLK, kpos, ends))
            return 0

        return lax.fori_loop(0, count, over_i, 0)

    lax.fori_loop(0, NB, over_j, 0)
    for k in range(NB):
        at = rows(lax.rem(info[9] + k, NB))
        dk = 2.0 * dkv[at, 0:BLK]
        gp[k][:, :BLK] = (dkv[at, BLK:] * dsig[k][:, BLK : 2 * BLK].astype(F32)).astype(BF16)
        gp[k][:, BLK:] = (dk * dsig[k][:, 3 * BLK :].astype(F32)).astype(BF16)


def input_rows(info, gp, w, parts, total):
    for d in range(NB):
        owner = lax.rem(info[9] + NB - d, NB)
        for n, part in enumerate(parts):
            lanes = pl.ds(pl.multiple_of(part * D + owner * BLK, BLK), BLK)
            total = total + nt(gp[d][:, n * BLK : (n + 1) * BLK], w[:, lanes])
    return total


def input_early_body(info, *refs):
    gp, (w, cot, out) = refs[0:4], refs[4:7]
    out[...] = input_rows(info, gp, w, (0, 2), cot[...].astype(F32))


def input_late_body(info, *refs):
    gp, (w, early, out) = refs[0:4], refs[4:7]
    out[...] = input_rows(info, gp, w, (1, 3), early[...]).astype(BF16)


def along(x, axis, d):
    return lax.ppermute(x, axis, [(i, (i + d) % 4) for i in range(4)])


def swap(x):
    return lax.ppermute(x, "c", [(0, 1), (1, 0)])


def gather_z(x):
    return [x, along(x, "z", -1), along(x, "z", 2), along(x, "z", 1)]


def to_owners(pieces):
    got = []
    for step in range(4):
        route = []
        for xc in range(8):
            for y in range(4):
                for z in range(4):
                    src = (xc * 4 + y) * 4 + z
                    dst = ((2 * z + xc // 4) * 4 + xc % 4) * 4 + (y + step) % 4
                    route.append((src, dst))
        got.append(lax.ppermute(pieces[step], ("x", "c", "y", "z"), route))
    return got[0] + got[1] + got[2] + got[3]


def exchange(parts, axis):
    return [parts[0]] + [along(parts[d], axis, d) for d in (1, 2, 3)]


def f32(shape):
    return jax.ShapeDtypeStruct(shape, F32)


def bf16(shape):
    return jax.ShapeDtypeStruct(shape, BF16)


def body(events, cotangent, hist, w_in, w_out):
    z = lax.axis_index("z")
    info = jnp.concatenate(
        [hist[0], jnp.stack([lax.axis_index("y"), z, lax.axis_index("c"), lax.axis_index("x")]).astype(jnp.int32)]
    )
    ev, cot = events[0], cotangent[0]
    evs = gather_z(ev)
    kvs, qs, gs, dsigs, kv_prevs = [], [], [], [None] * 4, []
    for blocks in ((0,), (1, 3), (2,)):
        n = len(blocks)
        kv, q, g, *dsig = call(
            project_body,
            (bf16((n * BLK, 2 * BLK)), bf16((n * BLK, BLK)), bf16((n * BLK, BLK))) + (bf16((BLK, 4 * BLK)),) * n,
            n + 1, 2 * n * BLK * D * D, 4 << 20,
        )(info, *[evs[b] for b in blocks], w_in)
        kvs.append(kv)
        qs.append(q)
        gs.append(g)
        for b, d in zip(blocks, dsig):
            dsigs[b] = d
        kv_prevs.append(along(kv, "y", 1))
    ggs = call(grad_gated_body, (bf16((BLK, BLK)),) * 4, 2, 1 << 29, 2 << 20)(info, cot, w_out)
    ggs = exchange(ggs, "z")
    cot_late, _ = lax.optimization_barrier((cot, kvs[2]))
    cots = gather_z(cot_late)
    q, kv, att = call(
        forward_local_body, (bf16((GRP, BLK)), bf16((GRP, 2 * BLK)), f32((GRP, BLK))), 6, 5 << 30, 4 << 20
    )(info, *qs, *kvs)
    q_next = along(q, "y", -1)
    att, kv_prev, gg, gate, stats = call(
        forward_halo_body,
        (f32((GRP, BLK)), bf16((GRP, 2 * BLK)), bf16((GRP, BLK)), bf16((GRP, BLK)), f32((8, GRP))),
        12, 5 << 30, 4 << 20,
    )(info, q, att, *kv_prevs, *ggs, *gs)
    gatt, gated, gp_g = call(
        norm_body, (bf16((GRP, BLK)),) * 3, 11, 1 << 30, 4 << 20, [pltpu.VMEM((GRP, DH), F32)]
    )(info, att, gg, gate, *gather_z(stats), *dsigs)
    g_next = along(gatt, "y", -1)
    part = call(
        early_weights_body, f32((8, 128, 512)), 10, 1 << 30, 4 << 20,
        [pltpu.VMEM((D, BLK), F32), pltpu.VMEM((BLK, D), F32)],
    )(info, *evs, *cots, gated, gp_g)
    early_sum = lax.psum_scatter(part, ("x", "c"), scatter_dimension=0)
    gatt, _ = lax.optimization_barrier((gatt, part))
    *gp_gq, dkv = call(
        backward_local_body, (bf16((BLK, 2 * BLK)),) * 4 + (f32((GRP, 2 * BLK)),), 9, 10 << 30, 4 << 20,
        [pltpu.VMEM((GRP, BLK), F32)],
    )(info, q, gatt, kv, kv_prev, gp_g, *dsigs)
    rows_gq = exchange(gp_gq, "z")
    gp_vk = call(
        backward_later_body, (bf16((BLK, 2 * BLK)),) * 4, 8, 5 << 30, 4 << 20, [pltpu.VMEM((GRP, 2 * BLK), F32)]
    )(info, q_next, g_next, kv, dkv, *dsigs)
    rows_vk = exchange(gp_vk, "z")
    gp_late, rows_gq = lax.optimization_barrier((gp_vk, rows_gq))
    send, keep = call(
        late_weights_body,
        (bf16((4, 128, 768)), f32((4, 128, 768))), 12, 2 << 30, 4 << 20,
        [pltpu.VMEM((D, 3 * BLK), F32)],
    )(info, *evs, *gp_gq, *gp_late)
    *away, own = call(
        add_core_body, (bf16((128, 768)),) * 3 + (f32((128, 768)),), 2, 1 << 20, 4 << 20
    )(info, keep, swap(send))
    sums = exchange([own] + away, "x")
    early = call(input_early_body, f32((BLK, D)), 6, 1 << 30, 8 << 20)(info, *rows_gq, w_in, cot)
    grad_events = call(input_late_body, bf16((BLK, D)), 6, 1 << 30, 8 << 20)(info, *rows_vk, w_in, early)
    early_sum, grad_events = lax.optimization_barrier((early_sum, grad_events))
    part_in, *pieces = call(
        add_x_body, (bf16((128, D)),) + (f32((8, D)),) * 4, 5, 1 << 20, 1 << 20
    )(info, *sums, early_sum)
    got = lax.all_to_all(part_in.reshape(16, 8, D), ("y", "z"), 0, 0)
    grad_w_out = to_owners(pieces).astype(BF16)
    got = jnp.sum(got.reshape(4, 4, 8, 4, BLK).astype(F32), axis=0)
    got = got.transpose(1, 2, 0, 3).reshape(8, 4 * D)
    got = jnp.concatenate([got[:, :D], got[:, 2 * D : 3 * D], got[:, D : 2 * D], got[:, 3 * D :]], axis=1)
    return grad_events[None], got.astype(BF16), grad_w_out


def solution(mesh):
    axes = ("x", "c", "y", "z")
    split = Mesh(mesh.devices.reshape(4, 2, 4, 4), axes)
    dp, seq = ("x", "c"), ("y", "z")
    return jax.shard_map(
        body,
        mesh=split,
        in_specs=(P(dp, seq, None), P(dp, seq, None), P(dp, None), P(), P()),
        out_specs=(P(dp, seq, None), P(axes, None), P(axes, None)),
        check_vma=False,
    )
```

```python
import jax
import jax.numpy as jnp
from jax import lax
from jax.experimental import pallas as pl
from jax.experimental.pallas import tpu as pltpu
from jax.sharding import Mesh
from jax.sharding import PartitionSpec as P

BLK = 256
NB = 4
DH = 128
GRP = NB * BLK
D = 1024
F32 = jnp.float32
BF16 = jnp.bfloat16
SCALE = 1.0 / 256.0
VMEM = pl.BlockSpec(memory_space=pltpu.VMEM)
SMEM = pl.BlockSpec(memory_space=pltpu.SMEM)


def call(body, outs, n_in, flops, nbytes, scratch=()):
    return pl.pallas_call(
        body,
        out_shape=outs,
        in_specs=[SMEM] + [VMEM] * n_in,
        out_specs=jax.tree.map(lambda _: VMEM, outs),
        scratch_shapes=scratch,
        compiler_params=pltpu.CompilerParams(vmem_limit_bytes=20 * 1024 * 1024),
        cost_estimate=pl.CostEstimate(flops=flops, bytes_accessed=nbytes, transcendentals=0),
    )


def nt(a, b):
    return lax.dot_general(a, b, (((1,), (1,)), ((), ())), preferred_element_type=F32)


def nn(a, b):
    return lax.dot_general(a, b, (((1,), (0,)), ((), ())), preferred_element_type=F32)


def tn(a, b):
    return lax.dot_general(a, b, (((0,), (0,)), ((), ())), preferred_element_type=F32)


def history_ends(info):
    ends, total = [], jnp.int32(0)
    for k in range(8):
        total = total + info[k]
        ends.append(total)
    return ends


def start_of(pos, ends):
    start = jnp.zeros_like(pos)
    for e in ends:
        start = jnp.where(pos >= e, e, start)
    return start


def end_of(pos, ends):
    end = ends[-1]
    for e in reversed(ends):
        end = jnp.where(e > pos, e, end)
    return end


def rows(i):
    return pl.ds(pl.multiple_of(i * BLK, BLK), BLK)


def head(h, base=0):
    return slice(base + h * DH, base + (h + 1) * DH)


def project_body(info, *refs):
    n = (len(refs) - 4) // 2
    ev, (w, kv, q, g), dsig = refs[:n], refs[n : n + 4], refs[n + 4 :]
    for b in range(n):
        x, at = ev[b][...], slice(b * BLK, (b + 1) * BLK)
        for p in range(4):
            lanes = pl.ds(pl.multiple_of(p * D + info[9] * BLK, BLK), BLK)
            proj = nn(x, w[:, lanes])
            sig = 0.5 + 0.5 * jnp.tanh(0.5 * proj)
            act = (proj * sig).astype(BF16)
            if p == 0:
                g[at, :] = act
            elif p == 1:
                kv[at, BLK:] = act
            elif p == 2:
                q[at, :] = (0.5 * act.astype(F32)).astype(BF16)
            else:
                kv[at, :BLK] = act
            dsig[b][:, p * BLK : (p + 1) * BLK] = (sig * (1.0 + proj * (1.0 - sig))).astype(BF16)


def grad_gated_body(info, cot, w, *outs):
    for d in range(NB):
        owner = lax.rem(info[9] + d, NB)
        outs[d][:, :BLK] = nt(cot[...], w[rows(owner), :]).astype(BF16)
        outs[d][:, BLK:] = cot[:, pl.ds(pl.multiple_of(owner * BLK, BLK), BLK)]


def keep_rows(qpos, kpos, ends):
    r = qpos + lax.broadcasted_iota(jnp.int32, (BLK, 1), 0)
    c = kpos + lax.broadcasted_iota(jnp.int32, (1, BLK), 1)
    return jnp.where((c >= start_of(r, ends)) & (c <= r), SCALE, 0.0)


def keep_cols(qpos, kpos, ends):
    r = qpos + lax.broadcasted_iota(jnp.int32, (1, BLK), 1)
    c = kpos + lax.broadcasted_iota(jnp.int32, (BLK, 1), 0)
    return jnp.where((c >= start_of(r, ends)) & (c <= r), SCALE, 0.0)


def attend(q, kv, att, i, j, keep):
    for h in range(2):
        u = nt(q[rows(i), head(h)], kv[rows(j), head(h)])
        w = (u * (1.0 + jnp.tanh(u)) * keep).astype(BF16)
        att[rows(i), head(h)] += nn(w, kv[rows(j), head(h, BLK)])


def block_of(parts, k):
    part, at = ((0, 0), (1, 0), (2, 0), (1, BLK))[k]
    return parts[part][at : at + BLK, :]


def forward_local_body(info, *refs):
    q_in, kv_in = refs[0:3], refs[3:6]
    q, kv, att = refs[6:]
    ends = history_ends(info)
    base = info[8] * GRP
    for k in range(NB):
        at = rows(lax.rem(info[9] + k, NB))
        q[at, :] = block_of(q_in, k)
        kv[at, :] = block_of(kv_in, k)
    att[...] = jnp.zeros_like(att)

    def over_i(i, _):
        qpos = base + i * BLK
        first = jnp.maximum(start_of(qpos, ends) - base, 0) // BLK

        def over_j(j, _):
            attend(q, kv, att, i, j, keep_rows(qpos, base + j * BLK, ends))
            return 0

        return lax.fori_loop(first, i + 1, over_j, 0)

    lax.fori_loop(0, NB, over_i, 0)


def halo_first(i, qpos, prev, ends):
    start = start_of(qpos, ends)
    return jnp.where(start >= prev + GRP, NB, jnp.maximum((start - prev) // BLK, i))


def forward_halo_body(info, *refs):
    q, att_in = refs[0:2]
    kv_in, gg_in, gate_in = refs[2:5], refs[5:9], refs[9:12]
    att, kv, gg, cot, gate, stats = refs[12:18]
    ends = history_ends(info)
    base = info[8] * GRP
    prev = base - GRP
    att[...] = att_in[...]
    for k in range(NB):
        at = rows(lax.rem(info[9] + k, NB))
        kv[at, :] = block_of(kv_in, k)
        gate[at, :] = block_of(gate_in, k)
        gg[at, :] = gg_in[(4 - k) % 4][:, :BLK]
        cot[at, :] = gg_in[(4 - k) % 4][:, BLK:]

    def over_i(i, _):
        qpos = base + i * BLK

        def over_j(j, _):
            attend(q, kv, att, i, j, keep_rows(qpos, prev + j * BLK, ends))
            return 0

        return lax.fori_loop(halo_first(i, qpos, prev, ends), NB, over_j, 0)

    lax.fori_loop(0, NB, over_i, 0)
    a = att[...]
    gn = gg[...].astype(F32) * gate[...].astype(F32)
    mean = jnp.sum(a, axis=1, keepdims=True) / BLK
    cent = a - mean
    m2 = jnp.sum(cent * cent, axis=1, keepdims=True)
    g1 = jnp.sum(gn, axis=1, keepdims=True)
    ga = jnp.sum(gn * cent, axis=1, keepdims=True)
    lane = lax.broadcasted_iota(jnp.int32, (GRP, DH), 1)
    packed = jnp.where(lane == 0, mean, jnp.where(lane == 1, m2, jnp.where(lane == 2, g1, ga)))
    stats[...] = packed.T[:8, :]


def norm_body(info, *refs):
    att, gg, gate = refs[0:3]
    stats, dsig = refs[3:7], refs[7:11]
    gatt, gated, gp, table = refs[11:15]
    parts = [s[...] for s in stats]
    mean = (parts[0][0:1] + parts[1][0:1] + parts[2][0:1] + parts[3][0:1]) * 0.25
    m2 = jnp.zeros_like(mean)
    g1 = jnp.zeros_like(mean)
    ga = jnp.zeros_like(mean)
    for p in parts:
        off = p[0:1] - mean
        m2 = m2 + p[1:2] + BLK * off * off
        g1 = g1 + p[2:3]
        ga = ga + p[3:4] + off * p[2:3]
    inv = lax.rsqrt(m2 / D + 1e-6)
    row = lax.broadcasted_iota(jnp.int32, (DH, GRP), 0)
    cols = jnp.where(row == 0, mean, jnp.where(row == 1, inv, jnp.where(row == 2, g1 / D, ga * inv / D)))
    table[...] = cols.T
    for k in range(NB):
        at = rows(lax.rem(info[9] + k, NB))
        t = table[at, :]
        mean_c, inv_c, g1_c, ga_c = (t[:, n : n + 1] for n in range(4))
        normed = (att[at, :] - mean_c) * inv_c
        g = gate[at, :].astype(F32)
        grad_gated = gg[at, :].astype(F32)
        gatt[at, :] = (inv_c * (grad_gated * g - g1_c - normed * ga_c)).astype(BF16)
        gated[at, :] = (normed * g).astype(BF16)
        gp[at, :] = (grad_gated * normed * dsig[k][:, 0:BLK].astype(F32)).astype(BF16)


def early_weights_body(info, *refs):
    ev, (gp_g, gp_q, acc) = refs[0:4], refs[4:7]
    for k in range(NB):
        at = rows(lax.rem(info[9] + k, NB))
        for lanes, gp in ((slice(0, BLK), gp_g), (slice(BLK, 2 * BLK), gp_q)):
            part = tn(ev[k][...], gp[at, :])
            acc[:, lanes] = part if k == 0 else acc[:, lanes] + part


def late_weights_body(info, *refs):
    ev, gp, gated = refs[0:4], refs[4:8], refs[8:12]
    cot, early, send, keep, acc = refs[12:17]
    for k in range(NB):
        part = tn(ev[k][...], gp[k][:, 2 * BLK :])
        acc[:, : 2 * BLK] = part if k == 0 else acc[:, : 2 * BLK] + part
        acc[rows(lax.rem(info[9] + k, NB)), 2 * BLK :] = tn(gated[k][...], cot[...])
    for x in range(4):
        for out, c, kind in ((send, 1 - info[10], BF16), (keep, info[10], F32)):
            at = pl.ds(pl.multiple_of((x * 2 + c) * 128, 128), 128)
            out[x, :, : 2 * BLK] = early[at, :].astype(kind)
            out[x, :, 2 * BLK :] = acc[at, :].astype(kind)


def add_core_body(info, keep, got, to_1, to_2, to_3, own):
    own[...] = keep[info[11]] + got[info[11]].astype(F32)
    for d, out in ((1, to_1), (2, to_2), (3, to_3)):
        at = lax.rem(info[11] + d, 4)
        out[...] = (keep[at] + got[at].astype(F32)).astype(BF16)


def add_x_body(info, own, got_1, got_2, got_3, total):
    part = own[...] + got_1[...].astype(F32) + got_2[...].astype(F32) + got_3[...].astype(F32)
    total[...] = part.astype(BF16)


def last_sum_body(info, got, grad_w_in, grad_w_out):
    for z in range(4):
        part = got[z].astype(F32)
        for y in range(1, 4):
            part = part + got[y * 4 + z].astype(F32)
        part = part.astype(BF16)
        for n, to in enumerate((0, 2, 1, 3)):
            at = to * D + z * BLK
            grad_w_in[:, at : at + BLK] = part[:, n * BLK : (n + 1) * BLK]
        grad_w_out[:, z * BLK : (z + 1) * BLK] = part[:, 4 * BLK :]


def silu_parts(u):
    t = jnp.tanh(u)
    a = 1.0 + t
    ut = u * t
    return u + ut, a * ((1.0 + u) - ut)


def key_side(q, g, kv, dkv, dq, i, j, keep):
    half = keep * 0.5
    for h in range(2):
        qi, gi = q[rows(i), head(h)], g[rows(i), head(h)]
        kj, vj = kv[rows(j), head(h)], kv[rows(j), head(h, BLK)]
        silu, slope = silu_parts(nt(kj, qi))
        w = (silu * keep).astype(BF16)
        ds = (nt(vj, gi) * slope * half).astype(BF16)
        dkv[rows(j), head(h, BLK)] += nn(w, gi)
        dkv[rows(j), head(h)] += nn(ds, qi)
        if dq is not None:
            dq[rows(i), head(h)] += tn(ds, kj)


def query_side(q, g, kv, dq, i, j, keep):
    half = keep * 0.5
    for h in range(2):
        kj, vj = kv[rows(j), head(h)], kv[rows(j), head(h, BLK)]
        slope = silu_parts(nt(q[rows(i), head(h)], kj))[1]
        ds = (nt(g[rows(i), head(h)], vj) * slope * half).astype(BF16)
        dq[rows(i), head(h)] += nn(ds, kj)


def backward_local_body(info, *refs):
    q, g, kv, kv_prev = refs[0:4]
    dsig = refs[4:8]
    gp_q, dkv, dq = refs[8:11]
    ends = history_ends(info)
    base = info[8] * GRP
    prev = base - GRP
    dq[...] = jnp.zeros_like(dq)
    dkv[...] = jnp.zeros_like(dkv)

    def over_j(j, _):
        kpos = base + j * BLK
        last = jnp.minimum((end_of(kpos + BLK - 1, ends) - 1 - base) // BLK, NB - 1)

        def over_i(i, _):
            key_side(q, g, kv, dkv, dq, i, j, keep_cols(base + i * BLK, kpos, ends))
            return 0

        return lax.fori_loop(j, last + 1, over_i, 0)

    lax.fori_loop(0, NB, over_j, 0)

    def halo_i(i, _):
        qpos = base + i * BLK

        def halo_j(j, _):
            query_side(q, g, kv_prev, dq, i, j, keep_rows(qpos, prev + j * BLK, ends))
            return 0

        return lax.fori_loop(halo_first(i, qpos, prev, ends), NB, halo_j, 0)

    lax.fori_loop(0, NB, halo_i, 0)
    for k in range(NB):
        at = rows(lax.rem(info[9] + k, NB))
        gp_q[at, :] = (dq[at, :] * dsig[k][:, 2 * BLK : 3 * BLK].astype(F32)).astype(BF16)


def backward_later_body(info, *refs):
    q, g, kv, dkv_in, gp_g, gp_q = refs[0:6]
    dsig, gp = refs[6:10], refs[10:14]
    dkv = refs[14]
    ends = history_ends(info)
    base = info[8] * GRP
    later = base + GRP
    dkv[...] = dkv_in[...]

    def over_j(j, _):
        kpos = base + j * BLK
        end = end_of(kpos + BLK - 1, ends)
        count = jnp.where(end > later, jnp.minimum((end - 1 - later) // BLK, j) + 1, 0)

        def over_i(i, _):
            key_side(q, g, kv, dkv, None, i, j, keep_cols(later + i * BLK, kpos, ends))
            return 0

        return lax.fori_loop(0, count, over_i, 0)

    lax.fori_loop(0, NB, over_j, 0)
    for k in range(NB):
        at = rows(lax.rem(info[9] + k, NB))
        dk = 2.0 * dkv[at, 0:BLK]
        gp[k][:, :BLK] = gp_g[at, :]
        gp[k][:, BLK : 2 * BLK] = gp_q[at, :]
        gp[k][:, 2 * BLK : 3 * BLK] = (dkv[at, BLK:] * dsig[k][:, BLK : 2 * BLK].astype(F32)).astype(BF16)
        gp[k][:, 3 * BLK :] = (dk * dsig[k][:, 3 * BLK :].astype(F32)).astype(BF16)


def input_body(info, *refs):
    gp, (w, cot, out) = refs[0:4], refs[4:7]
    total = cot[...].astype(F32)
    for d in range(NB):
        owner = lax.rem(info[9] + NB - d, NB)
        for n, part in enumerate((0, 2, 1, 3)):
            lanes = pl.ds(pl.multiple_of(part * D + owner * BLK, BLK), BLK)
            total = total + nt(gp[d][:, n * BLK : (n + 1) * BLK], w[:, lanes])
    out[...] = total.astype(BF16)


def along(x, axis, d):
    return lax.ppermute(x, axis, [(i, (i + d) % 4) for i in range(4)])


def swap(x):
    return lax.ppermute(x, "c", [(0, 1), (1, 0)])


def gather_z(x):
    return [x, along(x, "z", -1), along(x, "z", 2), along(x, "z", 1)]


def exchange(parts, axis):
    return [parts[0]] + [along(parts[d], axis, d) for d in (1, 2, 3)]


def f32(shape):
    return jax.ShapeDtypeStruct(shape, F32)


def bf16(shape):
    return jax.ShapeDtypeStruct(shape, BF16)


def body(events, cotangent, hist, w_in, w_out):
    z = lax.axis_index("z")
    info = jnp.concatenate(
        [hist[0], jnp.stack([lax.axis_index("y"), z, lax.axis_index("c"), lax.axis_index("x")]).astype(jnp.int32)]
    )
    ev, cot = events[0], cotangent[0]
    near = along(ev, "z", -1), along(ev, "z", 1)
    evs = [ev, near[0], None, near[1]]
    kvs, qs, gs, dsigs, kv_prevs = [], [], [], [None] * 4, []
    for blocks in ((0,), (1, 3), (2,)):
        n = len(blocks)
        if blocks == (1, 3):
            ev_far, *near, _ = lax.optimization_barrier((ev, *near, kvs[0]))
            evs = [ev, near[0], along(ev_far, "z", 2), near[1]]
        kv, q, g, *dsig = call(
            project_body,
            (bf16((n * BLK, 2 * BLK)), bf16((n * BLK, BLK)), bf16((n * BLK, BLK))) + (bf16((BLK, 4 * BLK)),) * n,
            n + 1, 2 * n * BLK * D * D, 4 << 20,
        )(info, *[evs[b] for b in blocks], w_in)
        kvs.append(kv)
        qs.append(q)
        gs.append(g)
        for b, d in zip(blocks, dsig):
            dsigs[b] = d
        kv_prevs.append(along(kv, "y", 1))
    ggs = call(grad_gated_body, (bf16((BLK, 2 * BLK)),) * 4, 2, 1 << 29, 2 << 20)(info, cot, w_out)
    *ggs, _ = lax.optimization_barrier((*ggs, evs[2]))
    ggs = exchange(ggs, "z")
    q, kv, att = call(
        forward_local_body, (bf16((GRP, BLK)), bf16((GRP, 2 * BLK)), f32((GRP, BLK))), 6, 5 << 30, 4 << 20
    )(info, *qs, *kvs)
    q_next = along(q, "y", -1)
    att, kv_prev, gg, cot_z, gate, stats = call(
        forward_halo_body,
        (f32((GRP, BLK)), bf16((GRP, 2 * BLK))) + (bf16((GRP, BLK)),) * 3 + (f32((8, GRP)),),
        12, 5 << 30, 4 << 20,
    )(info, q, att, *kv_prevs, *ggs, *gs)
    gatt, gated, gp_g = call(
        norm_body, (bf16((GRP, BLK)),) * 3, 11, 1 << 30, 4 << 20, [pltpu.VMEM((GRP, DH), F32)]
    )(info, att, gg, gate, *gather_z(stats), *dsigs)
    g_next = along(gatt, "y", -1)
    gateds = gather_z(gated)
    gp_q, dkv = call(
        backward_local_body, (bf16((GRP, BLK)), f32((GRP, 2 * BLK))), 8, 10 << 30, 4 << 20,
        [pltpu.VMEM((GRP, BLK), F32)],
    )(info, q, gatt, kv, kv_prev, *dsigs)
    early = call(early_weights_body, f32((D, 2 * BLK)), 6, 1 << 30, 4 << 20)(info, *evs, gp_g, gp_q)
    q_next, g_next, early = lax.optimization_barrier((q_next, g_next, early))
    gp = call(
        backward_later_body, (bf16((BLK, 4 * BLK)),) * 4, 10, 5 << 30, 4 << 20, [pltpu.VMEM((GRP, 2 * BLK), F32)]
    )(info, q_next, g_next, kv, dkv, gp_g, gp_q, *dsigs)
    send, keep = call(
        late_weights_body,
        (bf16((4, 128, 5 * BLK)), f32((4, 128, 5 * BLK))), 14, 2 << 30, 4 << 20,
        [pltpu.VMEM((D, 3 * BLK), F32)],
    )(info, *evs, *gp, *gateds, cot_z, early)
    gp_rows = exchange(gp, "z")
    *away, own = call(
        add_core_body, (bf16((128, 5 * BLK)),) * 3 + (f32((128, 5 * BLK)),), 2, 1 << 20, 4 << 20
    )(info, keep, swap(send))
    sums = exchange([own] + away, "x")
    grad_events = call(input_body, bf16((BLK, D)), 6, 2 << 30, 8 << 20)(info, *gp_rows, w_in, cot)
    own, grad_events = lax.optimization_barrier((sums[0], grad_events))
    total = call(add_x_body, bf16((128, 5 * BLK)), 4, 1 << 20, 1 << 20)(info, own, *sums[1:])
    got = lax.all_to_all(total.reshape(16, 8, 5 * BLK), ("y", "z"), 0, 0)
    grad_w_in, grad_w_out = call(last_sum_body, (bf16((8, 4 * D)), bf16((8, D))), 1, 1 << 20, 1 << 20)(info, got)
    return grad_events[None], grad_w_in, grad_w_out


def solution(mesh):
    axes = ("x", "c", "y", "z")
    split = Mesh(mesh.devices.reshape(4, 2, 4, 4), axes)
    dp, seq = ("x", "c"), ("y", "z")
    return jax.shard_map(
        body,
        mesh=split,
        in_specs=(P(dp, seq, None), P(dp, seq, None), P(dp, None), P(), P()),
        out_specs=(P(dp, seq, None), P(axes, None), P(axes, None)),
        check_vma=False,
    )
```

```python
import jax
import jax.numpy as jnp
from jax import lax
from jax.experimental import pallas as pl
from jax.experimental.pallas import tpu as pltpu
from jax.sharding import Mesh
from jax.sharding import PartitionSpec as P

BLK = 256
NB = 4
DH = 128
GRP = NB * BLK
D = 1024
F32 = jnp.float32
BF16 = jnp.bfloat16
SCALE = 1.0 / 256.0
VMEM = pl.BlockSpec(memory_space=pltpu.VMEM)
SMEM = pl.BlockSpec(memory_space=pltpu.SMEM)


def call(body, outs, n_in, flops, nbytes, scratch=()):
    return pl.pallas_call(
        body,
        out_shape=outs,
        in_specs=[SMEM] + [VMEM] * n_in,
        out_specs=jax.tree.map(lambda _: VMEM, outs),
        scratch_shapes=scratch,
        compiler_params=pltpu.CompilerParams(vmem_limit_bytes=20 * 1024 * 1024),
        cost_estimate=pl.CostEstimate(flops=flops, bytes_accessed=nbytes, transcendentals=0),
    )


def nt(a, b):
    return lax.dot_general(a, b, (((1,), (1,)), ((), ())), preferred_element_type=F32)


def nn(a, b):
    return lax.dot_general(a, b, (((1,), (0,)), ((), ())), preferred_element_type=F32)


def tn(a, b):
    return lax.dot_general(a, b, (((0,), (0,)), ((), ())), preferred_element_type=F32)


def history_ends(info):
    ends, total = [], jnp.int32(0)
    for k in range(8):
        total = total + info[k]
        ends.append(total)
    return ends


def start_of(pos, ends):
    start = jnp.zeros_like(pos)
    for e in ends:
        start = jnp.where(pos >= e, e, start)
    return start


def end_of(pos, ends):
    end = ends[-1]
    for e in reversed(ends):
        end = jnp.where(e > pos, e, end)
    return end


def rows(i):
    return pl.ds(pl.multiple_of(i * BLK, BLK), BLK)


def head(h, base=0):
    return slice(base + h * DH, base + (h + 1) * DH)


def project_body(info, *refs):
    n = (len(refs) - 4) // 2
    ev, (w, kv, q, g), dsig = refs[:n], refs[n : n + 4], refs[n + 4 :]
    for b in range(n):
        x, at = ev[b][...], slice(b * BLK, (b + 1) * BLK)
        for p in range(4):
            lanes = pl.ds(pl.multiple_of(p * D + info[9] * BLK, BLK), BLK)
            proj = nn(x, w[:, lanes])
            sig = 0.5 + 0.5 * jnp.tanh(0.5 * proj)
            act = (proj * sig).astype(BF16)
            if p == 0:
                g[at, :] = act
            elif p == 1:
                kv[at, BLK:] = act
            elif p == 2:
                q[at, :] = (0.5 * act.astype(F32)).astype(BF16)
            else:
                kv[at, :BLK] = act
            dsig[b][:, p * BLK : (p + 1) * BLK] = (sig * (1.0 + proj * (1.0 - sig))).astype(BF16)


def grad_gated_body(info, cot, w, *outs):
    for d in range(NB):
        owner = lax.rem(info[9] + d, NB)
        outs[d][:, :BLK] = nt(cot[...], w[rows(owner), :]).astype(BF16)
        outs[d][:, BLK:] = cot[:, pl.ds(pl.multiple_of(owner * BLK, BLK), BLK)]


def keep_rows(qpos, kpos, ends):
    r = qpos + lax.broadcasted_iota(jnp.int32, (BLK, 1), 0)
    c = kpos + lax.broadcasted_iota(jnp.int32, (1, BLK), 1)
    return jnp.where((c >= start_of(r, ends)) & (c <= r), SCALE, 0.0)


def keep_cols(qpos, kpos, ends):
    r = qpos + lax.broadcasted_iota(jnp.int32, (1, BLK), 1)
    c = kpos + lax.broadcasted_iota(jnp.int32, (BLK, 1), 0)
    return jnp.where((c >= start_of(r, ends)) & (c <= r), SCALE, 0.0)


def attend(q, kv, att, i, j, keep):
    for h in range(2):
        u = nt(q[rows(i), head(h)], kv[rows(j), head(h)])
        w = (u * (1.0 + jnp.tanh(u)) * keep).astype(BF16)
        att[rows(i), head(h)] += nn(w, kv[rows(j), head(h, BLK)])


def block_of(parts, k):
    part, at = ((0, 0), (1, 0), (2, 0), (1, BLK))[k]
    return parts[part][at : at + BLK, :]


def forward_local_body(info, *refs):
    q_in, kv_in = refs[0:3], refs[3:6]
    q, kv, att = refs[6:]
    ends = history_ends(info)
    base = info[8] * GRP
    for k in range(NB):
        at = rows(lax.rem(info[9] + k, NB))
        q[at, :] = block_of(q_in, k)
        kv[at, :] = block_of(kv_in, k)
    att[...] = jnp.zeros_like(att)

    def over_i(i, _):
        qpos = base + i * BLK
        first = jnp.maximum(start_of(qpos, ends) - base, 0) // BLK

        def over_j(j, _):
            attend(q, kv, att, i, j, keep_rows(qpos, base + j * BLK, ends))
            return 0

        return lax.fori_loop(first, i + 1, over_j, 0)

    lax.fori_loop(0, NB, over_i, 0)


def halo_first(i, qpos, prev, ends):
    start = start_of(qpos, ends)
    return jnp.where(start >= prev + GRP, NB, jnp.maximum((start - prev) // BLK, i))


def forward_halo_body(info, *refs):
    q, att_in = refs[0:2]
    kv_in, gg_in, gate_in = refs[2:5], refs[5:9], refs[9:12]
    att, kv, gg, cot, gate, stats = refs[12:18]
    ends = history_ends(info)
    base = info[8] * GRP
    prev = base - GRP
    att[...] = att_in[...]
    for k in range(NB):
        at = rows(lax.rem(info[9] + k, NB))
        kv[at, :] = block_of(kv_in, k)
        gate[at, :] = block_of(gate_in, k)
        gg[at, :] = gg_in[(4 - k) % 4][:, :BLK]
        cot[at, :] = gg_in[(4 - k) % 4][:, BLK:]

    def over_i(i, _):
        qpos = base + i * BLK

        def over_j(j, _):
            attend(q, kv, att, i, j, keep_rows(qpos, prev + j * BLK, ends))
            return 0

        return lax.fori_loop(halo_first(i, qpos, prev, ends), NB, over_j, 0)

    lax.fori_loop(0, NB, over_i, 0)
    a = att[...]
    gn = gg[...].astype(F32) * gate[...].astype(F32)
    mean = jnp.sum(a, axis=1, keepdims=True) / BLK
    cent = a - mean
    m2 = jnp.sum(cent * cent, axis=1, keepdims=True)
    g1 = jnp.sum(gn, axis=1, keepdims=True)
    ga = jnp.sum(gn * cent, axis=1, keepdims=True)
    lane = lax.broadcasted_iota(jnp.int32, (GRP, DH), 1)
    packed = jnp.where(lane == 0, mean, jnp.where(lane == 1, m2, jnp.where(lane == 2, g1, ga)))
    stats[...] = packed.T[:8, :]


def norm_body(info, *refs):
    att, gg, gate = refs[0:3]
    stats, dsig = refs[3:7], refs[7:11]
    gatt, gated, gp, table = refs[11:15]
    parts = [s[...] for s in stats]
    mean = (parts[0][0:1] + parts[1][0:1] + parts[2][0:1] + parts[3][0:1]) * 0.25
    m2 = jnp.zeros_like(mean)
    g1 = jnp.zeros_like(mean)
    ga = jnp.zeros_like(mean)
    for p in parts:
        off = p[0:1] - mean
        m2 = m2 + p[1:2] + BLK * off * off
        g1 = g1 + p[2:3]
        ga = ga + p[3:4] + off * p[2:3]
    inv = lax.rsqrt(m2 / D + 1e-6)
    row = lax.broadcasted_iota(jnp.int32, (DH, GRP), 0)
    cols = jnp.where(row == 0, mean, jnp.where(row == 1, inv, jnp.where(row == 2, g1 / D, ga * inv / D)))
    table[...] = cols.T
    for k in range(NB):
        at = rows(lax.rem(info[9] + k, NB))
        t = table[at, :]
        mean_c, inv_c, g1_c, ga_c = (t[:, n : n + 1] for n in range(4))
        normed = (att[at, :] - mean_c) * inv_c
        g = gate[at, :].astype(F32)
        grad_gated = gg[at, :].astype(F32)
        gatt[at, :] = (inv_c * (grad_gated * g - g1_c - normed * ga_c)).astype(BF16)
        gated[at, :] = (normed * g).astype(BF16)
        gp[at, :] = (grad_gated * normed * dsig[k][:, 0:BLK].astype(F32)).astype(BF16)


def early_weights_body(info, *refs):
    ev, (gp_g, gp_q, acc) = refs[0:4], refs[4:7]
    for k in range(NB):
        at = rows(lax.rem(info[9] + k, NB))
        for lanes, gp in ((slice(0, BLK), gp_g), (slice(BLK, 2 * BLK), gp_q)):
            part = tn(ev[k][...], gp[at, :])
            acc[:, lanes] = part if k == 0 else acc[:, lanes] + part


def late_weights_body(info, *refs):
    ev, gp, gated = refs[0:4], refs[4:8], refs[8:12]
    cot, early, send, keep, acc = refs[12:17]
    for k in range(NB):
        part = tn(ev[k][...], gp[k][:, 2 * BLK :])
        acc[:, : 2 * BLK] = part if k == 0 else acc[:, : 2 * BLK] + part
        acc[rows(lax.rem(info[9] + k, NB)), 2 * BLK :] = tn(gated[k][...], cot[...])
    for x in range(4):
        for out, c, kind in ((send, 1 - info[10], BF16), (keep, info[10], F32)):
            at = pl.ds(pl.multiple_of((x * 2 + c) * 128, 128), 128)
            out[x, :, : 2 * BLK] = early[at, :].astype(kind)
            out[x, :, 2 * BLK :] = acc[at, :].astype(kind)


def add_core_body(info, keep, got, out):
    out[...] = (keep[...] + got[...].astype(F32)).astype(BF16)


def add_x_body(info, got, total):
    part = got[0].astype(F32) + got[1].astype(F32) + got[2].astype(F32) + got[3].astype(F32)
    total[...] = part.astype(BF16)


def last_sum_body(info, got, grad_w_in, grad_w_out):
    for z in range(4):
        part = got[z].astype(F32)
        for y in range(1, 4):
            part = part + got[y * 4 + z].astype(F32)
        part = part.astype(BF16)
        for n, to in enumerate((0, 2, 1, 3)):
            at = to * D + z * BLK
            grad_w_in[:, at : at + BLK] = part[:, n * BLK : (n + 1) * BLK]
        grad_w_out[:, z * BLK : (z + 1) * BLK] = part[:, 4 * BLK :]


def silu_parts(u):
    t = jnp.tanh(u)
    a = 1.0 + t
    ut = u * t
    return u + ut, a * ((1.0 + u) - ut)


def key_side(q, g, kv, dkv, dq, i, j, keep):
    half = keep * 0.5
    for h in range(2):
        qi, gi = q[rows(i), head(h)], g[rows(i), head(h)]
        kj, vj = kv[rows(j), head(h)], kv[rows(j), head(h, BLK)]
        silu, slope = silu_parts(nt(kj, qi))
        w = (silu * keep).astype(BF16)
        ds = (nt(vj, gi) * slope * half).astype(BF16)
        dkv[rows(j), head(h, BLK)] += nn(w, gi)
        dkv[rows(j), head(h)] += nn(ds, qi)
        if dq is not None:
            dq[rows(i), head(h)] += tn(ds, kj)


def query_side(q, g, kv, dq, i, j, keep):
    half = keep * 0.5
    for h in range(2):
        kj, vj = kv[rows(j), head(h)], kv[rows(j), head(h, BLK)]
        slope = silu_parts(nt(q[rows(i), head(h)], kj))[1]
        ds = (nt(g[rows(i), head(h)], vj) * slope * half).astype(BF16)
        dq[rows(i), head(h)] += nn(ds, kj)


def backward_local_body(info, *refs):
    q, g, kv, kv_prev = refs[0:4]
    dsig = refs[4:8]
    gp_q, dkv, dq = refs[8:11]
    ends = history_ends(info)
    base = info[8] * GRP
    prev = base - GRP
    dq[...] = jnp.zeros_like(dq)
    dkv[...] = jnp.zeros_like(dkv)

    def over_j(j, _):
        kpos = base + j * BLK
        last = jnp.minimum((end_of(kpos + BLK - 1, ends) - 1 - base) // BLK, NB - 1)

        def over_i(i, _):
            key_side(q, g, kv, dkv, dq, i, j, keep_cols(base + i * BLK, kpos, ends))
            return 0

        return lax.fori_loop(j, last + 1, over_i, 0)

    lax.fori_loop(0, NB, over_j, 0)

    def halo_i(i, _):
        qpos = base + i * BLK

        def halo_j(j, _):
            query_side(q, g, kv_prev, dq, i, j, keep_rows(qpos, prev + j * BLK, ends))
            return 0

        return lax.fori_loop(halo_first(i, qpos, prev, ends), NB, halo_j, 0)

    lax.fori_loop(0, NB, halo_i, 0)
    for k in range(NB):
        at = rows(lax.rem(info[9] + k, NB))
        gp_q[at, :] = (dq[at, :] * dsig[k][:, 2 * BLK : 3 * BLK].astype(F32)).astype(BF16)


def backward_later_body(info, *refs):
    q, g, kv, dkv_in, gp_g, gp_q = refs[0:6]
    dsig, gp = refs[6:10], refs[10:14]
    dkv = refs[14]
    ends = history_ends(info)
    base = info[8] * GRP
    later = base + GRP
    dkv[...] = dkv_in[...]

    def over_j(j, _):
        kpos = base + j * BLK
        end = end_of(kpos + BLK - 1, ends)
        count = jnp.where(end > later, jnp.minimum((end - 1 - later) // BLK, j) + 1, 0)

        def over_i(i, _):
            key_side(q, g, kv, dkv, None, i, j, keep_cols(later + i * BLK, kpos, ends))
            return 0

        return lax.fori_loop(0, count, over_i, 0)

    lax.fori_loop(0, NB, over_j, 0)
    for k in range(NB):
        at = rows(lax.rem(info[9] + k, NB))
        dk = 2.0 * dkv[at, 0:BLK]
        gp[k][:, :BLK] = gp_g[at, :]
        gp[k][:, BLK : 2 * BLK] = gp_q[at, :]
        gp[k][:, 2 * BLK : 3 * BLK] = (dkv[at, BLK:] * dsig[k][:, BLK : 2 * BLK].astype(F32)).astype(BF16)
        gp[k][:, 3 * BLK :] = (dk * dsig[k][:, 3 * BLK :].astype(F32)).astype(BF16)


def input_body(info, *refs):
    gp, w, (cot, out, acc) = refs[0:4], refs[4:8], refs[8:11]
    for d in range(NB):

        @pl.when(pl.program_id(0) == d)
        def _(d=d):
            part = cot[...].astype(F32) if d == 0 else acc[...]
            for n in range(4):
                part = part + nt(gp[d][:, n * BLK : (n + 1) * BLK], w[n][...])
            if d < NB - 1:
                acc[...] = part
            else:
                out[...] = part.astype(BF16)


def input_grad(info, gp, w_in, cot):
    def columns(part):
        return pl.BlockSpec((D, BLK), lambda d, at: (0, part * 4 + lax.rem(at[9] + NB - d, NB)))

    whole = pl.BlockSpec((BLK, D), lambda d, at: (0, 0))
    return pl.pallas_call(
        input_body,
        grid_spec=pltpu.PrefetchScalarGridSpec(
            num_scalar_prefetch=1,
            grid=(NB,),
            in_specs=[whole] * 4 + [columns(p) for p in (0, 2, 1, 3)] + [whole],
            out_specs=whole,
            scratch_shapes=[pltpu.VMEM((BLK, D), F32)],
        ),
        out_shape=bf16((BLK, D)),
        compiler_params=pltpu.CompilerParams(vmem_limit_bytes=20 * 1024 * 1024),
        cost_estimate=pl.CostEstimate(flops=40 << 30, bytes_accessed=8 << 20, transcendentals=0),
    )(info, *gp, w_in, w_in, w_in, w_in, cot)


def along(x, axis, d):
    return lax.ppermute(x, axis, [(i, (i + d) % 4) for i in range(4)])


def swap(x):
    return lax.ppermute(x, "c", [(0, 1), (1, 0)])


def gather_z(x):
    return [x, along(x, "z", -1), along(x, "z", 2), along(x, "z", 1)]


def exchange(parts, axis):
    return [parts[0]] + [along(parts[d], axis, d) for d in (1, 2, 3)]


def f32(shape):
    return jax.ShapeDtypeStruct(shape, F32)


def bf16(shape):
    return jax.ShapeDtypeStruct(shape, BF16)


def body(events, cotangent, hist, w_in, w_out):
    z = lax.axis_index("z")
    info = jnp.concatenate(
        [hist[0], jnp.stack([lax.axis_index("y"), z, lax.axis_index("c"), lax.axis_index("x")]).astype(jnp.int32)]
    )
    ev, cot = events[0], cotangent[0]
    near = along(ev, "z", -1), along(ev, "z", 1)
    evs = [ev, near[0], None, near[1]]
    kvs, qs, gs, dsigs, kv_prevs = [], [], [], [None] * 4, []
    for blocks in ((0,), (1, 3), (2,)):
        n = len(blocks)
        if blocks == (1, 3):
            ev_far, *near, _ = lax.optimization_barrier((ev, *near, kvs[0]))
            evs = [ev, near[0], along(ev_far, "z", 2), near[1]]
        kv, q, g, *dsig = call(
            project_body,
            (bf16((n * BLK, 2 * BLK)), bf16((n * BLK, BLK)), bf16((n * BLK, BLK))) + (bf16((BLK, 4 * BLK)),) * n,
            n + 1, 2 * n * BLK * D * D, 4 << 20,
        )(info, *[evs[b] for b in blocks], w_in)
        kvs.append(kv)
        qs.append(q)
        gs.append(g)
        for b, d in zip(blocks, dsig):
            dsigs[b] = d
        kv_prevs.append(along(kv, "y", 1))
    ggs = call(grad_gated_body, (bf16((BLK, 2 * BLK)),) * 4, 2, 1 << 29, 2 << 20)(info, cot, w_out)
    *ggs, _ = lax.optimization_barrier((*ggs, evs[2]))
    ggs = exchange(ggs, "z")
    q, kv, att = call(
        forward_local_body, (bf16((GRP, BLK)), bf16((GRP, 2 * BLK)), f32((GRP, BLK))), 6, 5 << 30, 4 << 20
    )(info, *qs, *kvs)
    q_next = along(q, "y", -1)
    att, kv_prev, gg, cot_z, gate, stats = call(
        forward_halo_body,
        (f32((GRP, BLK)), bf16((GRP, 2 * BLK))) + (bf16((GRP, BLK)),) * 3 + (f32((8, GRP)),),
        12, 5 << 30, 4 << 20,
    )(info, q, att, *kv_prevs, *ggs, *gs)
    gatt, gated, gp_g = call(
        norm_body, (bf16((GRP, BLK)),) * 3, 11, 1 << 30, 4 << 20, [pltpu.VMEM((GRP, DH), F32)]
    )(info, att, gg, gate, *gather_z(stats), *dsigs)
    g_next = along(gatt, "y", -1)
    gateds = gather_z(gated)
    gp_q, dkv = call(
        backward_local_body, (bf16((GRP, BLK)), f32((GRP, 2 * BLK))), 8, 1 << 20, 1 << 20,
        [pltpu.VMEM((GRP, BLK), F32)],
    )(info, q, gatt, kv, kv_prev, *dsigs)
    early = call(early_weights_body, f32((D, 2 * BLK)), 6, 1 << 20, 1 << 20)(info, *evs, gp_g, gp_q)
    q_next, g_next, early = lax.optimization_barrier((q_next, g_next, early))
    gp = call(
        backward_later_body, (bf16((BLK, 4 * BLK)),) * 4, 10, 5 << 30, 4 << 20, [pltpu.VMEM((GRP, 2 * BLK), F32)]
    )(info, q_next, g_next, kv, dkv, gp_g, gp_q, *dsigs)
    send, keep = call(
        late_weights_body,
        (bf16((4, 128, 5 * BLK)), f32((4, 128, 5 * BLK))), 14, 1 << 20, 1 << 20,
        [pltpu.VMEM((D, 3 * BLK), F32)],
    )(info, *evs, *gp, *gateds, cot_z, early)
    gp_rows = exchange(gp, "z")
    mine = call(
        add_core_body, bf16((4, 128, 5 * BLK)), 2, 1 << 20, 1 << 20
    )(info, keep, swap(send))
    sums = lax.all_to_all(mine, "x", 0, 0)
    grad_events = input_grad(info, gp_rows, w_in, cot)
    sums, grad_events = lax.optimization_barrier((sums, grad_events))
    total = call(add_x_body, bf16((128, 5 * BLK)), 1, 1 << 20, 1 << 20)(info, sums)
    got = lax.all_to_all(total.reshape(16, 8, 5 * BLK), ("y", "z"), 0, 0)
    grad_w_in, grad_w_out = call(last_sum_body, (bf16((8, 4 * D)), bf16((8, D))), 1, 1 << 20, 1 << 20)(info, got)
    return grad_events[None], grad_w_in, grad_w_out


def solution(mesh):
    axes = ("x", "c", "y", "z")
    split = Mesh(mesh.devices.reshape(4, 2, 4, 4), axes)
    dp, seq = ("x", "c"), ("y", "z")
    return jax.shard_map(
        body,
        mesh=split,
        in_specs=(P(dp, seq, None), P(dp, seq, None), P(dp, None), P(), P()),
        out_specs=(P(dp, seq, None), P(axes, None), P(axes, None)),
        check_vma=False,
    )
```

```python
import jax
import jax.numpy as jnp
from jax import lax
from jax.experimental import pallas as pl
from jax.experimental.pallas import tpu as pltpu
from jax.sharding import Mesh
from jax.sharding import PartitionSpec as P

BLK = 256
NB = 4
DH = 128
GRP = NB * BLK
D = 1024
F32 = jnp.float32
BF16 = jnp.bfloat16
SCALE = 1.0 / 256.0
VMEM = pl.BlockSpec(memory_space=pltpu.VMEM)
SMEM = pl.BlockSpec(memory_space=pltpu.SMEM)


def call(body, outs, n_in, flops, nbytes, scratch=(), scalars=1):
    return pl.pallas_call(
        body,
        out_shape=outs,
        in_specs=[SMEM] * scalars + [VMEM] * n_in,
        out_specs=jax.tree.map(lambda _: VMEM, outs),
        scratch_shapes=scratch,
        compiler_params=pltpu.CompilerParams(vmem_limit_bytes=20 * 1024 * 1024),
        cost_estimate=pl.CostEstimate(flops=flops, bytes_accessed=nbytes, transcendentals=0),
    )


def nt(a, b):
    return lax.dot_general(a, b, (((1,), (1,)), ((), ())), preferred_element_type=F32)


def nn(a, b):
    return lax.dot_general(a, b, (((1,), (0,)), ((), ())), preferred_element_type=F32)


def tn(a, b):
    return lax.dot_general(a, b, (((0,), (0,)), ((), ())), preferred_element_type=F32)


def history_ends(info):
    ends, total = [], jnp.int32(0)
    for k in range(8):
        total = total + info[k]
        ends.append(total)
    return ends


def start_of(pos, ends):
    start = jnp.zeros_like(pos)
    for e in ends:
        start = jnp.where(pos >= e, e, start)
    return start


def end_of(pos, ends):
    end = ends[-1]
    for e in reversed(ends):
        end = jnp.where(e > pos, e, end)
    return end


def rows(i):
    return pl.ds(pl.multiple_of(i * BLK, BLK), BLK)


def head(h, base=0):
    return slice(base + h * DH, base + (h + 1) * DH)


def project_body(info, *refs):
    n = (len(refs) - 4) // 2
    ev, (w, kv, q, g), dsig = refs[:n], refs[n : n + 4], refs[n + 4 :]
    for b in range(n):
        x, at = ev[b][...], slice(b * BLK, (b + 1) * BLK)
        for p in range(4):
            lanes = pl.ds(pl.multiple_of(p * D + info[9] * BLK, BLK), BLK)
            proj = nn(x, w[:, lanes])
            sig = 0.5 + 0.5 * jnp.tanh(0.5 * proj)
            act = (proj * sig).astype(BF16)
            if p == 0:
                g[at, :] = act
            elif p == 1:
                kv[at, BLK:] = act
            elif p == 2:
                q[at, :] = (0.5 * act.astype(F32)).astype(BF16)
            else:
                kv[at, :BLK] = act
            dsig[b][:, p * BLK : (p + 1) * BLK] = (sig * (1.0 + proj * (1.0 - sig))).astype(BF16)


def grad_gated_body(info, cot, w, *outs):
    for d in range(NB):
        owner = lax.rem(info[9] + d, NB)
        outs[d][:, :BLK] = nt(cot[...], w[rows(owner), :]).astype(BF16)
        outs[d][:, BLK:] = cot[:, pl.ds(pl.multiple_of(owner * BLK, BLK), BLK)]


def keep_rows(qpos, kpos, ends):
    r = qpos + lax.broadcasted_iota(jnp.int32, (BLK, 1), 0)
    c = kpos + lax.broadcasted_iota(jnp.int32, (1, BLK), 1)
    return jnp.where((c >= start_of(r, ends)) & (c <= r), SCALE, 0.0)


def keep_cols(qpos, kpos, ends):
    r = qpos + lax.broadcasted_iota(jnp.int32, (1, BLK), 1)
    c = kpos + lax.broadcasted_iota(jnp.int32, (BLK, 1), 0)
    return jnp.where((c >= start_of(r, ends)) & (c <= r), SCALE, 0.0)


def attend(q, kv, att, i, j, keep):
    for h in range(2):
        u = nt(q[rows(i), head(h)], kv[rows(j), head(h)])
        w = (u * (1.0 + jnp.tanh(u)) * keep).astype(BF16)
        att[rows(i), head(h)] += nn(w, kv[rows(j), head(h, BLK)])


def block_of(parts, k):
    part, at = ((0, 0), (1, 0), (2, 0), (1, BLK))[k]
    return parts[part][at : at + BLK, :]


def forward_local_body(info, *refs):
    q_in, kv_in = refs[0:3], refs[3:6]
    q, kv, att = refs[6:]
    ends = history_ends(info)
    base = info[8] * GRP
    for k in range(NB):
        at = rows(lax.rem(info[9] + k, NB))
        q[at, :] = block_of(q_in, k)
        kv[at, :] = block_of(kv_in, k)
    att[...] = jnp.zeros_like(att)

    def over_i(i, _):
        qpos = base + i * BLK
        first = jnp.maximum(start_of(qpos, ends) - base, 0) // BLK

        def over_j(j, _):
            attend(q, kv, att, i, j, keep_rows(qpos, base + j * BLK, ends))
            return 0

        return lax.fori_loop(first, i + 1, over_j, 0)

    lax.fori_loop(0, NB, over_i, 0)


def halo_first(i, qpos, prev, ends):
    start = start_of(qpos, ends)
    return jnp.where(start >= prev + GRP, NB, jnp.maximum((start - prev) // BLK, i))


def forward_halo_body(info, *refs):
    q, att_in = refs[0:2]
    kv_in, gg_in, gate_in = refs[2:5], refs[5:9], refs[9:12]
    att, kv, gg, cot, gate, stats = refs[12:18]
    ends = history_ends(info)
    base = info[8] * GRP
    prev = base - GRP
    att[...] = att_in[...]
    for k in range(NB):
        at = rows(lax.rem(info[9] + k, NB))
        kv[at, :] = block_of(kv_in, k)
        gate[at, :] = block_of(gate_in, k)
        gg[at, :] = gg_in[(4 - k) % 4][:, :BLK]
        cot[at, :] = gg_in[(4 - k) % 4][:, BLK:]

    def over_i(i, _):
        qpos = base + i * BLK

        def over_j(j, _):
            attend(q, kv, att, i, j, keep_rows(qpos, prev + j * BLK, ends))
            return 0

        return lax.fori_loop(halo_first(i, qpos, prev, ends), NB, over_j, 0)

    lax.fori_loop(0, NB, over_i, 0)
    a = att[...]
    gn = gg[...].astype(F32) * gate[...].astype(F32)
    mean = jnp.sum(a, axis=1, keepdims=True) / BLK
    cent = a - mean
    m2 = jnp.sum(cent * cent, axis=1, keepdims=True)
    g1 = jnp.sum(gn, axis=1, keepdims=True)
    ga = jnp.sum(gn * cent, axis=1, keepdims=True)
    lane = lax.broadcasted_iota(jnp.int32, (GRP, DH), 1)
    packed = jnp.where(lane == 0, mean, jnp.where(lane == 1, m2, jnp.where(lane == 2, g1, ga)))
    stats[...] = packed.T[:8, :]


def norm_body(info, *refs):
    att, gg, gate = refs[0:3]
    stats, dsig = refs[3:7], refs[7:11]
    gatt, gated, gp, table = refs[11:15]
    parts = [s[...] for s in stats]
    mean = (parts[0][0:1] + parts[1][0:1] + parts[2][0:1] + parts[3][0:1]) * 0.25
    m2 = jnp.zeros_like(mean)
    g1 = jnp.zeros_like(mean)
    ga = jnp.zeros_like(mean)
    for p in parts:
        off = p[0:1] - mean
        m2 = m2 + p[1:2] + BLK * off * off
        g1 = g1 + p[2:3]
        ga = ga + p[3:4] + off * p[2:3]
    inv = lax.rsqrt(m2 / D + 1e-6)
    row = lax.broadcasted_iota(jnp.int32, (DH, GRP), 0)
    cols = jnp.where(row == 0, mean, jnp.where(row == 1, inv, jnp.where(row == 2, g1 / D, ga * inv / D)))
    table[...] = cols.T
    for k in range(NB):
        at = rows(lax.rem(info[9] + k, NB))
        t = table[at, :]
        mean_c, inv_c, g1_c, ga_c = (t[:, n : n + 1] for n in range(4))
        normed = (att[at, :] - mean_c) * inv_c
        g = gate[at, :].astype(F32)
        grad_gated = gg[at, :].astype(F32)
        gatt[at, :] = (inv_c * (grad_gated * g - g1_c - normed * ga_c)).astype(BF16)
        gated[at, :] = (normed * g).astype(BF16)
        gp[at, :] = (grad_gated * normed * dsig[k][:, 0:BLK].astype(F32)).astype(BF16)


def early_weights_body(info, *refs):
    ev, (gp_g, gp_q, acc) = refs[0:4], refs[4:7]
    for k in range(NB):
        at = rows(lax.rem(info[9] + k, NB))
        for lanes, gp in ((slice(0, BLK), gp_g), (slice(BLK, 2 * BLK), gp_q)):
            part = tn(ev[k][...], gp[at, :])
            acc[:, lanes] = part if k == 0 else acc[:, lanes] + part


def late_weights_body(info, *refs):
    ev, gp, gated = refs[0:4], refs[4:8], refs[8:12]
    cot, early, send, keep, acc = refs[12:17]
    for k in range(NB):
        part = tn(ev[k][...], gp[k][:, 2 * BLK :])
        acc[:, : 2 * BLK] = part if k == 0 else acc[:, : 2 * BLK] + part
        acc[rows(lax.rem(info[9] + k, NB)), 2 * BLK :] = tn(gated[k][...], cot[...])
    for x in range(4):
        for out, c, kind in ((send, 1 - info[10], BF16), (keep, info[10], F32)):
            at = pl.ds(pl.multiple_of((x * 2 + c) * 128, 128), 128)
            out[x, :, : 2 * BLK] = early[at, :].astype(kind)
            out[x, :, 2 * BLK :] = acc[at, :].astype(kind)


def add_core_body(keep, got, out):
    out[...] = (keep[...] + got[...].astype(F32)).astype(BF16)


def add_x_body(got, total):
    part = got[0].astype(F32) + got[1].astype(F32) + got[2].astype(F32) + got[3].astype(F32)
    total[...] = part.astype(BF16)


def last_sum_body(got, grad_w_in, grad_w_out):
    for z in range(4):
        part = got[z].astype(F32)
        for y in range(1, 4):
            part = part + got[y * 4 + z].astype(F32)
        part = part.astype(BF16)
        for n, to in enumerate((0, 2, 1, 3)):
            at = to * D + z * BLK
            grad_w_in[:, at : at + BLK] = part[:, n * BLK : (n + 1) * BLK]
        grad_w_out[:, z * BLK : (z + 1) * BLK] = part[:, 4 * BLK :]


def silu_parts(u):
    t = jnp.tanh(u)
    a = 1.0 + t
    ut = u * t
    return u + ut, a * ((1.0 + u) - ut)


def key_side(q, g, kv, dkv, dq, i, j, keep):
    half = keep * 0.5
    for h in range(2):
        qi, gi = q[rows(i), head(h)], g[rows(i), head(h)]
        kj, vj = kv[rows(j), head(h)], kv[rows(j), head(h, BLK)]
        silu, slope = silu_parts(nt(kj, qi))
        w = (silu * keep).astype(BF16)
        ds = (nt(vj, gi) * slope * half).astype(BF16)
        dkv[rows(j), head(h, BLK)] += nn(w, gi)
        dkv[rows(j), head(h)] += nn(ds, qi)
        if dq is not None:
            dq[rows(i), head(h)] += tn(ds, kj)


def query_side(q, g, kv, dq, i, j, keep):
    half = keep * 0.5
    for h in range(2):
        kj, vj = kv[rows(j), head(h)], kv[rows(j), head(h, BLK)]
        slope = silu_parts(nt(q[rows(i), head(h)], kj))[1]
        ds = (nt(g[rows(i), head(h)], vj) * slope * half).astype(BF16)
        dq[rows(i), head(h)] += nn(ds, kj)


def backward_local_body(info, *refs):
    q, g, kv, kv_prev = refs[0:4]
    dsig = refs[4:8]
    gp_q, dkv, dq = refs[8:11]
    ends = history_ends(info)
    base = info[8] * GRP
    prev = base - GRP
    dq[...] = jnp.zeros_like(dq)
    dkv[...] = jnp.zeros_like(dkv)

    def over_j(j, _):
        kpos = base + j * BLK
        last = jnp.minimum((end_of(kpos + BLK - 1, ends) - 1 - base) // BLK, NB - 1)

        def over_i(i, _):
            key_side(q, g, kv, dkv, dq, i, j, keep_cols(base + i * BLK, kpos, ends))
            return 0

        return lax.fori_loop(j, last + 1, over_i, 0)

    lax.fori_loop(0, NB, over_j, 0)

    def halo_i(i, _):
        qpos = base + i * BLK

        def halo_j(j, _):
            query_side(q, g, kv_prev, dq, i, j, keep_rows(qpos, prev + j * BLK, ends))
            return 0

        return lax.fori_loop(halo_first(i, qpos, prev, ends), NB, halo_j, 0)

    lax.fori_loop(0, NB, halo_i, 0)
    for k in range(NB):
        at = rows(lax.rem(info[9] + k, NB))
        gp_q[at, :] = (dq[at, :] * dsig[k][:, 2 * BLK : 3 * BLK].astype(F32)).astype(BF16)


def backward_later_body(info, *refs):
    q, g, kv, dkv_in, gp_g, gp_q = refs[0:6]
    dsig, gp = refs[6:10], refs[10:14]
    dkv = refs[14]
    ends = history_ends(info)
    base = info[8] * GRP
    later = base + GRP
    dkv[...] = dkv_in[...]

    def over_j(j, _):
        kpos = base + j * BLK
        end = end_of(kpos + BLK - 1, ends)
        count = jnp.where(end > later, jnp.minimum((end - 1 - later) // BLK, j) + 1, 0)

        def over_i(i, _):
            key_side(q, g, kv, dkv, None, i, j, keep_cols(later + i * BLK, kpos, ends))
            return 0

        return lax.fori_loop(0, count, over_i, 0)

    lax.fori_loop(0, NB, over_j, 0)
    for k in range(NB):
        at = rows(lax.rem(info[9] + k, NB))
        dk = 2.0 * dkv[at, 0:BLK]
        gp[k][:, :BLK] = gp_g[at, :]
        gp[k][:, BLK : 2 * BLK] = gp_q[at, :]
        gp[k][:, 2 * BLK : 3 * BLK] = (dkv[at, BLK:] * dsig[k][:, BLK : 2 * BLK].astype(F32)).astype(BF16)
        gp[k][:, 3 * BLK :] = (dk * dsig[k][:, 3 * BLK :].astype(F32)).astype(BF16)


def input_near_body(info, *refs):
    gp, w, (cot, out) = refs[0:3], refs[3:7], refs[7:9]
    for d in range(3):

        @pl.when(pl.program_id(0) == d)
        def _(d=d):
            part = cot[...].astype(F32) if d == 0 else out[...]
            for n in range(4):
                part = part + nt(gp[d][:, n * BLK : (n + 1) * BLK], w[n][...])
            out[...] = part


def input_far_body(info, gp, w, near, out, acc):
    part = nt(gp[...], w[...])
    n = pl.program_id(0)

    @pl.when(n == 0)
    def _():
        acc[...] = near[...] + part

    @pl.when((n > 0) & (n < 3))
    def _():
        acc[...] += part

    @pl.when(n == 3)
    def _():
        out[...] = (acc[...] + part).astype(BF16)


def streamed(body, steps, in_specs, out, scratch, flops):
    return pl.pallas_call(
        body,
        grid_spec=pltpu.PrefetchScalarGridSpec(
            num_scalar_prefetch=1,
            grid=(steps,),
            in_specs=in_specs,
            out_specs=pl.BlockSpec((BLK, D), lambda i, at: (0, 0)),
            scratch_shapes=scratch,
        ),
        out_shape=out,
        compiler_params=pltpu.CompilerParams(vmem_limit_bytes=56 * 1024 * 1024),
        cost_estimate=pl.CostEstimate(flops=flops, bytes_accessed=8 << 20, transcendentals=0),
    )


def input_near(info, gp, w_in, cot):
    def columns(part):
        return pl.BlockSpec((D, BLK), lambda i, at: (0, part * 4 + lax.rem(at[9] + NB - i - i // 2, NB)))

    whole = pl.BlockSpec((BLK, D), lambda i, at: (0, 0))
    specs = [whole] * 3 + [columns(p) for p in (0, 2, 1, 3)] + [whole]
    return streamed(input_near_body, 3, specs, f32((BLK, D)), [], 40 << 30)(
        info, gp[0], gp[1], gp[3], w_in, w_in, w_in, w_in, cot
    )


def input_far(info, gp, w_in, near):
    specs = [
        pl.BlockSpec((BLK, BLK), lambda n, at: (0, n)),
        pl.BlockSpec((D, BLK), lambda n, at: (0, (n % 2 * 2 + n // 2) * 4 + lax.rem(at[9] + 2, NB))),
        pl.BlockSpec((BLK, D), lambda n, at: (0, 0)),
    ]
    return streamed(input_far_body, 4, specs, bf16((BLK, D)), [pltpu.VMEM((BLK, D), F32)], 1 << 30)(
        info, gp[2], w_in, near
    )


def along(x, axis, d):
    return lax.ppermute(x, axis, [(i, (i + d) % 4) for i in range(4)])


def swap(x):
    return lax.ppermute(x, "c", [(0, 1), (1, 0)])


def gather_z(x):
    return [x, along(x, "z", -1), along(x, "z", 2), along(x, "z", 1)]


def exchange(parts, axis):
    return [parts[0]] + [along(parts[d], axis, d) for d in (1, 2, 3)]


def f32(shape):
    return jax.ShapeDtypeStruct(shape, F32)


def bf16(shape):
    return jax.ShapeDtypeStruct(shape, BF16)


def body(events, cotangent, hist, w_in, w_out):
    z = lax.axis_index("z")
    info = jnp.concatenate(
        [hist[0], jnp.stack([lax.axis_index("y"), z, lax.axis_index("c"), lax.axis_index("x")]).astype(jnp.int32)]
    )
    ev, cot = events[0], cotangent[0]
    near = along(ev, "z", -1), along(ev, "z", 1)
    evs = [ev, near[0], None, near[1]]
    kvs, qs, gs, dsigs, kv_prevs = [], [], [], [None] * 4, []
    for blocks in ((0,), (1, 3), (2,)):
        n = len(blocks)
        if blocks == (1, 3):
            ev_far, *near, _ = lax.optimization_barrier((ev, *near, kvs[0]))
            evs = [ev, near[0], along(ev_far, "z", 2), near[1]]
        kv, q, g, *dsig = call(
            project_body,
            (bf16((n * BLK, 2 * BLK)), bf16((n * BLK, BLK)), bf16((n * BLK, BLK))) + (bf16((BLK, 4 * BLK)),) * n,
            n + 1, 2 * n * BLK * D * D, 4 << 20,
        )(info, *[evs[b] for b in blocks], w_in)
        kvs.append(kv)
        qs.append(q)
        gs.append(g)
        for b, d in zip(blocks, dsig):
            dsigs[b] = d
        kv_prevs.append(along(kv, "y", 1))
    ggs = call(grad_gated_body, (bf16((BLK, 2 * BLK)),) * 4, 2, 1 << 29, 2 << 20)(info, cot, w_out)
    *ggs, _ = lax.optimization_barrier((*ggs, evs[2]))
    ggs = exchange(ggs, "z")
    q, kv, att = call(
        forward_local_body, (bf16((GRP, BLK)), bf16((GRP, 2 * BLK)), f32((GRP, BLK))), 6, 5 << 30, 4 << 20
    )(info, *qs, *kvs)
    q_next = along(q, "y", -1)
    att, kv_prev, gg, cot_z, gate, stats = call(
        forward_halo_body,
        (f32((GRP, BLK)), bf16((GRP, 2 * BLK))) + (bf16((GRP, BLK)),) * 3 + (f32((8, GRP)),),
        12, 5 << 30, 4 << 20,
    )(info, q, att, *kv_prevs, *ggs, *gs)
    gatt, gated, gp_g = call(
        norm_body, (bf16((GRP, BLK)),) * 3, 11, 1 << 30, 4 << 20, [pltpu.VMEM((GRP, DH), F32)]
    )(info, att, gg, gate, *gather_z(stats), *dsigs)
    g_next = along(gatt, "y", -1)
    gateds = gather_z(gated)
    gp_q, dkv = call(
        backward_local_body, (bf16((GRP, BLK)), f32((GRP, 2 * BLK))), 8, 1 << 20, 1 << 20,
        [pltpu.VMEM((GRP, BLK), F32)],
    )(info, q, gatt, kv, kv_prev, *dsigs)
    early = call(early_weights_body, f32((D, 2 * BLK)), 6, 1 << 20, 1 << 20)(info, *evs, gp_g, gp_q)
    q_next, g_next, early = lax.optimization_barrier((q_next, g_next, early))
    gp = call(
        backward_later_body, (bf16((BLK, 4 * BLK)),) * 4, 10, 5 << 30, 4 << 20, [pltpu.VMEM((GRP, 2 * BLK), F32)]
    )(info, q_next, g_next, kv, dkv, gp_g, gp_q, *dsigs)
    send, keep = call(
        late_weights_body,
        (bf16((4, 128, 5 * BLK)), f32((4, 128, 5 * BLK))), 14, 1 << 20, 1 << 20,
        [pltpu.VMEM((D, 3 * BLK), F32)],
    )(info, *evs, *gp, *gateds, cot_z, early)
    gp_rows = exchange(gp, "z")
    mine = call(
        add_core_body, bf16((4, 128, 5 * BLK)), 2, 1 << 20, 1 << 20, scalars=0
    )(keep, swap(send))
    sums = lax.all_to_all(mine, "x", 0, 0)
    near_rows = input_near(info, gp_rows, w_in, cot)
    sums, near_rows = lax.optimization_barrier((sums, near_rows))
    total = call(add_x_body, bf16((128, 5 * BLK)), 1, 1 << 20, 1 << 20, scalars=0)(sums)
    _, near_rows = lax.optimization_barrier((total, near_rows))
    grad_events = input_far(info, gp_rows, w_in, near_rows)
    got = lax.all_to_all(total.reshape(16, 8, 5 * BLK), ("y", "z"), 0, 0)
    grad_w_in, grad_w_out = call(last_sum_body, (bf16((8, 4 * D)), bf16((8, D))), 1, 1 << 20, 1 << 20, scalars=0)(got)
    return grad_events[None], grad_w_in, grad_w_out


def solution(mesh):
    axes = ("x", "c", "y", "z")
    split = Mesh(mesh.devices.reshape(4, 2, 4, 4), axes)
    dp, seq = ("x", "c"), ("y", "z")
    return jax.shard_map(
        body,
        mesh=split,
        in_specs=(P(dp, seq, None), P(dp, seq, None), P(dp, None), P(), P()),
        out_specs=(P(dp, seq, None), P(axes, None), P(axes, None)),
        check_vma=False,
    )
```

```python
import jax
import jax.numpy as jnp
from jax import lax
from jax.experimental import pallas as pl
from jax.experimental.pallas import tpu as pltpu
from jax.sharding import Mesh
from jax.sharding import PartitionSpec as P

BLK = 256
NB = 4
DH = 128
GRP = NB * BLK
D = 1024
F32 = jnp.float32
BF16 = jnp.bfloat16
SCALE = 1.0 / 256.0
VMEM = pl.BlockSpec(memory_space=pltpu.VMEM)
SMEM = pl.BlockSpec(memory_space=pltpu.SMEM)


def call(body, outs, n_in, flops, nbytes, scratch=(), scalars=1):
    return pl.pallas_call(
        body,
        out_shape=outs,
        in_specs=[SMEM] * scalars + [VMEM] * n_in,
        out_specs=jax.tree.map(lambda _: VMEM, outs),
        scratch_shapes=scratch,
        compiler_params=pltpu.CompilerParams(vmem_limit_bytes=20 * 1024 * 1024),
        cost_estimate=pl.CostEstimate(flops=flops, bytes_accessed=nbytes, transcendentals=0),
    )


def nt(a, b):
    return lax.dot_general(a, b, (((1,), (1,)), ((), ())), preferred_element_type=F32)


def nn(a, b):
    return lax.dot_general(a, b, (((1,), (0,)), ((), ())), preferred_element_type=F32)


def tn(a, b):
    return lax.dot_general(a, b, (((0,), (0,)), ((), ())), preferred_element_type=F32)


def history_ends(info):
    ends, total = [], jnp.int32(0)
    for k in range(8):
        total = total + info[k]
        ends.append(total)
    return ends


def start_of(pos, ends):
    start = jnp.zeros_like(pos)
    for e in ends:
        start = jnp.where(pos >= e, e, start)
    return start


def end_of(pos, ends):
    end = ends[-1]
    for e in reversed(ends):
        end = jnp.where(e > pos, e, end)
    return end


def rows(i):
    return pl.ds(pl.multiple_of(i * BLK, BLK), BLK)


def head(h, base=0):
    return slice(base + h * DH, base + (h + 1) * DH)


def project_body(info, *refs):
    n = (len(refs) - 4) // 2
    ev, (w, kv, q, g), dsig = refs[:n], refs[n : n + 4], refs[n + 4 :]
    for b in range(n):
        x, at = ev[b][...], slice(b * BLK, (b + 1) * BLK)
        for p in range(4):
            lanes = pl.ds(pl.multiple_of(p * D + info[9] * BLK, BLK), BLK)
            proj = nn(x, w[:, lanes])
            sig = 0.5 + 0.5 * jnp.tanh(0.5 * proj)
            act = (proj * sig).astype(BF16)
            if p == 0:
                g[at, :] = act
            elif p == 1:
                kv[at, BLK:] = act
            elif p == 2:
                q[at, :] = (0.5 * act.astype(F32)).astype(BF16)
            else:
                kv[at, :BLK] = act
            dsig[b][:, p * BLK : (p + 1) * BLK] = (sig * (1.0 + proj * (1.0 - sig))).astype(BF16)


def grad_gated_body(info, cot, w, *outs):
    for d in range(NB):
        owner = lax.rem(info[9] + d, NB)
        outs[d][:, :BLK] = nt(cot[...], w[rows(owner), :]).astype(BF16)
        outs[d][:, BLK:] = cot[:, pl.ds(pl.multiple_of(owner * BLK, BLK), BLK)]


def keep_rows(qpos, kpos, ends):
    r = qpos + lax.broadcasted_iota(jnp.int32, (BLK, 1), 0)
    c = kpos + lax.broadcasted_iota(jnp.int32, (1, BLK), 1)
    return jnp.where((c >= start_of(r, ends)) & (c <= r), SCALE, 0.0)


def keep_cols(qpos, kpos, ends):
    r = qpos + lax.broadcasted_iota(jnp.int32, (1, BLK), 1)
    c = kpos + lax.broadcasted_iota(jnp.int32, (BLK, 1), 0)
    return jnp.where((c >= start_of(r, ends)) & (c <= r), SCALE, 0.0)


def attend(q, kv, att, i, j, keep):
    for h in range(2):
        u = nt(q[rows(i), head(h)], kv[rows(j), head(h)])
        w = (u * (1.0 + jnp.tanh(u)) * keep).astype(BF16)
        att[rows(i), head(h)] += nn(w, kv[rows(j), head(h, BLK)])


def block_of(parts, k):
    part, at = ((0, 0), (1, 0), (2, 0), (1, BLK))[k]
    return parts[part][at : at + BLK, :]


def forward_local_body(info, *refs):
    q_in, kv_in = refs[0:3], refs[3:6]
    q, kv, att = refs[6:]
    ends = history_ends(info)
    base = info[8] * GRP
    for k in range(NB):
        at = rows(lax.rem(info[9] + k, NB))
        q[at, :] = block_of(q_in, k)
        kv[at, :] = block_of(kv_in, k)
    att[...] = jnp.zeros_like(att)

    def over_i(i, _):
        qpos = base + i * BLK
        first = jnp.maximum(start_of(qpos, ends) - base, 0) // BLK

        def over_j(j, _):
            attend(q, kv, att, i, j, keep_rows(qpos, base + j * BLK, ends))
            return 0

        return lax.fori_loop(first, i + 1, over_j, 0)

    lax.fori_loop(0, NB, over_i, 0)


def halo_first(i, qpos, prev, ends):
    start = start_of(qpos, ends)
    return jnp.where(start >= prev + GRP, NB, jnp.maximum((start - prev) // BLK, i))


def forward_halo_body(info, *refs):
    q, att_in = refs[0:2]
    kv_in, gg_in, gate_in = refs[2:5], refs[5:9], refs[9:12]
    att, kv, gg, cot, gate, stats = refs[12:18]
    ends = history_ends(info)
    base = info[8] * GRP
    prev = base - GRP
    att[...] = att_in[...]
    for k in range(NB):
        at = rows(lax.rem(info[9] + k, NB))
        kv[at, :] = block_of(kv_in, k)
        gate[at, :] = block_of(gate_in, k)
        gg[at, :] = gg_in[(4 - k) % 4][:, :BLK]
        cot[at, :] = gg_in[(4 - k) % 4][:, BLK:]

    def over_i(i, _):
        qpos = base + i * BLK

        def over_j(j, _):
            attend(q, kv, att, i, j, keep_rows(qpos, prev + j * BLK, ends))
            return 0

        return lax.fori_loop(halo_first(i, qpos, prev, ends), NB, over_j, 0)

    lax.fori_loop(0, NB, over_i, 0)
    a = att[...]
    gn = gg[...].astype(F32) * gate[...].astype(F32)
    mean = jnp.sum(a, axis=1, keepdims=True) / BLK
    cent = a - mean
    m2 = jnp.sum(cent * cent, axis=1, keepdims=True)
    g1 = jnp.sum(gn, axis=1, keepdims=True)
    ga = jnp.sum(gn * cent, axis=1, keepdims=True)
    lane = lax.broadcasted_iota(jnp.int32, (GRP, DH), 1)
    packed = jnp.where(lane == 0, mean, jnp.where(lane == 1, m2, jnp.where(lane == 2, g1, ga)))
    stats[...] = packed.T[:8, :]


def norm_body(info, *refs):
    att, gg, gate = refs[0:3]
    stats, dsig = refs[3:7], refs[7:11]
    gatt, gated, gp, table = refs[11:15]
    parts = [s[...] for s in stats]
    mean = (parts[0][0:1] + parts[1][0:1] + parts[2][0:1] + parts[3][0:1]) * 0.25
    m2 = jnp.zeros_like(mean)
    g1 = jnp.zeros_like(mean)
    ga = jnp.zeros_like(mean)
    for p in parts:
        off = p[0:1] - mean
        m2 = m2 + p[1:2] + BLK * off * off
        g1 = g1 + p[2:3]
        ga = ga + p[3:4] + off * p[2:3]
    inv = lax.rsqrt(m2 / D + 1e-6)
    row = lax.broadcasted_iota(jnp.int32, (DH, GRP), 0)
    cols = jnp.where(row == 0, mean, jnp.where(row == 1, inv, jnp.where(row == 2, g1 / D, ga * inv / D)))
    table[...] = cols.T
    for k in range(NB):
        at = rows(lax.rem(info[9] + k, NB))
        t = table[at, :]
        mean_c, inv_c, g1_c, ga_c = (t[:, n : n + 1] for n in range(4))
        normed = (att[at, :] - mean_c) * inv_c
        g = gate[at, :].astype(F32)
        grad_gated = gg[at, :].astype(F32)
        gatt[at, :] = (inv_c * (grad_gated * g - g1_c - normed * ga_c)).astype(BF16)
        gated[at, :] = (normed * g).astype(BF16)
        gp[at, :] = (grad_gated * normed * dsig[k][:, 0:BLK].astype(F32)).astype(BF16)


def early_weights_body(info, *refs):
    ev, (gp_g, gp_q, acc) = refs[0:4], refs[4:7]
    for k in range(NB):
        at = rows(lax.rem(info[9] + k, NB))
        for lanes, gp in ((slice(0, BLK), gp_g), (slice(BLK, 2 * BLK), gp_q)):
            part = tn(ev[k][...], gp[at, :])
            acc[:, lanes] = part if k == 0 else acc[:, lanes] + part


def late_weights_body(info, *refs):
    ev, gp, gated = refs[0:4], refs[4:8], refs[8:12]
    cot, early, send, keep, acc = refs[12:17]
    for k in range(NB):
        part = tn(ev[k][...], gp[k][:, 2 * BLK :])
        acc[:, : 2 * BLK] = part if k == 0 else acc[:, : 2 * BLK] + part
        acc[rows(lax.rem(info[9] + k, NB)), 2 * BLK :] = tn(gated[k][...], cot[...])
    for x in range(4):
        for out, c, kind in ((send, 1 - info[10], BF16), (keep, info[10], F32)):
            at = pl.ds(pl.multiple_of((x * 2 + c) * 128, 128), 128)
            out[x, :, : 2 * BLK] = early[at, :].astype(kind)
            out[x, :, 2 * BLK :] = acc[at, :].astype(kind)


def add_core_body(keep, got, out):
    out[...] = (keep[...] + got[...].astype(F32)).astype(BF16)


def add_x_body(got, total):
    part = got[0].astype(F32) + got[1].astype(F32) + got[2].astype(F32) + got[3].astype(F32)
    total[...] = part.astype(BF16)


def last_sum_body(got, grad_w_in, grad_w_out):
    for z in range(4):
        part = got[z].astype(F32)
        for y in range(1, 4):
            part = part + got[y * 4 + z].astype(F32)
        part = part.astype(BF16)
        for n, to in enumerate((0, 2, 1, 3)):
            at = to * D + z * BLK
            grad_w_in[:, at : at + BLK] = part[:, n * BLK : (n + 1) * BLK]
        grad_w_out[:, z * BLK : (z + 1) * BLK] = part[:, 4 * BLK :]


def silu_parts(u):
    t = jnp.tanh(u)
    a = 1.0 + t
    ut = u * t
    return u + ut, a * ((1.0 + u) - ut)


def key_side(q, g, kv, dkv, dq, i, j, keep):
    half = keep * 0.5
    for h in range(2):
        qi, gi = q[rows(i), head(h)], g[rows(i), head(h)]
        kj, vj = kv[rows(j), head(h)], kv[rows(j), head(h, BLK)]
        silu, slope = silu_parts(nt(kj, qi))
        w = (silu * keep).astype(BF16)
        ds = (nt(vj, gi) * slope * half).astype(BF16)
        dkv[rows(j), head(h, BLK)] += nn(w, gi)
        dkv[rows(j), head(h)] += nn(ds, qi)
        if dq is not None:
            dq[rows(i), head(h)] += tn(ds, kj)


def query_side(q, g, kv, dq, i, j, keep):
    half = keep * 0.5
    for h in range(2):
        kj, vj = kv[rows(j), head(h)], kv[rows(j), head(h, BLK)]
        slope = silu_parts(nt(q[rows(i), head(h)], kj))[1]
        ds = (nt(g[rows(i), head(h)], vj) * slope * half).astype(BF16)
        dq[rows(i), head(h)] += nn(ds, kj)


def backward_local_body(info, *refs):
    q, g, kv, kv_prev = refs[0:4]
    dsig = refs[4:8]
    gp_q, dkv, dq = refs[8:11]
    ends = history_ends(info)
    base = info[8] * GRP
    prev = base - GRP
    dq[...] = jnp.zeros_like(dq)
    dkv[...] = jnp.zeros_like(dkv)

    def over_j(j, _):
        kpos = base + j * BLK
        last = jnp.minimum((end_of(kpos + BLK - 1, ends) - 1 - base) // BLK, NB - 1)

        def over_i(i, _):
            key_side(q, g, kv, dkv, dq, i, j, keep_cols(base + i * BLK, kpos, ends))
            return 0

        return lax.fori_loop(j, last + 1, over_i, 0)

    lax.fori_loop(0, NB, over_j, 0)

    def halo_i(i, _):
        qpos = base + i * BLK

        def halo_j(j, _):
            query_side(q, g, kv_prev, dq, i, j, keep_rows(qpos, prev + j * BLK, ends))
            return 0

        return lax.fori_loop(halo_first(i, qpos, prev, ends), NB, halo_j, 0)

    lax.fori_loop(0, NB, halo_i, 0)
    for k in range(NB):
        at = rows(lax.rem(info[9] + k, NB))
        gp_q[at, :] = (dq[at, :] * dsig[k][:, 2 * BLK : 3 * BLK].astype(F32)).astype(BF16)


def backward_later_body(info, *refs):
    q, g, kv, dkv_in, gp_g, gp_q = refs[0:6]
    dsig, gp = refs[6:10], refs[10:14]
    dkv = refs[14]
    ends = history_ends(info)
    base = info[8] * GRP
    later = base + GRP
    dkv[...] = dkv_in[...]

    def over_j(j, _):
        kpos = base + j * BLK
        end = end_of(kpos + BLK - 1, ends)
        count = jnp.where(end > later, jnp.minimum((end - 1 - later) // BLK, j) + 1, 0)

        def over_i(i, _):
            key_side(q, g, kv, dkv, None, i, j, keep_cols(later + i * BLK, kpos, ends))
            return 0

        return lax.fori_loop(0, count, over_i, 0)

    lax.fori_loop(0, NB, over_j, 0)
    for k in range(NB):
        at = rows(lax.rem(info[9] + k, NB))
        dk = 2.0 * dkv[at, 0:BLK]
        gp[k][:, :BLK] = gp_g[at, :]
        gp[k][:, BLK : 2 * BLK] = gp_q[at, :]
        gp[k][:, 2 * BLK : 3 * BLK] = (dkv[at, BLK:] * dsig[k][:, BLK : 2 * BLK].astype(F32)).astype(BF16)
        gp[k][:, 3 * BLK :] = (dk * dsig[k][:, 3 * BLK :].astype(F32)).astype(BF16)


def input_body(info, *refs):
    gp, (w, cot), outs = refs[0:4], refs[4:6], refs[6:10]
    for k in range(NB):
        total = cot[...].astype(F32) if k == 0 else None
        for n, part in enumerate((0, 2, 1, 3)):
            lanes = pl.ds(pl.multiple_of(part * D + info[9] * BLK, BLK), BLK)
            term = nt(gp[k][:, n * BLK : (n + 1) * BLK], w[:, lanes])
            total = term if total is None else total + term
        outs[k][...] = total.astype(outs[k].dtype)


def add_rows_body(own, got_1, got_2, got_3, out):
    total = own[...] + got_1[...].astype(F32) + got_2[...].astype(F32) + got_3[...].astype(F32)
    out[...] = total.astype(BF16)


def along(x, axis, d):
    return lax.ppermute(x, axis, [(i, (i + d) % 4) for i in range(4)])


def swap(x):
    return lax.ppermute(x, "c", [(0, 1), (1, 0)])


def gather_z(x):
    return [x, along(x, "z", -1), along(x, "z", 2), along(x, "z", 1)]


def exchange(parts, axis):
    return [parts[0]] + [along(parts[d], axis, d) for d in (1, 2, 3)]


def f32(shape):
    return jax.ShapeDtypeStruct(shape, F32)


def bf16(shape):
    return jax.ShapeDtypeStruct(shape, BF16)


def body(events, cotangent, hist, w_in, w_out):
    z = lax.axis_index("z")
    info = jnp.concatenate(
        [hist[0], jnp.stack([lax.axis_index("y"), z, lax.axis_index("c"), lax.axis_index("x")]).astype(jnp.int32)]
    )
    ev, cot = events[0], cotangent[0]
    near = along(ev, "z", -1), along(ev, "z", 1)
    evs = [ev, near[0], None, near[1]]
    kvs, qs, gs, dsigs, kv_prevs = [], [], [], [None] * 4, []
    for blocks in ((0,), (1, 3), (2,)):
        n = len(blocks)
        if blocks == (1, 3):
            ev_far, *near, _ = lax.optimization_barrier((ev, *near, kvs[0]))
            evs = [ev, near[0], along(ev_far, "z", 2), near[1]]
        kv, q, g, *dsig = call(
            project_body,
            (bf16((n * BLK, 2 * BLK)), bf16((n * BLK, BLK)), bf16((n * BLK, BLK))) + (bf16((BLK, 4 * BLK)),) * n,
            n + 1, 2 * n * BLK * D * D, 4 << 20,
        )(info, *[evs[b] for b in blocks], w_in)
        kvs.append(kv)
        qs.append(q)
        gs.append(g)
        for b, d in zip(blocks, dsig):
            dsigs[b] = d
        kv_prevs.append(along(kv, "y", 1))
    ggs = call(grad_gated_body, (bf16((BLK, 2 * BLK)),) * 4, 2, 1 << 29, 2 << 20)(info, cot, w_out)
    *ggs, _ = lax.optimization_barrier((*ggs, evs[2]))
    ggs = exchange(ggs, "z")
    q, kv, att = call(
        forward_local_body, (bf16((GRP, BLK)), bf16((GRP, 2 * BLK)), f32((GRP, BLK))), 6, 5 << 30, 4 << 20
    )(info, *qs, *kvs)
    q_next = along(q, "y", -1)
    att, kv_prev, gg, cot_z, gate, stats = call(
        forward_halo_body,
        (f32((GRP, BLK)), bf16((GRP, 2 * BLK))) + (bf16((GRP, BLK)),) * 3 + (f32((8, GRP)),),
        12, 5 << 30, 4 << 20,
    )(info, q, att, *kv_prevs, *ggs, *gs)
    gatt, gated, gp_g = call(
        norm_body, (bf16((GRP, BLK)),) * 3, 11, 1 << 30, 4 << 20, [pltpu.VMEM((GRP, DH), F32)]
    )(info, att, gg, gate, *gather_z(stats), *dsigs)
    g_next = along(gatt, "y", -1)
    gateds = gather_z(gated)
    gp_q, dkv = call(
        backward_local_body, (bf16((GRP, BLK)), f32((GRP, 2 * BLK))), 8, 1 << 20, 1 << 20,
        [pltpu.VMEM((GRP, BLK), F32)],
    )(info, q, gatt, kv, kv_prev, *dsigs)
    early = call(early_weights_body, f32((D, 2 * BLK)), 6, 1 << 20, 1 << 20)(info, *evs, gp_g, gp_q)
    q_next, g_next, early = lax.optimization_barrier((q_next, g_next, early))
    gp = call(
        backward_later_body, (bf16((BLK, 4 * BLK)),) * 4, 10, 5 << 30, 4 << 20, [pltpu.VMEM((GRP, 2 * BLK), F32)]
    )(info, q_next, g_next, kv, dkv, gp_g, gp_q, *dsigs)
    send, keep = call(
        late_weights_body,
        (bf16((4, 128, 5 * BLK)), f32((4, 128, 5 * BLK))), 14, 1 << 20, 1 << 20,
        [pltpu.VMEM((D, 3 * BLK), F32)],
    )(info, *evs, *gp, *gateds, cot_z, early)
    partial = call(
        input_body, (f32((BLK, D)),) + (bf16((BLK, D)),) * 3, 6, 1 << 20, 1 << 20
    )(info, *gp, w_in, cot)
    partial = exchange(partial, "z")
    keep, partial[0] = lax.optimization_barrier((keep, partial[0]))
    mine = call(
        add_core_body, bf16((4, 128, 5 * BLK)), 2, 1 << 20, 1 << 20, scalars=0
    )(keep, swap(send))
    sums = lax.all_to_all(mine, "x", 0, 0)
    total = call(add_x_body, bf16((128, 5 * BLK)), 1, 1 << 20, 1 << 20, scalars=0)(sums)
    _, own_rows = lax.optimization_barrier((total, partial[0]))
    grad_events = call(
        add_rows_body, bf16((BLK, D)), 4, 1 << 20, 4 << 20, scalars=0
    )(own_rows, *partial[1:])
    got = lax.all_to_all(total.reshape(16, 8, 5 * BLK), ("y", "z"), 0, 0)
    grad_w_in, grad_w_out = call(last_sum_body, (bf16((8, 4 * D)), bf16((8, D))), 1, 1 << 20, 1 << 20, scalars=0)(got)
    return grad_events[None], grad_w_in, grad_w_out


def solution(mesh):
    axes = ("x", "c", "y", "z")
    split = Mesh(mesh.devices.reshape(4, 2, 4, 4), axes)
    dp, seq = ("x", "c"), ("y", "z")
    return jax.shard_map(
        body,
        mesh=split,
        in_specs=(P(dp, seq, None), P(dp, seq, None), P(dp, None), P(), P()),
        out_specs=(P(dp, seq, None), P(axes, None), P(axes, None)),
        check_vma=False,
    )
```

```python
import jax
import jax.numpy as jnp
from jax import lax
from jax.experimental import pallas as pl
from jax.experimental.pallas import tpu as pltpu
from jax.sharding import Mesh
from jax.sharding import PartitionSpec as P

BLK = 256
NB = 4
DH = 128
GRP = NB * BLK
D = 1024
F32 = jnp.float32
BF16 = jnp.bfloat16
SCALE = 1.0 / 256.0
VMEM = pl.BlockSpec(memory_space=pltpu.VMEM)
SMEM = pl.BlockSpec(memory_space=pltpu.SMEM)


def call(body, outs, n_in, flops, nbytes, scratch=(), scalars=1):
    return pl.pallas_call(
        body,
        out_shape=outs,
        in_specs=[SMEM] * scalars + [VMEM] * n_in,
        out_specs=jax.tree.map(lambda _: VMEM, outs),
        scratch_shapes=scratch,
        compiler_params=pltpu.CompilerParams(vmem_limit_bytes=20 * 1024 * 1024),
        cost_estimate=pl.CostEstimate(flops=flops, bytes_accessed=nbytes, transcendentals=0),
    )


def nt(a, b):
    return lax.dot_general(a, b, (((1,), (1,)), ((), ())), preferred_element_type=F32)


def nn(a, b):
    return lax.dot_general(a, b, (((1,), (0,)), ((), ())), preferred_element_type=F32)


def tn(a, b):
    return lax.dot_general(a, b, (((0,), (0,)), ((), ())), preferred_element_type=F32)


def history_ends(info):
    ends, total = [], jnp.int32(0)
    for k in range(8):
        total = total + info[k]
        ends.append(total)
    return ends


def start_of(pos, ends):
    start = jnp.zeros_like(pos)
    for e in ends:
        start = jnp.where(pos >= e, e, start)
    return start


def end_of(pos, ends):
    end = ends[-1]
    for e in reversed(ends):
        end = jnp.where(e > pos, e, end)
    return end


def rows(i):
    return pl.ds(pl.multiple_of(i * BLK, BLK), BLK)


def head(h, base=0):
    return slice(base + h * DH, base + (h + 1) * DH)


def project_body(info, *refs):
    n = (len(refs) - 4) // 2
    ev, (w, kv, q, g), dsig = refs[:n], refs[n : n + 4], refs[n + 4 :]
    for b in range(n):
        x, at = ev[b][...], slice(b * BLK, (b + 1) * BLK)
        for p in range(4):
            lanes = pl.ds(pl.multiple_of(p * D + info[9] * BLK, BLK), BLK)
            proj = nn(x, w[:, lanes])
            sig = 0.5 + 0.5 * jnp.tanh(0.5 * proj)
            act = (proj * sig).astype(BF16)
            if p == 0:
                g[at, :] = act
            elif p == 1:
                kv[at, BLK:] = act
            elif p == 2:
                q[at, :] = (0.5 * act.astype(F32)).astype(BF16)
            else:
                kv[at, :BLK] = act
            dsig[b][:, p * BLK : (p + 1) * BLK] = (sig * (1.0 + proj * (1.0 - sig))).astype(BF16)


def grad_gated_body(info, cot, w, *outs):
    for d in range(NB):
        owner = lax.rem(info[9] + d, NB)
        outs[d][:, :BLK] = nt(cot[...], w[rows(owner), :]).astype(BF16)
        outs[d][:, BLK:] = cot[:, pl.ds(pl.multiple_of(owner * BLK, BLK), BLK)]


def keep_rows(qpos, kpos, ends):
    r = qpos + lax.broadcasted_iota(jnp.int32, (BLK, 1), 0)
    c = kpos + lax.broadcasted_iota(jnp.int32, (1, BLK), 1)
    return jnp.where((c >= start_of(r, ends)) & (c <= r), SCALE, 0.0)


def keep_cols(qpos, kpos, ends):
    r = qpos + lax.broadcasted_iota(jnp.int32, (1, BLK), 1)
    c = kpos + lax.broadcasted_iota(jnp.int32, (BLK, 1), 0)
    return jnp.where((c >= start_of(r, ends)) & (c <= r), SCALE, 0.0)


def attend(q, kv, att, i, j, keep):
    for h in range(2):
        u = nt(q[rows(i), head(h)], kv[rows(j), head(h)])
        w = (u * (1.0 + jnp.tanh(u)) * keep).astype(BF16)
        att[rows(i), head(h)] += nn(w, kv[rows(j), head(h, BLK)])


def block_of(parts, k):
    part, at = ((0, 0), (1, 0), (2, 0), (1, BLK))[k]
    return parts[part][at : at + BLK, :]


def forward_local_body(info, *refs):
    q_in, kv_in = refs[0:3], refs[3:6]
    q, kv, att = refs[6:]
    ends = history_ends(info)
    base = info[8] * GRP
    for k in range(NB):
        at = rows(lax.rem(info[9] + k, NB))
        q[at, :] = block_of(q_in, k)
        kv[at, :] = block_of(kv_in, k)
    att[...] = jnp.zeros_like(att)

    def over_i(i, _):
        qpos = base + i * BLK
        first = jnp.maximum(start_of(qpos, ends) - base, 0) // BLK

        def over_j(j, _):
            attend(q, kv, att, i, j, keep_rows(qpos, base + j * BLK, ends))
            return 0

        return lax.fori_loop(first, i + 1, over_j, 0)

    lax.fori_loop(0, NB, over_i, 0)


def halo_first(i, qpos, prev, ends):
    start = start_of(qpos, ends)
    return jnp.where(start >= prev + GRP, NB, jnp.maximum((start - prev) // BLK, i))


def forward_halo_body(info, *refs):
    q, att_in = refs[0:2]
    kv_in, gg_in, gate_in = refs[2:5], refs[5:9], refs[9:12]
    att, kv, gg, cot, gate, stats = refs[12:18]
    ends = history_ends(info)
    base = info[8] * GRP
    prev = base - GRP
    att[...] = att_in[...]
    for k in range(NB):
        at = rows(lax.rem(info[9] + k, NB))
        kv[at, :] = block_of(kv_in, k)
        gate[at, :] = block_of(gate_in, k)
        gg[at, :] = gg_in[(4 - k) % 4][:, :BLK]
        cot[at, :] = gg_in[(4 - k) % 4][:, BLK:]

    def over_i(i, _):
        qpos = base + i * BLK

        def over_j(j, _):
            attend(q, kv, att, i, j, keep_rows(qpos, prev + j * BLK, ends))
            return 0

        return lax.fori_loop(halo_first(i, qpos, prev, ends), NB, over_j, 0)

    lax.fori_loop(0, NB, over_i, 0)
    a = att[...]
    gn = gg[...].astype(F32) * gate[...].astype(F32)
    mean = jnp.sum(a, axis=1, keepdims=True) / BLK
    cent = a - mean
    m2 = jnp.sum(cent * cent, axis=1, keepdims=True)
    g1 = jnp.sum(gn, axis=1, keepdims=True)
    ga = jnp.sum(gn * cent, axis=1, keepdims=True)
    lane = lax.broadcasted_iota(jnp.int32, (GRP, DH), 1)
    packed = jnp.where(lane == 0, mean, jnp.where(lane == 1, m2, jnp.where(lane == 2, g1, ga)))
    stats[...] = packed.T[:8, :]


def norm_body(info, *refs):
    att, gg, gate = refs[0:3]
    stats, dsig = refs[3:7], refs[7:11]
    gatt, gated, gp, table = refs[11:15]
    parts = [s[...] for s in stats]
    mean = (parts[0][0:1] + parts[1][0:1] + parts[2][0:1] + parts[3][0:1]) * 0.25
    m2 = jnp.zeros_like(mean)
    g1 = jnp.zeros_like(mean)
    ga = jnp.zeros_like(mean)
    for p in parts:
        off = p[0:1] - mean
        m2 = m2 + p[1:2] + BLK * off * off
        g1 = g1 + p[2:3]
        ga = ga + p[3:4] + off * p[2:3]
    inv = lax.rsqrt(m2 / D + 1e-6)
    row = lax.broadcasted_iota(jnp.int32, (DH, GRP), 0)
    cols = jnp.where(row == 0, mean, jnp.where(row == 1, inv, jnp.where(row == 2, g1 / D, ga * inv / D)))
    table[...] = cols.T
    for k in range(NB):
        at = rows(lax.rem(info[9] + k, NB))
        t = table[at, :]
        mean_c, inv_c, g1_c, ga_c = (t[:, n : n + 1] for n in range(4))
        normed = (att[at, :] - mean_c) * inv_c
        g = gate[at, :].astype(F32)
        grad_gated = gg[at, :].astype(F32)
        gatt[at, :] = (inv_c * (grad_gated * g - g1_c - normed * ga_c)).astype(BF16)
        gated[at, :] = (normed * g).astype(BF16)
        gp[at, :] = (grad_gated * normed * dsig[k][:, 0:BLK].astype(F32)).astype(BF16)


def early_weights_body(info, *refs):
    ev, (gp_g, gp_q, acc) = refs[0:4], refs[4:7]
    for k in range(NB):
        at = rows(lax.rem(info[9] + k, NB))
        for lanes, gp in ((slice(0, BLK), gp_g), (slice(BLK, 2 * BLK), gp_q)):
            part = tn(ev[k][...], gp[at, :])
            acc[:, lanes] = part if k == 0 else acc[:, lanes] + part


def late_weights_body(info, *refs):
    ev, gp, gated = refs[0:4], refs[4:8], refs[8:12]
    cot, early, send, keep, acc = refs[12:17]
    for k in range(NB):
        part = tn(ev[k][...], gp[k][:, 2 * BLK :])
        acc[:, : 2 * BLK] = part if k == 0 else acc[:, : 2 * BLK] + part
        acc[rows(lax.rem(info[9] + k, NB)), 2 * BLK :] = tn(gated[k][...], cot[...])
    for x in range(4):
        for out, c, kind in ((send, 1 - info[10], BF16), (keep, info[10], F32)):
            at = pl.ds(pl.multiple_of((x * 2 + c) * 128, 128), 128)
            out[x, :, : 2 * BLK] = early[at, :].astype(kind)
            out[x, :, 2 * BLK :] = acc[at, :].astype(kind)


def add_core_body(keep, got, out):
    out[...] = (keep[...] + got[...].astype(F32)).astype(BF16)


def add_x_body(got, total):
    part = got[0].astype(F32) + got[1].astype(F32) + got[2].astype(F32) + got[3].astype(F32)
    total[...] = part.astype(BF16)


def last_sum_body(got, grad_w_in, grad_w_out):
    for z in range(4):
        part = got[z].astype(F32)
        for y in range(1, 4):
            part = part + got[y * 4 + z].astype(F32)
        part = part.astype(BF16)
        for n, to in enumerate((0, 2, 1, 3)):
            at = to * D + z * BLK
            grad_w_in[:, at : at + BLK] = part[:, n * BLK : (n + 1) * BLK]
        grad_w_out[:, z * BLK : (z + 1) * BLK] = part[:, 4 * BLK :]


def silu_parts(u):
    t = jnp.tanh(u)
    a = 1.0 + t
    ut = u * t
    return u + ut, a * ((1.0 + u) - ut)


def key_side(q, g, kv, dkv, dq, i, j, keep):
    half = keep * 0.5
    for h in range(2):
        qi, gi = q[rows(i), head(h)], g[rows(i), head(h)]
        kj, vj = kv[rows(j), head(h)], kv[rows(j), head(h, BLK)]
        silu, slope = silu_parts(nt(kj, qi))
        w = (silu * keep).astype(BF16)
        ds = (nt(vj, gi) * slope * half).astype(BF16)
        dkv[rows(j), head(h, BLK)] += nn(w, gi)
        dkv[rows(j), head(h)] += nn(ds, qi)
        if dq is not None:
            dq[rows(i), head(h)] += tn(ds, kj)


def query_side(q, g, kv, dq, i, j, keep):
    half = keep * 0.5
    for h in range(2):
        kj, vj = kv[rows(j), head(h)], kv[rows(j), head(h, BLK)]
        slope = silu_parts(nt(q[rows(i), head(h)], kj))[1]
        ds = (nt(g[rows(i), head(h)], vj) * slope * half).astype(BF16)
        dq[rows(i), head(h)] += nn(ds, kj)


def backward_local_body(info, *refs):
    q, g, kv, kv_prev = refs[0:4]
    dsig = refs[4:8]
    gp_q, dkv, dq = refs[8:11]
    ends = history_ends(info)
    base = info[8] * GRP
    prev = base - GRP
    dq[...] = jnp.zeros_like(dq)
    dkv[...] = jnp.zeros_like(dkv)

    def over_j(j, _):
        kpos = base + j * BLK
        last = jnp.minimum((end_of(kpos + BLK - 1, ends) - 1 - base) // BLK, NB - 1)

        def over_i(i, _):
            key_side(q, g, kv, dkv, dq, i, j, keep_cols(base + i * BLK, kpos, ends))
            return 0

        return lax.fori_loop(j, last + 1, over_i, 0)

    lax.fori_loop(0, NB, over_j, 0)

    def halo_i(i, _):
        qpos = base + i * BLK

        def halo_j(j, _):
            query_side(q, g, kv_prev, dq, i, j, keep_rows(qpos, prev + j * BLK, ends))
            return 0

        return lax.fori_loop(halo_first(i, qpos, prev, ends), NB, halo_j, 0)

    lax.fori_loop(0, NB, halo_i, 0)
    for k in range(NB):
        at = rows(lax.rem(info[9] + k, NB))
        gp_q[at, :] = (dq[at, :] * dsig[k][:, 2 * BLK : 3 * BLK].astype(F32)).astype(BF16)


def backward_later_body(info, *refs):
    q, g, kv, dkv_in, gp_g, gp_q = refs[0:6]
    dsig, gp = refs[6:10], refs[10:14]
    dkv = refs[14]
    ends = history_ends(info)
    base = info[8] * GRP
    later = base + GRP
    dkv[...] = dkv_in[...]

    def over_j(j, _):
        kpos = base + j * BLK
        end = end_of(kpos + BLK - 1, ends)
        count = jnp.where(end > later, jnp.minimum((end - 1 - later) // BLK, j) + 1, 0)

        def over_i(i, _):
            key_side(q, g, kv, dkv, None, i, j, keep_cols(later + i * BLK, kpos, ends))
            return 0

        return lax.fori_loop(0, count, over_i, 0)

    lax.fori_loop(0, NB, over_j, 0)
    for k in range(NB):
        at = rows(lax.rem(info[9] + k, NB))
        dk = 2.0 * dkv[at, 0:BLK]
        gp[k][:, :BLK] = gp_g[at, :]
        gp[k][:, BLK : 2 * BLK] = gp_q[at, :]
        gp[k][:, 2 * BLK : 3 * BLK] = (dkv[at, BLK:] * dsig[k][:, BLK : 2 * BLK].astype(F32)).astype(BF16)
        gp[k][:, 3 * BLK :] = (dk * dsig[k][:, 3 * BLK :].astype(F32)).astype(BF16)


def input_body(info, *refs):
    gp, (w, cot), outs = refs[0:4], refs[4:6], refs[6:10]
    for k in range(NB):
        total = cot[...].astype(F32) if k == 0 else None
        for n, part in enumerate((0, 2, 1, 3)):
            lanes = pl.ds(pl.multiple_of(part * D + info[9] * BLK, BLK), BLK)
            term = nt(gp[k][:, n * BLK : (n + 1) * BLK], w[:, lanes])
            total = term if total is None else total + term
        outs[k][...] = total.astype(outs[k].dtype)


def add_near_body(own, got_1, got_3, out):
    out[...] = own[...] + got_1[...].astype(F32) + got_3[...].astype(F32)


def add_far_body(near, got_2, out):
    out[...] = (near[...] + got_2[...].astype(F32)).astype(BF16)


def along(x, axis, d):
    return lax.ppermute(x, axis, [(i, (i + d) % 4) for i in range(4)])


def swap(x):
    return lax.ppermute(x, "c", [(0, 1), (1, 0)])


def gather_z(x):
    return [x, along(x, "z", -1), along(x, "z", 2), along(x, "z", 1)]


def exchange(parts, axis):
    return [parts[0]] + [along(parts[d], axis, d) for d in (1, 2, 3)]


def f32(shape):
    return jax.ShapeDtypeStruct(shape, F32)


def bf16(shape):
    return jax.ShapeDtypeStruct(shape, BF16)


def body(events, cotangent, hist, w_in, w_out):
    z = lax.axis_index("z")
    info = jnp.concatenate(
        [hist[0], jnp.stack([lax.axis_index("y"), z, lax.axis_index("c"), lax.axis_index("x")]).astype(jnp.int32)]
    )
    ev, cot = events[0], cotangent[0]
    near = along(ev, "z", -1), along(ev, "z", 1)
    evs = [ev, near[0], None, near[1]]
    kvs, qs, gs, dsigs, kv_prevs = [], [], [], [None] * 4, []
    for blocks in ((0,), (1, 3), (2,)):
        n = len(blocks)
        if blocks == (1, 3):
            ev_far, *near, _ = lax.optimization_barrier((ev, *near, kvs[0]))
            evs = [ev, near[0], along(ev_far, "z", 2), near[1]]
        kv, q, g, *dsig = call(
            project_body,
            (bf16((n * BLK, 2 * BLK)), bf16((n * BLK, BLK)), bf16((n * BLK, BLK))) + (bf16((BLK, 4 * BLK)),) * n,
            n + 1, 1 << 20, 1 << 20,
        )(info, *[evs[b] for b in blocks], w_in)
        kvs.append(kv)
        qs.append(q)
        gs.append(g)
        for b, d in zip(blocks, dsig):
            dsigs[b] = d
        kv_prevs.append(along(kv, "y", 1))
    ggs = call(grad_gated_body, (bf16((BLK, 2 * BLK)),) * 4, 2, 1 << 20, 1 << 20)(info, cot, w_out)
    *ggs, _ = lax.optimization_barrier((*ggs, evs[2]))
    ggs = exchange(ggs, "z")
    q, kv, att = call(
        forward_local_body, (bf16((GRP, BLK)), bf16((GRP, 2 * BLK)), f32((GRP, BLK))), 6, 5 << 30, 4 << 20
    )(info, *qs, *kvs)
    q_next = along(q, "y", -1)
    att, kv_prev, gg, cot_z, gate, stats = call(
        forward_halo_body,
        (f32((GRP, BLK)), bf16((GRP, 2 * BLK))) + (bf16((GRP, BLK)),) * 3 + (f32((8, GRP)),),
        12, 5 << 30, 4 << 20,
    )(info, q, att, *kv_prevs, *ggs, *gs)
    gatt, gated, gp_g = call(
        norm_body, (bf16((GRP, BLK)),) * 3, 11, 1 << 30, 4 << 20, [pltpu.VMEM((GRP, DH), F32)]
    )(info, att, gg, gate, *gather_z(stats), *dsigs)
    g_next = along(gatt, "y", -1)
    gateds = gather_z(gated)
    gp_q, dkv = call(
        backward_local_body, (bf16((GRP, BLK)), f32((GRP, 2 * BLK))), 8, 1 << 20, 1 << 20,
        [pltpu.VMEM((GRP, BLK), F32)],
    )(info, q, gatt, kv, kv_prev, *dsigs)
    early = call(early_weights_body, f32((D, 2 * BLK)), 6, 1 << 20, 1 << 20)(info, *evs, gp_g, gp_q)
    q_next, g_next, early = lax.optimization_barrier((q_next, g_next, early))
    gp = call(
        backward_later_body, (bf16((BLK, 4 * BLK)),) * 4, 10, 5 << 30, 4 << 20, [pltpu.VMEM((GRP, 2 * BLK), F32)]
    )(info, q_next, g_next, kv, dkv, gp_g, gp_q, *dsigs)
    *partial, = call(
        input_body, (f32((BLK, D)),) + (bf16((BLK, D)),) * 3, 6, 1 << 20, 1 << 20
    )(info, *gp, w_in, cot)
    early, partial[0] = lax.optimization_barrier((early, partial[0]))
    partial = exchange(partial, "z")
    send, keep = call(
        late_weights_body,
        (bf16((4, 128, 5 * BLK)), f32((4, 128, 5 * BLK))), 14, 1 << 20, 1 << 20,
        [pltpu.VMEM((D, 3 * BLK), F32)],
    )(info, *evs, *gp, *gateds, cot_z, early)
    mine = call(
        add_core_body, bf16((4, 128, 5 * BLK)), 2, 1 << 20, 1 << 20, scalars=0
    )(keep, swap(send))
    sums = lax.all_to_all(mine, "x", 0, 0)
    near_rows = call(
        add_near_body, f32((BLK, D)), 3, 40 << 30, 4 << 20, scalars=0
    )(partial[0], partial[1], partial[3])
    sums, near_rows = lax.optimization_barrier((sums, near_rows))
    total = call(add_x_body, bf16((128, 5 * BLK)), 1, 1 << 20, 1 << 20, scalars=0)(sums)
    _, near_rows = lax.optimization_barrier((total, near_rows))
    grad_events = call(add_far_body, bf16((BLK, D)), 2, 1 << 20, 4 << 20, scalars=0)(near_rows, partial[2])
    got = lax.all_to_all(total.reshape(16, 8, 5 * BLK), ("y", "z"), 0, 0)
    grad_w_in, grad_w_out = call(last_sum_body, (bf16((8, 4 * D)), bf16((8, D))), 1, 1 << 20, 1 << 20, scalars=0)(got)
    return grad_events[None], grad_w_in, grad_w_out


def solution(mesh):
    axes = ("x", "c", "y", "z")
    split = Mesh(mesh.devices.reshape(4, 2, 4, 4), axes)
    dp, seq = ("x", "c"), ("y", "z")
    return jax.shard_map(
        body,
        mesh=split,
        in_specs=(P(dp, seq, None), P(dp, seq, None), P(dp, None), P(), P()),
        out_specs=(P(dp, seq, None), P(axes, None), P(axes, None)),
        check_vma=False,
    )
```

```python
import jax
import jax.numpy as jnp
from jax import lax
from jax.experimental import pallas as pl
from jax.experimental.pallas import tpu as pltpu
from jax.sharding import Mesh
from jax.sharding import PartitionSpec as P

BLK = 256
NB = 4
DH = 128
GRP = NB * BLK
D = 1024
F32 = jnp.float32
BF16 = jnp.bfloat16
SCALE = 1.0 / 256.0
VMEM = pl.BlockSpec(memory_space=pltpu.VMEM)
SMEM = pl.BlockSpec(memory_space=pltpu.SMEM)


def call(body, outs, n_in, flops, nbytes, scratch=(), scalars=1):
    return pl.pallas_call(
        body,
        out_shape=outs,
        in_specs=[SMEM] * scalars + [VMEM] * n_in,
        out_specs=jax.tree.map(lambda _: VMEM, outs),
        scratch_shapes=scratch,
        compiler_params=pltpu.CompilerParams(vmem_limit_bytes=20 * 1024 * 1024),
        cost_estimate=pl.CostEstimate(flops=flops, bytes_accessed=nbytes, transcendentals=0),
    )


def nt(a, b):
    return lax.dot_general(a, b, (((1,), (1,)), ((), ())), preferred_element_type=F32)


def nn(a, b):
    return lax.dot_general(a, b, (((1,), (0,)), ((), ())), preferred_element_type=F32)


def tn(a, b):
    return lax.dot_general(a, b, (((0,), (0,)), ((), ())), preferred_element_type=F32)


def history_ends(info):
    ends, total = [], jnp.int32(0)
    for k in range(8):
        total = total + info[k]
        ends.append(total)
    return ends


def start_of(pos, ends):
    start = jnp.zeros_like(pos)
    for e in ends:
        start = jnp.where(pos >= e, e, start)
    return start


def end_of(pos, ends):
    end = ends[-1]
    for e in reversed(ends):
        end = jnp.where(e > pos, e, end)
    return end


def rows(i):
    return pl.ds(pl.multiple_of(i * BLK, BLK), BLK)


def head(h, base=0):
    return slice(base + h * DH, base + (h + 1) * DH)


def project_body(info, *refs):
    n = (len(refs) - 4) // 2
    ev, (w, kv, q, g), dsig = refs[:n], refs[n : n + 4], refs[n + 4 :]
    for b in range(n):
        x, at = ev[b][...], slice(b * BLK, (b + 1) * BLK)
        for p in range(4):
            lanes = pl.ds(pl.multiple_of(p * D + info[9] * BLK, BLK), BLK)
            proj = nn(x, w[:, lanes])
            sig = 0.5 + 0.5 * jnp.tanh(0.5 * proj)
            act = (proj * sig).astype(BF16)
            if p == 0:
                g[at, :] = act
            elif p == 1:
                kv[at, BLK:] = act
            elif p == 2:
                q[at, :] = (0.5 * act.astype(F32)).astype(BF16)
            else:
                kv[at, :BLK] = act
            dsig[b][:, p * BLK : (p + 1) * BLK] = (sig * (1.0 + proj * (1.0 - sig))).astype(BF16)


def grad_gated_body(info, cot, w, *outs):
    for d in range(NB):
        owner = lax.rem(info[9] + d, NB)
        outs[d][:, :BLK] = nt(cot[...], w[rows(owner), :]).astype(BF16)
        outs[d][:, BLK:] = cot[:, pl.ds(pl.multiple_of(owner * BLK, BLK), BLK)]


def keep_rows(qpos, kpos, ends):
    r = qpos + lax.broadcasted_iota(jnp.int32, (BLK, 1), 0)
    c = kpos + lax.broadcasted_iota(jnp.int32, (1, BLK), 1)
    return jnp.where((c >= start_of(r, ends)) & (c <= r), SCALE, 0.0)


def keep_cols(qpos, kpos, ends):
    r = qpos + lax.broadcasted_iota(jnp.int32, (1, BLK), 1)
    c = kpos + lax.broadcasted_iota(jnp.int32, (BLK, 1), 0)
    return jnp.where((c >= start_of(r, ends)) & (c <= r), SCALE, 0.0)


def attend(q, kv, att, i, j, keep):
    for h in range(2):
        u = nt(q[rows(i), head(h)], kv[rows(j), head(h)])
        w = (u * (1.0 + jnp.tanh(u)) * keep).astype(BF16)
        att[rows(i), head(h)] += nn(w, kv[rows(j), head(h, BLK)])


def block_of(parts, k):
    part, at = ((0, 0), (1, 0), (2, 0), (1, BLK))[k]
    return parts[part][at : at + BLK, :]


def forward_local_body(info, *refs):
    q_in, kv_in = refs[0:3], refs[3:6]
    q, kv, att = refs[6:]
    ends = history_ends(info)
    base = info[8] * GRP
    for k in range(NB):
        at = rows(lax.rem(info[9] + k, NB))
        q[at, :] = block_of(q_in, k)
        kv[at, :] = block_of(kv_in, k)
    att[...] = jnp.zeros_like(att)

    def over_i(i, _):
        qpos = base + i * BLK
        first = jnp.maximum(start_of(qpos, ends) - base, 0) // BLK

        def over_j(j, _):
            attend(q, kv, att, i, j, keep_rows(qpos, base + j * BLK, ends))
            return 0

        return lax.fori_loop(first, i + 1, over_j, 0)

    lax.fori_loop(0, NB, over_i, 0)


def halo_first(i, qpos, prev, ends):
    start = start_of(qpos, ends)
    return jnp.where(start >= prev + GRP, NB, jnp.maximum((start - prev) // BLK, i))


def forward_halo_body(info, *refs):
    q, att_in = refs[0:2]
    kv_in, gg_in, gate_in = refs[2:5], refs[5:9], refs[9:12]
    att, kv, gg, cot, gate, stats = refs[12:18]
    ends = history_ends(info)
    base = info[8] * GRP
    prev = base - GRP
    att[...] = att_in[...]
    for k in range(NB):
        at = rows(lax.rem(info[9] + k, NB))
        kv[at, :] = block_of(kv_in, k)
        gate[at, :] = block_of(gate_in, k)
        gg[at, :] = gg_in[(4 - k) % 4][:, :BLK]
        cot[at, :] = gg_in[(4 - k) % 4][:, BLK:]

    def over_i(i, _):
        qpos = base + i * BLK

        def over_j(j, _):
            attend(q, kv, att, i, j, keep_rows(qpos, prev + j * BLK, ends))
            return 0

        return lax.fori_loop(halo_first(i, qpos, prev, ends), NB, over_j, 0)

    lax.fori_loop(0, NB, over_i, 0)
    a = att[...]
    gn = gg[...].astype(F32) * gate[...].astype(F32)
    mean = jnp.sum(a, axis=1, keepdims=True) / BLK
    cent = a - mean
    m2 = jnp.sum(cent * cent, axis=1, keepdims=True)
    g1 = jnp.sum(gn, axis=1, keepdims=True)
    ga = jnp.sum(gn * cent, axis=1, keepdims=True)
    lane = lax.broadcasted_iota(jnp.int32, (GRP, DH), 1)
    packed = jnp.where(lane == 0, mean, jnp.where(lane == 1, m2, jnp.where(lane == 2, g1, ga)))
    stats[...] = packed.T[:8, :]


def norm_body(info, *refs):
    att, gg, gate = refs[0:3]
    stats, dsig = refs[3:7], refs[7:11]
    gatt, gated, gp, table = refs[11:15]
    parts = [s[...] for s in stats]
    mean = (parts[0][0:1] + parts[1][0:1] + parts[2][0:1] + parts[3][0:1]) * 0.25
    m2 = jnp.zeros_like(mean)
    g1 = jnp.zeros_like(mean)
    ga = jnp.zeros_like(mean)
    for p in parts:
        off = p[0:1] - mean
        m2 = m2 + p[1:2] + BLK * off * off
        g1 = g1 + p[2:3]
        ga = ga + p[3:4] + off * p[2:3]
    inv = lax.rsqrt(m2 / D + 1e-6)
    row = lax.broadcasted_iota(jnp.int32, (DH, GRP), 0)
    cols = jnp.where(row == 0, mean, jnp.where(row == 1, inv, jnp.where(row == 2, g1 / D, ga * inv / D)))
    table[...] = cols.T
    for k in range(NB):
        at = rows(lax.rem(info[9] + k, NB))
        t = table[at, :]
        mean_c, inv_c, g1_c, ga_c = (t[:, n : n + 1] for n in range(4))
        normed = (att[at, :] - mean_c) * inv_c
        g = gate[at, :].astype(F32)
        grad_gated = gg[at, :].astype(F32)
        gatt[at, :] = (inv_c * (grad_gated * g - g1_c - normed * ga_c)).astype(BF16)
        gated[at, :] = (normed * g).astype(BF16)
        gp[at, :] = (grad_gated * normed * dsig[k][:, 0:BLK].astype(F32)).astype(BF16)


def early_weights_body(info, *refs):
    ev, (gp_g, gp_q, acc) = refs[0:4], refs[4:7]
    for k in range(NB):
        at = rows(lax.rem(info[9] + k, NB))
        for lanes, gp in ((slice(0, BLK), gp_g), (slice(BLK, 2 * BLK), gp_q)):
            part = tn(ev[k][...], gp[at, :])
            acc[:, lanes] = part if k == 0 else acc[:, lanes] + part


def late_weights_body(info, *refs):
    ev, gp, gated = refs[0:4], refs[4:8], refs[8:12]
    cot, early, send, keep, acc = refs[12:17]
    for k in range(NB):
        part = tn(ev[k][...], gp[k][:, 2 * BLK :])
        acc[:, : 2 * BLK] = part if k == 0 else acc[:, : 2 * BLK] + part
        acc[rows(lax.rem(info[9] + k, NB)), 2 * BLK :] = tn(gated[k][...], cot[...])
    for x in range(4):
        for out, c, kind in ((send, 1 - info[10], BF16), (keep, info[10], F32)):
            at = pl.ds(pl.multiple_of((x * 2 + c) * 128, 128), 128)
            out[x, :, : 2 * BLK] = early[at, :].astype(kind)
            out[x, :, 2 * BLK :] = acc[at, :].astype(kind)


def add_core_body(keep, got, out):
    out[...] = (keep[...] + got[...].astype(F32)).astype(BF16)


def last_sum_body(got, grad_w_in, grad_w_out):
    for z in range(4):
        part = got[z].astype(F32)
        for xy in range(1, 16):
            part = part + got[xy * 4 + z].astype(F32)
        part = part.astype(BF16)
        for n, to in enumerate((0, 2, 1, 3)):
            at = to * D + z * BLK
            grad_w_in[:, at : at + BLK] = part[:, n * BLK : (n + 1) * BLK]
        grad_w_out[:, z * BLK : (z + 1) * BLK] = part[:, 4 * BLK :]


def silu_parts(u):
    t = jnp.tanh(u)
    a = 1.0 + t
    ut = u * t
    return u + ut, a * ((1.0 + u) - ut)


def key_side(q, g, kv, dkv, dq, i, j, keep):
    half = keep * 0.5
    for h in range(2):
        qi, gi = q[rows(i), head(h)], g[rows(i), head(h)]
        kj, vj = kv[rows(j), head(h)], kv[rows(j), head(h, BLK)]
        silu, slope = silu_parts(nt(kj, qi))
        w = (silu * keep).astype(BF16)
        ds = (nt(vj, gi) * slope * half).astype(BF16)
        dkv[rows(j), head(h, BLK)] += nn(w, gi)
        dkv[rows(j), head(h)] += nn(ds, qi)
        if dq is not None:
            dq[rows(i), head(h)] += tn(ds, kj)


def query_side(q, g, kv, dq, i, j, keep):
    half = keep * 0.5
    for h in range(2):
        kj, vj = kv[rows(j), head(h)], kv[rows(j), head(h, BLK)]
        slope = silu_parts(nt(q[rows(i), head(h)], kj))[1]
        ds = (nt(g[rows(i), head(h)], vj) * slope * half).astype(BF16)
        dq[rows(i), head(h)] += nn(ds, kj)


def backward_local_body(info, *refs):
    q, g, kv, kv_prev = refs[0:4]
    dsig = refs[4:8]
    gp_q, dkv, dq = refs[8:11]
    ends = history_ends(info)
    base = info[8] * GRP
    prev = base - GRP
    dq[...] = jnp.zeros_like(dq)
    dkv[...] = jnp.zeros_like(dkv)

    def over_j(j, _):
        kpos = base + j * BLK
        last = jnp.minimum((end_of(kpos + BLK - 1, ends) - 1 - base) // BLK, NB - 1)

        def over_i(i, _):
            key_side(q, g, kv, dkv, dq, i, j, keep_cols(base + i * BLK, kpos, ends))
            return 0

        return lax.fori_loop(j, last + 1, over_i, 0)

    lax.fori_loop(0, NB, over_j, 0)

    def halo_i(i, _):
        qpos = base + i * BLK

        def halo_j(j, _):
            query_side(q, g, kv_prev, dq, i, j, keep_rows(qpos, prev + j * BLK, ends))
            return 0

        return lax.fori_loop(halo_first(i, qpos, prev, ends), NB, halo_j, 0)

    lax.fori_loop(0, NB, halo_i, 0)
    for k in range(NB):
        at = rows(lax.rem(info[9] + k, NB))
        gp_q[at, :] = (dq[at, :] * dsig[k][:, 2 * BLK : 3 * BLK].astype(F32)).astype(BF16)


def backward_later_body(info, *refs):
    q, g, kv, dkv_in, gp_g, gp_q = refs[0:6]
    dsig, gp = refs[6:10], refs[10:14]
    dkv = refs[14]
    ends = history_ends(info)
    base = info[8] * GRP
    later = base + GRP
    dkv[...] = dkv_in[...]

    def over_j(j, _):
        kpos = base + j * BLK
        end = end_of(kpos + BLK - 1, ends)
        count = jnp.where(end > later, jnp.minimum((end - 1 - later) // BLK, j) + 1, 0)

        def over_i(i, _):
            key_side(q, g, kv, dkv, None, i, j, keep_cols(later + i * BLK, kpos, ends))
            return 0

        return lax.fori_loop(0, count, over_i, 0)

    lax.fori_loop(0, NB, over_j, 0)
    for k in range(NB):
        at = rows(lax.rem(info[9] + k, NB))
        dk = 2.0 * dkv[at, 0:BLK]
        gp[k][:, :BLK] = gp_g[at, :]
        gp[k][:, BLK : 2 * BLK] = gp_q[at, :]
        gp[k][:, 2 * BLK : 3 * BLK] = (dkv[at, BLK:] * dsig[k][:, BLK : 2 * BLK].astype(F32)).astype(BF16)
        gp[k][:, 3 * BLK :] = (dk * dsig[k][:, 3 * BLK :].astype(F32)).astype(BF16)


def input_body(info, *refs):
    gp, (w, cot), outs = refs[0:4], refs[4:6], refs[6:10]
    for k in range(NB):
        total = cot[...].astype(F32) if k == 0 else None
        for n, part in enumerate((0, 2, 1, 3)):
            lanes = pl.ds(pl.multiple_of(part * D + info[9] * BLK, BLK), BLK)
            term = nt(gp[k][:, n * BLK : (n + 1) * BLK], w[:, lanes])
            total = term if total is None else total + term
        outs[k][...] = total.astype(outs[k].dtype)


def add_rows_body(own, got_1, got_2, got_3, out):
    total = own[...] + got_1[...].astype(F32) + got_2[...].astype(F32) + got_3[...].astype(F32)
    out[...] = total.astype(BF16)


def along(x, axis, d):
    return lax.ppermute(x, axis, [(i, (i + d) % 4) for i in range(4)])


def swap(x):
    return lax.ppermute(x, "c", [(0, 1), (1, 0)])


def gather_z(x):
    return [x, along(x, "z", -1), along(x, "z", 2), along(x, "z", 1)]


def exchange(parts, axis):
    return [parts[0]] + [along(parts[d], axis, d) for d in (1, 2, 3)]


def f32(shape):
    return jax.ShapeDtypeStruct(shape, F32)


def bf16(shape):
    return jax.ShapeDtypeStruct(shape, BF16)


def body(events, cotangent, hist, w_in, w_out):
    z = lax.axis_index("z")
    info = jnp.concatenate(
        [hist[0], jnp.stack([lax.axis_index("y"), z, lax.axis_index("c"), lax.axis_index("x")]).astype(jnp.int32)]
    )
    ev, cot = events[0], cotangent[0]
    near = along(ev, "z", -1), along(ev, "z", 1)
    evs = [ev, near[0], None, near[1]]
    kvs, qs, gs, dsigs, kv_prevs = [], [], [], [None] * 4, []
    ggs = call(grad_gated_body, (bf16((BLK, 2 * BLK)),) * 4, 2, 1 << 20, 1 << 20)(info, cot, w_out)
    for blocks in ((0,), (1, 3), (2,)):
        n = len(blocks)
        if blocks == (1, 3):
            ev_far, *near, _ = lax.optimization_barrier((ev, *near, kvs[0]))
            evs = [ev, near[0], along(ev_far, "z", 2), near[1]]
        if blocks == (2,):
            *ggs, far = lax.optimization_barrier((*ggs, evs[2]))
            ggs, evs[2] = exchange(ggs, "z"), far
        kv, q, g, *dsig = call(
            project_body,
            (bf16((n * BLK, 2 * BLK)), bf16((n * BLK, BLK)), bf16((n * BLK, BLK))) + (bf16((BLK, 4 * BLK)),) * n,
            n + 1, 1 << 20, 1 << 20,
        )(info, *[evs[b] for b in blocks], w_in)
        kvs.append(kv)
        qs.append(q)
        gs.append(g)
        for b, d in zip(blocks, dsig):
            dsigs[b] = d
        kv_prevs.append(along(kv, "y", 1))
    q, kv, att = call(
        forward_local_body, (bf16((GRP, BLK)), bf16((GRP, 2 * BLK)), f32((GRP, BLK))), 6, 5 << 30, 4 << 20
    )(info, *qs, *kvs)
    q_next = along(q, "y", -1)
    att, kv_prev, gg, cot_z, gate, stats = call(
        forward_halo_body,
        (f32((GRP, BLK)), bf16((GRP, 2 * BLK))) + (bf16((GRP, BLK)),) * 3 + (f32((8, GRP)),),
        12, 5 << 30, 4 << 20,
    )(info, q, att, *kv_prevs, *ggs, *gs)
    gatt, gated, gp_g = call(
        norm_body, (bf16((GRP, BLK)),) * 3, 11, 1 << 30, 4 << 20, [pltpu.VMEM((GRP, DH), F32)]
    )(info, att, gg, gate, *gather_z(stats), *dsigs)
    g_next = along(gatt, "y", -1)
    gateds = gather_z(gated)
    gp_q, dkv = call(
        backward_local_body, (bf16((GRP, BLK)), f32((GRP, 2 * BLK))), 8, 1 << 20, 1 << 20,
        [pltpu.VMEM((GRP, BLK), F32)],
    )(info, q, gatt, kv, kv_prev, *dsigs)
    early = call(early_weights_body, f32((D, 2 * BLK)), 6, 1 << 20, 1 << 20)(info, *evs, gp_g, gp_q)
    q_next, g_next, early = lax.optimization_barrier((q_next, g_next, early))
    gp = call(
        backward_later_body, (bf16((BLK, 4 * BLK)),) * 4, 10, 5 << 30, 4 << 20, [pltpu.VMEM((GRP, 2 * BLK), F32)]
    )(info, q_next, g_next, kv, dkv, gp_g, gp_q, *dsigs)
    *partial, = call(
        input_body, (f32((BLK, D)),) + (bf16((BLK, D)),) * 3, 6, 1 << 20, 1 << 20
    )(info, *gp, w_in, cot)
    early, partial[0] = lax.optimization_barrier((early, partial[0]))
    partial = exchange(partial, "z")
    send, keep = call(
        late_weights_body,
        (bf16((4, 128, 5 * BLK)), f32((4, 128, 5 * BLK))), 14, 1 << 20, 1 << 20,
        [pltpu.VMEM((D, 3 * BLK), F32)],
    )(info, *evs, *gp, *gateds, cot_z, early)
    mine = call(
        add_core_body, bf16((4, 128, 5 * BLK)), 2, 1 << 20, 1 << 20, scalars=0
    )(keep, swap(send))
    got = lax.all_to_all(mine.reshape(64, 8, 5 * BLK), ("x", "y", "z"), 0, 0)
    grad_events = call(add_rows_body, bf16((BLK, D)), 4, 40 << 30, 4 << 20, scalars=0)(*partial)
    grad_w_in, grad_w_out = call(last_sum_body, (bf16((8, 4 * D)), bf16((8, D))), 1, 1 << 20, 1 << 20, scalars=0)(got)
    return grad_events[None], grad_w_in, grad_w_out


def solution(mesh):
    axes = ("x", "c", "y", "z")
    split = Mesh(mesh.devices.reshape(4, 2, 4, 4), axes)
    dp, seq = ("x", "c"), ("y", "z")
    return jax.shard_map(
        body,
        mesh=split,
        in_specs=(P(dp, seq, None), P(dp, seq, None), P(dp, None), P(), P()),
        out_specs=(P(dp, seq, None), P(axes, None), P(axes, None)),
        check_vma=False,
    )
```

```python
import jax
import jax.numpy as jnp
from jax import lax
from jax.experimental import pallas as pl
from jax.experimental.pallas import tpu as pltpu
from jax.sharding import Mesh
from jax.sharding import PartitionSpec as P

BLK = 256
NB = 4
DH = 128
GRP = NB * BLK
D = 1024
F32 = jnp.float32
BF16 = jnp.bfloat16
SCALE = 1.0 / 256.0
VMEM = pl.BlockSpec(memory_space=pltpu.VMEM)
SMEM = pl.BlockSpec(memory_space=pltpu.SMEM)


def call(body, outs, n_in, flops, nbytes, scratch=(), scalars=1):
    return pl.pallas_call(
        body,
        out_shape=outs,
        in_specs=[SMEM] * scalars + [VMEM] * n_in,
        out_specs=jax.tree.map(lambda _: VMEM, outs),
        scratch_shapes=scratch,
        compiler_params=pltpu.CompilerParams(vmem_limit_bytes=20 * 1024 * 1024),
        cost_estimate=pl.CostEstimate(flops=flops, bytes_accessed=nbytes, transcendentals=0),
    )


def nt(a, b):
    return lax.dot_general(a, b, (((1,), (1,)), ((), ())), preferred_element_type=F32)


def nn(a, b):
    return lax.dot_general(a, b, (((1,), (0,)), ((), ())), preferred_element_type=F32)


def tn(a, b):
    return lax.dot_general(a, b, (((0,), (0,)), ((), ())), preferred_element_type=F32)


def history_ends(info):
    ends, total = [], jnp.int32(0)
    for k in range(8):
        total = total + info[k]
        ends.append(total)
    return ends


def start_of(pos, ends):
    start = jnp.zeros_like(pos)
    for e in ends:
        start = jnp.where(pos >= e, e, start)
    return start


def end_of(pos, ends):
    end = ends[-1]
    for e in reversed(ends):
        end = jnp.where(e > pos, e, end)
    return end


def rows(i):
    return pl.ds(pl.multiple_of(i * BLK, BLK), BLK)


def head(h, base=0):
    return slice(base + h * DH, base + (h + 1) * DH)


def project_body(info, *refs):
    n = (len(refs) - 4) // 2
    ev, (w, kv, q, g), dsig = refs[:n], refs[n : n + 4], refs[n + 4 :]
    for b in range(n):
        x, at = ev[b][...], slice(b * BLK, (b + 1) * BLK)
        for p in range(4):
            lanes = pl.ds(pl.multiple_of(p * D + info[9] * BLK, BLK), BLK)
            proj = nn(x, w[:, lanes])
            sig = 0.5 + 0.5 * jnp.tanh(0.5 * proj)
            act = (proj * sig).astype(BF16)
            if p == 0:
                g[at, :] = act
            elif p == 1:
                kv[at, BLK:] = act
            elif p == 2:
                q[at, :] = (0.5 * act.astype(F32)).astype(BF16)
            else:
                kv[at, :BLK] = act
            dsig[b][:, p * BLK : (p + 1) * BLK] = (sig * (1.0 + proj * (1.0 - sig))).astype(BF16)


def grad_gated_body(info, cot, w, *outs):
    for d in range(NB):
        owner = lax.rem(info[9] + d, NB)
        outs[d][:, :BLK] = nt(cot[...], w[rows(owner), :]).astype(BF16)
        outs[d][:, BLK:] = cot[:, pl.ds(pl.multiple_of(owner * BLK, BLK), BLK)]


def keep_rows(qpos, kpos, ends):
    r = qpos + lax.broadcasted_iota(jnp.int32, (BLK, 1), 0)
    c = kpos + lax.broadcasted_iota(jnp.int32, (1, BLK), 1)
    return jnp.where((c >= start_of(r, ends)) & (c <= r), SCALE, 0.0)


def keep_cols(qpos, kpos, ends):
    r = qpos + lax.broadcasted_iota(jnp.int32, (1, BLK), 1)
    c = kpos + lax.broadcasted_iota(jnp.int32, (BLK, 1), 0)
    return jnp.where((c >= start_of(r, ends)) & (c <= r), SCALE, 0.0)


def attend(q, kv, att, i, j, keep):
    for h in range(2):
        u = nt(q[rows(i), head(h)], kv[rows(j), head(h)])
        w = (u * (1.0 + jnp.tanh(u)) * keep).astype(BF16)
        att[rows(i), head(h)] += nn(w, kv[rows(j), head(h, BLK)])


def block_of(parts, k):
    part, at = ((0, 0), (1, 0), (2, 0), (1, BLK))[k]
    return parts[part][at : at + BLK, :]


def forward_local_body(info, *refs):
    q_in, kv_in = refs[0:3], refs[3:6]
    q, kv, att = refs[6:]
    ends = history_ends(info)
    base = info[8] * GRP
    for k in range(NB):
        at = rows(lax.rem(info[9] + k, NB))
        q[at, :] = block_of(q_in, k)
        kv[at, :] = block_of(kv_in, k)
    att[...] = jnp.zeros_like(att)

    def over_i(i, _):
        qpos = base + i * BLK
        first = jnp.maximum(start_of(qpos, ends) - base, 0) // BLK

        def over_j(j, _):
            attend(q, kv, att, i, j, keep_rows(qpos, base + j * BLK, ends))
            return 0

        return lax.fori_loop(first, i + 1, over_j, 0)

    lax.fori_loop(0, NB, over_i, 0)


def halo_first(i, qpos, prev, ends):
    start = start_of(qpos, ends)
    return jnp.where(start >= prev + GRP, NB, jnp.maximum((start - prev) // BLK, i))


def forward_halo_body(info, *refs):
    q, att_in = refs[0:2]
    gg_in, kv_in, gate_in = refs[2:6], refs[6:9], refs[9:12]
    att, kv, gg, cot, gate, stats = refs[12:18]
    ends = history_ends(info)
    base = info[8] * GRP
    prev = base - GRP
    att[...] = att_in[...]
    for k in range(NB):
        at = rows(lax.rem(info[9] + k, NB))
        kv[at, :] = block_of(kv_in, k)
        gate[at, :] = block_of(gate_in, k)
        gg[at, :] = gg_in[(4 - k) % 4][:, :BLK]
        cot[at, :] = gg_in[(4 - k) % 4][:, BLK:]

    def over_i(i, _):
        qpos = base + i * BLK

        def over_j(j, _):
            attend(q, kv, att, i, j, keep_rows(qpos, prev + j * BLK, ends))
            return 0

        return lax.fori_loop(halo_first(i, qpos, prev, ends), NB, over_j, 0)

    lax.fori_loop(0, NB, over_i, 0)
    a = att[...]
    gn = gg[...].astype(F32) * gate[...].astype(F32)
    mean = jnp.sum(a, axis=1, keepdims=True) / BLK
    cent = a - mean
    m2 = jnp.sum(cent * cent, axis=1, keepdims=True)
    g1 = jnp.sum(gn, axis=1, keepdims=True)
    ga = jnp.sum(gn * cent, axis=1, keepdims=True)
    lane = lax.broadcasted_iota(jnp.int32, (GRP, DH), 1)
    packed = jnp.where(lane == 0, mean, jnp.where(lane == 1, m2, jnp.where(lane == 2, g1, ga)))
    stats[...] = packed.T[:8, :]


def norm_body(info, *refs):
    att, gg, gate = refs[0:3]
    stats, dsig = refs[3:7], refs[7:11]
    gatt, gated, gp, table = refs[11:15]
    parts = [s[...] for s in stats]
    mean = (parts[0][0:1] + parts[1][0:1] + parts[2][0:1] + parts[3][0:1]) * 0.25
    m2 = jnp.zeros_like(mean)
    g1 = jnp.zeros_like(mean)
    ga = jnp.zeros_like(mean)
    for p in parts:
        off = p[0:1] - mean
        m2 = m2 + p[1:2] + BLK * off * off
        g1 = g1 + p[2:3]
        ga = ga + p[3:4] + off * p[2:3]
    inv = lax.rsqrt(m2 / D + 1e-6)
    row = lax.broadcasted_iota(jnp.int32, (DH, GRP), 0)
    cols = jnp.where(row == 0, mean, jnp.where(row == 1, inv, jnp.where(row == 2, g1 / D, ga * inv / D)))
    table[...] = cols.T
    for k in range(NB):
        at = rows(lax.rem(info[9] + k, NB))
        t = table[at, :]
        mean_c, inv_c, g1_c, ga_c = (t[:, n : n + 1] for n in range(4))
        normed = (att[at, :] - mean_c) * inv_c
        g = gate[at, :].astype(F32)
        grad_gated = gg[at, :].astype(F32)
        gatt[at, :] = (inv_c * (grad_gated * g - g1_c - normed * ga_c)).astype(BF16)
        gated[at, :] = (normed * g).astype(BF16)
        gp[at, :] = (grad_gated * normed * dsig[k][:, 0:BLK].astype(F32)).astype(BF16)


def pack(info, acc, send, keep):
    for x in range(4):
        for out, c, kind in ((send, 1 - info[10], BF16), (keep, info[10], F32)):
            at = pl.ds(pl.multiple_of((x * 2 + c) * 128, 128), 128)
            out[x, :, :] = acc[at, :].astype(kind)


def early_weights_body(info, *refs):
    ev, (gp_g, gp_q, send, keep, acc) = refs[0:4], refs[4:9]
    for k in range(NB):
        at = rows(lax.rem(info[9] + k, NB))
        for lanes, gp in ((slice(0, BLK), gp_g), (slice(BLK, 2 * BLK), gp_q)):
            part = tn(ev[k][...], gp[at, :])
            acc[:, lanes] = part if k == 0 else acc[:, lanes] + part
    pack(info, acc, send, keep)


def late_weights_body(info, *refs):
    ev, gp = refs[0:4], refs[4:8]
    send, keep, acc = refs[8:11]
    for k in range(NB):
        part = tn(ev[k][...], gp[k][:, 2 * BLK :])
        acc[...] = part if k == 0 else acc[...] + part
    pack(info, acc, send, keep)


def out_weights_body(info, *refs):
    gated, (cot, send, keep, acc) = refs[0:4], refs[4:8]
    for k in range(NB):
        acc[rows(lax.rem(info[9] + k, NB)), :] = tn(gated[k][...], cot[...])
    pack(info, acc, send, keep)


def add_core_body(keep_1, keep_2, keep_3, got_1, got_2, got_3, out):
    out[:, :, 0:512] = (keep_1[...] + got_1[...].astype(F32)).astype(BF16)
    out[:, :, 512:1024] = (keep_2[...] + got_2[...].astype(F32)).astype(BF16)
    out[:, :, 1024:] = (keep_3[...] + got_3[...].astype(F32)).astype(BF16)


def add_xy_body(got, total):
    part = got[0].astype(F32)
    for xy in range(1, 16):
        part = part + got[xy].astype(F32)
    total[...] = part.astype(BF16)


def last_body(got, grad_w_in, grad_w_out):
    for z in range(4):
        part = got[z]
        for n, to in enumerate((0, 2, 1, 3)):
            at = to * D + z * BLK
            grad_w_in[:, at : at + BLK] = part[:, n * BLK : (n + 1) * BLK]
        grad_w_out[:, z * BLK : (z + 1) * BLK] = part[:, 4 * BLK :]


def silu_parts(u):
    t = jnp.tanh(u)
    a = 1.0 + t
    ut = u * t
    return u + ut, a * ((1.0 + u) - ut)


def key_side(q, g, kv, dkv, dq, i, j, keep):
    half = keep * 0.5
    for h in range(2):
        qi, gi = q[rows(i), head(h)], g[rows(i), head(h)]
        kj, vj = kv[rows(j), head(h)], kv[rows(j), head(h, BLK)]
        silu, slope = silu_parts(nt(kj, qi))
        w = (silu * keep).astype(BF16)
        ds = (nt(vj, gi) * slope * half).astype(BF16)
        dkv[rows(j), head(h, BLK)] += nn(w, gi)
        dkv[rows(j), head(h)] += nn(ds, qi)
        if dq is not None:
            dq[rows(i), head(h)] += tn(ds, kj)


def query_side(q, g, kv, dq, i, j, keep):
    half = keep * 0.5
    for h in range(2):
        kj, vj = kv[rows(j), head(h)], kv[rows(j), head(h, BLK)]
        slope = silu_parts(nt(q[rows(i), head(h)], kj))[1]
        ds = (nt(g[rows(i), head(h)], vj) * slope * half).astype(BF16)
        dq[rows(i), head(h)] += nn(ds, kj)


def backward_local_body(info, *refs):
    q, g, kv, kv_prev = refs[0:4]
    dsig = refs[4:8]
    gp_q, dkv, dq = refs[8:11]
    ends = history_ends(info)
    base = info[8] * GRP
    prev = base - GRP
    dq[...] = jnp.zeros_like(dq)
    dkv[...] = jnp.zeros_like(dkv)

    def over_j(j, _):
        kpos = base + j * BLK
        last = jnp.minimum((end_of(kpos + BLK - 1, ends) - 1 - base) // BLK, NB - 1)

        def over_i(i, _):
            key_side(q, g, kv, dkv, dq, i, j, keep_cols(base + i * BLK, kpos, ends))
            return 0

        return lax.fori_loop(j, last + 1, over_i, 0)

    lax.fori_loop(0, NB, over_j, 0)

    def halo_i(i, _):
        qpos = base + i * BLK

        def halo_j(j, _):
            query_side(q, g, kv_prev, dq, i, j, keep_rows(qpos, prev + j * BLK, ends))
            return 0

        return lax.fori_loop(halo_first(i, qpos, prev, ends), NB, halo_j, 0)

    lax.fori_loop(0, NB, halo_i, 0)
    for k in range(NB):
        at = rows(lax.rem(info[9] + k, NB))
        gp_q[at, :] = (dq[at, :] * dsig[k][:, 2 * BLK : 3 * BLK].astype(F32)).astype(BF16)


def backward_later_body(info, *refs):
    q, g, kv, dkv_in, gp_g, gp_q = refs[0:6]
    dsig, gp = refs[6:10], refs[10:14]
    dkv = refs[14]
    ends = history_ends(info)
    base = info[8] * GRP
    later = base + GRP
    dkv[...] = dkv_in[...]

    def over_j(j, _):
        kpos = base + j * BLK
        end = end_of(kpos + BLK - 1, ends)
        count = jnp.where(end > later, jnp.minimum((end - 1 - later) // BLK, j) + 1, 0)

        def over_i(i, _):
            key_side(q, g, kv, dkv, None, i, j, keep_cols(later + i * BLK, kpos, ends))
            return 0

        return lax.fori_loop(0, count, over_i, 0)

    lax.fori_loop(0, NB, over_j, 0)
    for k in range(NB):
        at = rows(lax.rem(info[9] + k, NB))
        dk = 2.0 * dkv[at, 0:BLK]
        gp[k][:, :BLK] = gp_g[at, :]
        gp[k][:, BLK : 2 * BLK] = gp_q[at, :]
        gp[k][:, 2 * BLK : 3 * BLK] = (dkv[at, BLK:] * dsig[k][:, BLK : 2 * BLK].astype(F32)).astype(BF16)
        gp[k][:, 3 * BLK :] = (dk * dsig[k][:, 3 * BLK :].astype(F32)).astype(BF16)


def input_body(info, *refs):
    gp, (w, cot), outs = refs[0:4], refs[4:6], refs[6:10]
    for k in range(NB):
        total = cot[...].astype(F32) if k == 0 else None
        for n, part in enumerate((0, 2, 1, 3)):
            lanes = pl.ds(pl.multiple_of(part * D + info[9] * BLK, BLK), BLK)
            term = nt(gp[k][:, n * BLK : (n + 1) * BLK], w[:, lanes])
            total = term if total is None else total + term
        outs[k][...] = total.astype(outs[k].dtype)


def add_near_body(own, got_1, got_3, out):
    out[...] = own[...] + got_1[...].astype(F32) + got_3[...].astype(F32)


def add_far_body(near, got_2, out):
    out[...] = (near[...] + got_2[...].astype(F32)).astype(BF16)


def along(x, axis, d):
    return lax.ppermute(x, axis, [(i, (i + d) % 4) for i in range(4)])


def swap(x):
    return lax.ppermute(x, "c", [(0, 1), (1, 0)])


def gather_z(x):
    return [x, along(x, "z", -1), along(x, "z", 2), along(x, "z", 1)]


def exchange(parts, axis):
    return [parts[0]] + [along(parts[d], axis, d) for d in (1, 2, 3)]


def f32(shape):
    return jax.ShapeDtypeStruct(shape, F32)


def bf16(shape):
    return jax.ShapeDtypeStruct(shape, BF16)


def body(events, cotangent, hist, w_in, w_out):
    z = lax.axis_index("z")
    info = jnp.concatenate(
        [hist[0], jnp.stack([lax.axis_index("y"), z, lax.axis_index("c"), lax.axis_index("x")]).astype(jnp.int32)]
    )
    ev, cot = events[0], cotangent[0]
    near = along(ev, "z", -1), along(ev, "z", 1)
    evs = [ev, near[0], None, near[1]]
    kvs, qs, gs, dsigs, kv_prevs = [], [], [], [None] * 4, []
    for blocks in ((0,), (1, 3), (2,)):
        n = len(blocks)
        if blocks == (1, 3):
            ev_far, *near, _ = lax.optimization_barrier((ev, *near, kvs[0]))
            evs = [ev, near[0], along(ev_far, "z", 2), near[1]]
        kv, q, g, *dsig = call(
            project_body,
            (bf16((n * BLK, 2 * BLK)), bf16((n * BLK, BLK)), bf16((n * BLK, BLK))) + (bf16((BLK, 4 * BLK)),) * n,
            n + 1, 1 << 20, 1 << 20,
        )(info, *[evs[b] for b in blocks], w_in)
        kvs.append(kv)
        qs.append(q)
        gs.append(g)
        for b, d in zip(blocks, dsig):
            dsigs[b] = d
        kv_prevs.append(along(kv, "y", 1))
    ggs = call(grad_gated_body, (bf16((BLK, 2 * BLK)),) * 4, 2, 1 << 20, 1 << 20)(info, cot, w_out)
    *ggs, _ = lax.optimization_barrier((*ggs, evs[2]))
    ggs = exchange(ggs, "z")
    q, kv, att = call(
        forward_local_body, (bf16((GRP, BLK)), bf16((GRP, 2 * BLK)), f32((GRP, BLK))), 6, 5 << 30, 4 << 20
    )(info, *qs, *kvs)
    q_next = along(q, "y", -1)
    att, kv_prev, gg, cot_z, gate, stats = call(
        forward_halo_body,
        (f32((GRP, BLK)), bf16((GRP, 2 * BLK))) + (bf16((GRP, BLK)),) * 3 + (f32((8, GRP)),),
        12, 5 << 30, 4 << 20,
    )(info, q, att, *ggs, *kv_prevs, *gs)
    gatt, gated, gp_g = call(
        norm_body, (bf16((GRP, BLK)),) * 3, 11, 1 << 30, 4 << 20, [pltpu.VMEM((GRP, DH), F32)]
    )(info, att, gg, gate, *gather_z(stats), *dsigs)
    g_next = along(gatt, "y", -1)
    gateds = gather_z(gated)
    gp_q, dkv = call(
        backward_local_body, (bf16((GRP, BLK)), f32((GRP, 2 * BLK))), 8, 1 << 20, 1 << 20,
        [pltpu.VMEM((GRP, BLK), F32)],
    )(info, q, gatt, kv, kv_prev, *dsigs)
    def weights(kernel, cols, operands):
        send, keep = call(
            kernel, (bf16((4, 128, cols)), f32((4, 128, cols))), len(operands), 1 << 20, 1 << 20,
            [pltpu.VMEM((D, cols), F32)],
        )(info, *operands)
        return swap(send), keep

    got_1, keep_1 = weights(early_weights_body, 512, (*evs, gp_g, gp_q))
    q_next, g_next, keep_1 = lax.optimization_barrier((q_next, g_next, keep_1))
    gp = call(
        backward_later_body, (bf16((BLK, 4 * BLK)),) * 4, 10, 5 << 30, 4 << 20, [pltpu.VMEM((GRP, 2 * BLK), F32)]
    )(info, q_next, g_next, kv, dkv, gp_g, gp_q, *dsigs)
    got_2, keep_2 = weights(late_weights_body, 512, (*evs, *gp))
    *partial, = call(
        input_body, (f32((BLK, D)),) + (bf16((BLK, D)),) * 3, 6, 1 << 20, 1 << 20
    )(info, *gp, w_in, cot)
    cot_z, keep_2, partial[0] = lax.optimization_barrier((cot_z, keep_2, partial[0]))
    partial = exchange(partial, "z")
    got_3, keep_3 = weights(out_weights_body, 256, (*gateds, cot_z))
    mine = call(
        add_core_body, bf16((4, 128, 5 * BLK)), 6, 1 << 20, 1 << 20, scalars=0
    )(keep_1, keep_2, keep_3, got_1, got_2, got_3)
    sums = lax.all_to_all(mine.reshape(16, 32, 5 * BLK), ("x", "y"), 0, 0)
    near_rows = call(
        add_near_body, f32((BLK, D)), 3, 40 << 30, 4 << 20, scalars=0
    )(partial[0], partial[1], partial[3])
    sums, near_rows = lax.optimization_barrier((sums, near_rows))
    total = call(add_xy_body, bf16((32, 5 * BLK)), 1, 1 << 20, 1 << 20, scalars=0)(sums)
    _, near_rows = lax.optimization_barrier((total, near_rows))
    grad_events = call(add_far_body, bf16((BLK, D)), 2, 1 << 20, 4 << 20, scalars=0)(near_rows, partial[2])
    got = lax.all_to_all(total.reshape(4, 8, 5 * BLK), "z", 0, 0)
    grad_w_in, grad_w_out = call(
        last_body, (bf16((8, 4 * D)), bf16((8, D))), 1, 1 << 20, 1 << 20, scalars=0
    )(got)
    return grad_events[None], grad_w_in, grad_w_out


def solution(mesh):
    axes = ("x", "c", "y", "z")
    split = Mesh(mesh.devices.reshape(4, 2, 4, 4), axes)
    dp, seq = ("x", "c"), ("y", "z")
    return jax.shard_map(
        body,
        mesh=split,
        in_specs=(P(dp, seq, None), P(dp, seq, None), P(dp, None), P(), P()),
        out_specs=(P(dp, seq, None), P(axes, None), P(axes, None)),
        check_vma=False,
    )
```

```python
import jax
import jax.numpy as jnp
from jax import lax
from jax.experimental import pallas as pl
from jax.experimental.pallas import tpu as pltpu
from jax.sharding import Mesh
from jax.sharding import PartitionSpec as P

BLK = 256
NB = 4
DH = 128
GRP = NB * BLK
D = 1024
F32 = jnp.float32
BF16 = jnp.bfloat16
SCALE = 1.0 / 256.0
VMEM = pl.BlockSpec(memory_space=pltpu.VMEM)
SMEM = pl.BlockSpec(memory_space=pltpu.SMEM)


def call(body, outs, n_in, flops, nbytes, scratch=(), scalars=1):
    return pl.pallas_call(
        body,
        out_shape=outs,
        in_specs=[SMEM] * scalars + [VMEM] * n_in,
        out_specs=jax.tree.map(lambda _: VMEM, outs),
        scratch_shapes=scratch,
        compiler_params=pltpu.CompilerParams(vmem_limit_bytes=20 * 1024 * 1024),
        cost_estimate=pl.CostEstimate(flops=flops, bytes_accessed=nbytes, transcendentals=0),
    )


def nt(a, b):
    return lax.dot_general(a, b, (((1,), (1,)), ((), ())), preferred_element_type=F32)


def nn(a, b):
    return lax.dot_general(a, b, (((1,), (0,)), ((), ())), preferred_element_type=F32)


def tn(a, b):
    return lax.dot_general(a, b, (((0,), (0,)), ((), ())), preferred_element_type=F32)


def history_ends(info):
    ends, total = [], jnp.int32(0)
    for k in range(8):
        total = total + info[k]
        ends.append(total)
    return ends


def start_of(pos, ends):
    start = jnp.zeros_like(pos)
    for e in ends:
        start = jnp.where(pos >= e, e, start)
    return start


def end_of(pos, ends):
    end = ends[-1]
    for e in reversed(ends):
        end = jnp.where(e > pos, e, end)
    return end


def rows(i):
    return pl.ds(pl.multiple_of(i * BLK, BLK), BLK)


def head(h, base=0):
    return slice(base + h * DH, base + (h + 1) * DH)


def project_body(info, *refs):
    n = (len(refs) - 4) // 2
    ev, (w, kv, q, g), dsig = refs[:n], refs[n : n + 4], refs[n + 4 :]
    for b in range(n):
        x, at = ev[b][...], slice(b * BLK, (b + 1) * BLK)
        for p in range(4):
            lanes = pl.ds(pl.multiple_of(p * D + info[9] * BLK, BLK), BLK)
            proj = nn(x, w[:, lanes])
            sig = 0.5 + 0.5 * jnp.tanh(0.5 * proj)
            act = (proj * sig).astype(BF16)
            if p == 0:
                g[at, :] = act
            elif p == 1:
                kv[at, BLK:] = act
            elif p == 2:
                q[at, :] = (0.5 * act.astype(F32)).astype(BF16)
            else:
                kv[at, :BLK] = act
            dsig[b][:, p * BLK : (p + 1) * BLK] = (sig * (1.0 + proj * (1.0 - sig))).astype(BF16)


def grad_gated_body(info, cot, w, *outs):
    for d in range(NB):
        owner = lax.rem(info[9] + d, NB)
        outs[d][:, :BLK] = nt(cot[...], w[rows(owner), :]).astype(BF16)
        outs[d][:, BLK:] = cot[:, pl.ds(pl.multiple_of(owner * BLK, BLK), BLK)]


def keep_rows(qpos, kpos, ends):
    r = qpos + lax.broadcasted_iota(jnp.int32, (BLK, 1), 0)
    c = kpos + lax.broadcasted_iota(jnp.int32, (1, BLK), 1)
    return jnp.where((c >= start_of(r, ends)) & (c <= r), SCALE, 0.0)


def keep_cols(qpos, kpos, ends):
    r = qpos + lax.broadcasted_iota(jnp.int32, (1, BLK), 1)
    c = kpos + lax.broadcasted_iota(jnp.int32, (BLK, 1), 0)
    return jnp.where((c >= start_of(r, ends)) & (c <= r), SCALE, 0.0)


def attend(q, kv, att, i, j, keep):
    for h in range(2):
        u = nt(q[rows(i), head(h)], kv[rows(j), head(h)])
        w = (u * (1.0 + jnp.tanh(u)) * keep).astype(BF16)
        att[rows(i), head(h)] += nn(w, kv[rows(j), head(h, BLK)])


def block_of(parts, k):
    part, at = ((0, 0), (1, 0), (2, 0), (1, BLK))[k]
    return parts[part][at : at + BLK, :]


def forward_local_body(info, *refs):
    q_in, kv_in = refs[0:3], refs[3:6]
    q, kv, att = refs[6:]
    ends = history_ends(info)
    base = info[8] * GRP
    for k in range(NB):
        at = rows(lax.rem(info[9] + k, NB))
        q[at, :] = block_of(q_in, k)
        kv[at, :] = block_of(kv_in, k)
    att[...] = jnp.zeros_like(att)

    def over_i(i, _):
        qpos = base + i * BLK
        first = jnp.maximum(start_of(qpos, ends) - base, 0) // BLK

        def over_j(j, _):
            attend(q, kv, att, i, j, keep_rows(qpos, base + j * BLK, ends))
            return 0

        return lax.fori_loop(first, i + 1, over_j, 0)

    lax.fori_loop(0, NB, over_i, 0)


def halo_first(i, qpos, prev, ends):
    start = start_of(qpos, ends)
    return jnp.where(start >= prev + GRP, NB, jnp.maximum((start - prev) // BLK, i))


def forward_halo_body(info, *refs):
    q, att_in = refs[0:2]
    gg_in, kv_in, gate_in = refs[2:6], refs[6:9], refs[9:12]
    att, kv, gg, cot, gate, stats = refs[12:18]
    ends = history_ends(info)
    base = info[8] * GRP
    prev = base - GRP
    att[...] = att_in[...]
    for k in range(NB):
        at = rows(lax.rem(info[9] + k, NB))
        kv[at, :] = block_of(kv_in, k)
        gate[at, :] = block_of(gate_in, k)
        gg[at, :] = gg_in[(4 - k) % 4][:, :BLK]
        cot[at, :] = gg_in[(4 - k) % 4][:, BLK:]

    def over_i(i, _):
        qpos = base + i * BLK

        def over_j(j, _):
            attend(q, kv, att, i, j, keep_rows(qpos, prev + j * BLK, ends))
            return 0

        return lax.fori_loop(halo_first(i, qpos, prev, ends), NB, over_j, 0)

    lax.fori_loop(0, NB, over_i, 0)
    a = att[...]
    gn = gg[...].astype(F32) * gate[...].astype(F32)
    mean = jnp.sum(a, axis=1, keepdims=True) / BLK
    cent = a - mean
    m2 = jnp.sum(cent * cent, axis=1, keepdims=True)
    g1 = jnp.sum(gn, axis=1, keepdims=True)
    ga = jnp.sum(gn * cent, axis=1, keepdims=True)
    lane = lax.broadcasted_iota(jnp.int32, (GRP, DH), 1)
    packed = jnp.where(lane == 0, mean, jnp.where(lane == 1, m2, jnp.where(lane == 2, g1, ga)))
    stats[...] = packed.T[:8, :]


def norm_body(info, *refs):
    att, gg, gate = refs[0:3]
    stats, dsig = refs[3:7], refs[7:11]
    gatt, gated, gp, table = refs[11:15]
    parts = [s[...] for s in stats]
    mean = (parts[0][0:1] + parts[1][0:1] + parts[2][0:1] + parts[3][0:1]) * 0.25
    m2 = jnp.zeros_like(mean)
    g1 = jnp.zeros_like(mean)
    ga = jnp.zeros_like(mean)
    for p in parts:
        off = p[0:1] - mean
        m2 = m2 + p[1:2] + BLK * off * off
        g1 = g1 + p[2:3]
        ga = ga + p[3:4] + off * p[2:3]
    inv = lax.rsqrt(m2 / D + 1e-6)
    row = lax.broadcasted_iota(jnp.int32, (DH, GRP), 0)
    cols = jnp.where(row == 0, mean, jnp.where(row == 1, inv, jnp.where(row == 2, g1 / D, ga * inv / D)))
    table[...] = cols.T
    for k in range(NB):
        at = rows(lax.rem(info[9] + k, NB))
        t = table[at, :]
        mean_c, inv_c, g1_c, ga_c = (t[:, n : n + 1] for n in range(4))
        normed = (att[at, :] - mean_c) * inv_c
        g = gate[at, :].astype(F32)
        grad_gated = gg[at, :].astype(F32)
        gatt[at, :] = (inv_c * (grad_gated * g - g1_c - normed * ga_c)).astype(BF16)
        gated[at, :] = (normed * g).astype(BF16)
        gp[at, :] = (grad_gated * normed * dsig[k][:, 0:BLK].astype(F32)).astype(BF16)


def pack(info, acc, send, keep):
    for x in range(4):
        for out, c, kind in ((send, 1 - info[10], BF16), (keep, info[10], F32)):
            at = pl.ds(pl.multiple_of((x * 2 + c) * 128, 128), 128)
            out[x, :, :] = acc[at, :].astype(kind)


def early_weights_body(info, *refs):
    ev, (gp_g, gp_q, send, keep, acc) = refs[0:4], refs[4:9]
    for k in range(NB):
        at = rows(lax.rem(info[9] + k, NB))
        for lanes, gp in ((slice(0, BLK), gp_g), (slice(BLK, 2 * BLK), gp_q)):
            part = tn(ev[k][...], gp[at, :])
            acc[:, lanes] = part if k == 0 else acc[:, lanes] + part
    pack(info, acc, send, keep)


def late_weights_body(info, *refs):
    ev, gp = refs[0:4], refs[4:8]
    send, keep, acc = refs[8:11]
    for k in range(NB):
        part = tn(ev[k][...], gp[k][:, 2 * BLK :])
        acc[...] = part if k == 0 else acc[...] + part
    pack(info, acc, send, keep)


def out_weights_body(info, *refs):
    gated, (cot, send, keep, acc) = refs[0:4], refs[4:8]
    for k in range(NB):
        acc[rows(lax.rem(info[9] + k, NB)), :] = tn(gated[k][...], cot[...])
    pack(info, acc, send, keep)


def add_core_body(keep_1, keep_2, keep_3, got_1, got_2, got_3, out):
    out[:, :, 0:512] = (keep_1[...] + got_1[...].astype(F32)).astype(BF16)
    out[:, :, 512:1024] = (keep_2[...] + got_2[...].astype(F32)).astype(BF16)
    out[:, :, 1024:] = (keep_3[...] + got_3[...].astype(F32)).astype(BF16)


def add_xy_body(got, total):
    part = got[0].astype(F32)
    for xy in range(1, 16):
        part = part + got[xy].astype(F32)
    total[...] = part.astype(BF16)


def last_body(got, grad_w_in, grad_w_out):
    for z in range(4):
        part = got[z]
        for n, to in enumerate((0, 2, 1, 3)):
            at = to * D + z * BLK
            grad_w_in[:, at : at + BLK] = part[:, n * BLK : (n + 1) * BLK]
        grad_w_out[:, z * BLK : (z + 1) * BLK] = part[:, 4 * BLK :]


def silu_parts(u):
    t = jnp.tanh(u)
    a = 1.0 + t
    ut = u * t
    return u + ut, a * ((1.0 + u) - ut)


def key_side(q, g, kv, dkv, dq, i, j, keep):
    half = keep * 0.5
    for h in range(2):
        qi, gi = q[rows(i), head(h)], g[rows(i), head(h)]
        kj, vj = kv[rows(j), head(h)], kv[rows(j), head(h, BLK)]
        silu, slope = silu_parts(nt(kj, qi))
        w = (silu * keep).astype(BF16)
        ds = (nt(vj, gi) * slope * half).astype(BF16)
        dkv[rows(j), head(h, BLK)] += nn(w, gi)
        dkv[rows(j), head(h)] += nn(ds, qi)
        if dq is not None:
            dq[rows(i), head(h)] += tn(ds, kj)


def query_side(q, g, kv, dq, i, j, keep):
    half = keep * 0.5
    for h in range(2):
        kj, vj = kv[rows(j), head(h)], kv[rows(j), head(h, BLK)]
        slope = silu_parts(nt(q[rows(i), head(h)], kj))[1]
        ds = (nt(g[rows(i), head(h)], vj) * slope * half).astype(BF16)
        dq[rows(i), head(h)] += nn(ds, kj)


def backward_local_body(info, *refs):
    q, g, kv, kv_prev = refs[0:4]
    dsig = refs[4:8]
    gp_q, dkv, dq = refs[8:11]
    ends = history_ends(info)
    base = info[8] * GRP
    prev = base - GRP
    dq[...] = jnp.zeros_like(dq)
    dkv[...] = jnp.zeros_like(dkv)

    def over_j(j, _):
        kpos = base + j * BLK
        last = jnp.minimum((end_of(kpos + BLK - 1, ends) - 1 - base) // BLK, NB - 1)

        def over_i(i, _):
            key_side(q, g, kv, dkv, dq, i, j, keep_cols(base + i * BLK, kpos, ends))
            return 0

        return lax.fori_loop(j, last + 1, over_i, 0)

    lax.fori_loop(0, NB, over_j, 0)

    def halo_i(i, _):
        qpos = base + i * BLK

        def halo_j(j, _):
            query_side(q, g, kv_prev, dq, i, j, keep_rows(qpos, prev + j * BLK, ends))
            return 0

        return lax.fori_loop(halo_first(i, qpos, prev, ends), NB, halo_j, 0)

    lax.fori_loop(0, NB, halo_i, 0)
    for k in range(NB):
        at = rows(lax.rem(info[9] + k, NB))
        gp_q[at, :] = (dq[at, :] * dsig[k][:, 2 * BLK : 3 * BLK].astype(F32)).astype(BF16)


def backward_later_body(info, *refs):
    q, g, kv, dkv_in, gp_g, gp_q = refs[0:6]
    dsig, gp = refs[6:10], refs[10:14]
    dkv = refs[14]
    ends = history_ends(info)
    base = info[8] * GRP
    later = base + GRP
    dkv[...] = dkv_in[...]

    def over_j(j, _):
        kpos = base + j * BLK
        end = end_of(kpos + BLK - 1, ends)
        count = jnp.where(end > later, jnp.minimum((end - 1 - later) // BLK, j) + 1, 0)

        def over_i(i, _):
            key_side(q, g, kv, dkv, None, i, j, keep_cols(later + i * BLK, kpos, ends))
            return 0

        return lax.fori_loop(0, count, over_i, 0)

    lax.fori_loop(0, NB, over_j, 0)
    for k in range(NB):
        at = rows(lax.rem(info[9] + k, NB))
        dk = 2.0 * dkv[at, 0:BLK]
        gp[k][:, :BLK] = gp_g[at, :]
        gp[k][:, BLK : 2 * BLK] = gp_q[at, :]
        gp[k][:, 2 * BLK : 3 * BLK] = (dkv[at, BLK:] * dsig[k][:, BLK : 2 * BLK].astype(F32)).astype(BF16)
        gp[k][:, 3 * BLK :] = (dk * dsig[k][:, 3 * BLK :].astype(F32)).astype(BF16)


def input_body(info, *refs):
    gp, (w, cot), outs = refs[0:4], refs[4:6], refs[6:10]
    for k in range(NB):
        total = cot[...].astype(F32) if k == 0 else None
        for n, part in enumerate((0, 2, 1, 3)):
            lanes = pl.ds(pl.multiple_of(part * D + info[9] * BLK, BLK), BLK)
            term = nt(gp[k][:, n * BLK : (n + 1) * BLK], w[:, lanes])
            total = term if total is None else total + term
        outs[k][...] = total.astype(outs[k].dtype)


def add_near_body(own, got_1, got_3, out):
    out[...] = own[...] + got_1[...].astype(F32) + got_3[...].astype(F32)


def add_far_body(near, got_2, out):
    out[...] = (near[...] + got_2[...].astype(F32)).astype(BF16)


def along(x, axis, d):
    return lax.ppermute(x, axis, [(i, (i + d) % 4) for i in range(4)])


def swap(x):
    return lax.ppermute(x, "c", [(0, 1), (1, 0)])


def gather_z(x):
    return [x, along(x, "z", -1), along(x, "z", 2), along(x, "z", 1)]


def exchange(parts, axis):
    return [parts[0]] + [along(parts[d], axis, d) for d in (1, 2, 3)]


def f32(shape):
    return jax.ShapeDtypeStruct(shape, F32)


def bf16(shape):
    return jax.ShapeDtypeStruct(shape, BF16)


def body(events, cotangent, hist, w_in, w_out):
    z = lax.axis_index("z")
    info = jnp.concatenate(
        [hist[0], jnp.stack([lax.axis_index("y"), z, lax.axis_index("c"), lax.axis_index("x")]).astype(jnp.int32)]
    )
    ev, cot = events[0], cotangent[0]
    near = along(ev, "z", -1), along(ev, "z", 1)
    evs = [ev, near[0], None, near[1]]
    kvs, qs, gs, dsigs, kv_prevs = [], [], [], [None] * 4, []
    for blocks in ((0,), (1, 3), (2,)):
        n = len(blocks)
        if blocks == (1, 3):
            ev_far, *near, _ = lax.optimization_barrier((ev, *near, kvs[0]))
            evs = [ev, near[0], along(ev_far, "z", 2), near[1]]
        kv, q, g, *dsig = call(
            project_body,
            (bf16((n * BLK, 2 * BLK)), bf16((n * BLK, BLK)), bf16((n * BLK, BLK))) + (bf16((BLK, 4 * BLK)),) * n,
            n + 1, 1 << 20, 1 << 20,
        )(info, *[evs[b] for b in blocks], w_in)
        kvs.append(kv)
        qs.append(q)
        gs.append(g)
        for b, d in zip(blocks, dsig):
            dsigs[b] = d
        kv_prevs.append(along(kv, "y", 1))
    ggs = call(grad_gated_body, (bf16((BLK, 2 * BLK)),) * 4, 2, 1 << 20, 1 << 20)(info, cot, w_out)
    *ggs, _ = lax.optimization_barrier((*ggs, kvs[1]))
    ggs = exchange(ggs, "z")
    q, kv, att = call(
        forward_local_body, (bf16((GRP, BLK)), bf16((GRP, 2 * BLK)), f32((GRP, BLK))), 6, 5 << 30, 4 << 20
    )(info, *qs, *kvs)
    q_next = along(q, "y", -1)
    att, kv_prev, gg, cot_z, gate, stats = call(
        forward_halo_body,
        (f32((GRP, BLK)), bf16((GRP, 2 * BLK))) + (bf16((GRP, BLK)),) * 3 + (f32((8, GRP)),),
        12, 5 << 30, 4 << 20,
    )(info, q, att, *ggs, *kv_prevs, *gs)
    gatt, gated, gp_g = call(
        norm_body, (bf16((GRP, BLK)),) * 3, 11, 1 << 30, 4 << 20, [pltpu.VMEM((GRP, DH), F32)]
    )(info, att, gg, gate, *gather_z(stats), *dsigs)
    g_next = along(gatt, "y", -1)
    gateds = gather_z(gated)
    gp_q, dkv = call(
        backward_local_body, (bf16((GRP, BLK)), f32((GRP, 2 * BLK))), 8, 1 << 20, 1 << 20,
        [pltpu.VMEM((GRP, BLK), F32)],
    )(info, q, gatt, kv, kv_prev, *dsigs)
    def weights(kernel, cols, operands):
        send, keep = call(
            kernel, (bf16((4, 128, cols)), f32((4, 128, cols))), len(operands), 1 << 20, 1 << 20,
            [pltpu.VMEM((D, cols), F32)],
        )(info, *operands)
        return swap(send), keep

    got_1, keep_1 = weights(early_weights_body, 512, (*evs, gp_g, gp_q))
    q_next, g_next, keep_1 = lax.optimization_barrier((q_next, g_next, keep_1))
    gp = call(
        backward_later_body, (bf16((BLK, 4 * BLK)),) * 4, 10, 5 << 30, 4 << 20, [pltpu.VMEM((GRP, 2 * BLK), F32)]
    )(info, q_next, g_next, kv, dkv, gp_g, gp_q, *dsigs)
    got_2, keep_2 = weights(late_weights_body, 512, (*evs, *gp))
    *partial, = call(
        input_body, (f32((BLK, D)),) + (bf16((BLK, D)),) * 3, 6, 1 << 20, 1 << 20
    )(info, *gp, w_in, cot)
    cot_z, keep_2, partial[0] = lax.optimization_barrier((cot_z, keep_2, partial[0]))
    partial = exchange(partial, "z")
    got_3, keep_3 = weights(out_weights_body, 256, (*gateds, cot_z))
    mine = call(
        add_core_body, bf16((4, 128, 5 * BLK)), 6, 1 << 20, 1 << 20, scalars=0
    )(keep_1, keep_2, keep_3, got_1, got_2, got_3)
    sums = lax.all_to_all(mine.reshape(16, 32, 5 * BLK), ("x", "y"), 0, 0)
    near_rows = call(
        add_near_body, f32((BLK, D)), 3, 40 << 30, 4 << 20, scalars=0
    )(partial[0], partial[1], partial[3])
    sums, near_rows = lax.optimization_barrier((sums, near_rows))
    total = call(add_xy_body, bf16((32, 5 * BLK)), 1, 1 << 20, 1 << 20, scalars=0)(sums)
    _, near_rows = lax.optimization_barrier((total, near_rows))
    grad_events = call(add_far_body, bf16((BLK, D)), 2, 1 << 20, 4 << 20, scalars=0)(near_rows, partial[2])
    got = lax.all_to_all(total.reshape(4, 8, 5 * BLK), "z", 0, 0)
    grad_w_in, grad_w_out = call(
        last_body, (bf16((8, 4 * D)), bf16((8, D))), 1, 1 << 20, 1 << 20, scalars=0
    )(got)
    return grad_events[None], grad_w_in, grad_w_out


def solution(mesh):
    axes = ("x", "c", "y", "z")
    split = Mesh(mesh.devices.reshape(4, 2, 4, 4), axes)
    dp, seq = ("x", "c"), ("y", "z")
    return jax.shard_map(
        body,
        mesh=split,
        in_specs=(P(dp, seq, None), P(dp, seq, None), P(dp, None), P(), P()),
        out_specs=(P(dp, seq, None), P(axes, None), P(axes, None)),
        check_vma=False,
    )
```

```python
import jax
import jax.numpy as jnp
from jax import lax
from jax.experimental import pallas as pl
from jax.experimental.pallas import tpu as pltpu
from jax.sharding import Mesh
from jax.sharding import PartitionSpec as P

BLK = 256
NB = 4
DH = 128
GRP = NB * BLK
D = 1024
F32 = jnp.float32
BF16 = jnp.bfloat16
SCALE = 1.0 / 256.0
VMEM = pl.BlockSpec(memory_space=pltpu.VMEM)
SMEM = pl.BlockSpec(memory_space=pltpu.SMEM)


def call(body, outs, n_in, flops, nbytes, scratch=(), scalars=1):
    return pl.pallas_call(
        body,
        out_shape=outs,
        in_specs=[SMEM] * scalars + [VMEM] * n_in,
        out_specs=jax.tree.map(lambda _: VMEM, outs),
        scratch_shapes=scratch,
        compiler_params=pltpu.CompilerParams(vmem_limit_bytes=20 * 1024 * 1024),
        cost_estimate=pl.CostEstimate(flops=flops, bytes_accessed=nbytes, transcendentals=0),
    )


def nt(a, b):
    return lax.dot_general(a, b, (((1,), (1,)), ((), ())), preferred_element_type=F32)


def nn(a, b):
    return lax.dot_general(a, b, (((1,), (0,)), ((), ())), preferred_element_type=F32)


def tn(a, b):
    return lax.dot_general(a, b, (((0,), (0,)), ((), ())), preferred_element_type=F32)


def history_ends(info):
    ends, total = [], jnp.int32(0)
    for k in range(8):
        total = total + info[k]
        ends.append(total)
    return ends


def start_of(pos, ends):
    start = jnp.zeros_like(pos)
    for e in ends:
        start = jnp.where(pos >= e, e, start)
    return start


def end_of(pos, ends):
    end = ends[-1]
    for e in reversed(ends):
        end = jnp.where(e > pos, e, end)
    return end


def rows(i):
    return pl.ds(pl.multiple_of(i * BLK, BLK), BLK)


def head(h, base=0):
    return slice(base + h * DH, base + (h + 1) * DH)


def project_body(info, *refs):
    n = (len(refs) - 4) // 2
    ev, (w, kv, q, g), dsig = refs[:n], refs[n : n + 4], refs[n + 4 :]
    for b in range(n):
        x, at = ev[b][...], slice(b * BLK, (b + 1) * BLK)
        for p in range(4):
            lanes = pl.ds(pl.multiple_of(p * D + info[9] * BLK, BLK), BLK)
            proj = nn(x, w[:, lanes])
            sig = 0.5 + 0.5 * jnp.tanh(0.5 * proj)
            act = (proj * sig).astype(BF16)
            if p == 0:
                g[at, :] = act
            elif p == 1:
                kv[at, BLK:] = act
            elif p == 2:
                q[at, :] = (0.5 * act.astype(F32)).astype(BF16)
            else:
                kv[at, :BLK] = act
            dsig[b][:, p * BLK : (p + 1) * BLK] = (sig * (1.0 + proj * (1.0 - sig))).astype(BF16)


def grad_gated_body(info, cot, w, *outs):
    for d in range(NB):
        owner = lax.rem(info[9] + d, NB)
        outs[d][:, :BLK] = nt(cot[...], w[rows(owner), :]).astype(BF16)
        outs[d][:, BLK:] = cot[:, pl.ds(pl.multiple_of(owner * BLK, BLK), BLK)]


def keep_rows(qpos, kpos, ends):
    r = qpos + lax.broadcasted_iota(jnp.int32, (BLK, 1), 0)
    c = kpos + lax.broadcasted_iota(jnp.int32, (1, BLK), 1)
    return jnp.where((c >= start_of(r, ends)) & (c <= r), SCALE, 0.0)


def keep_cols(qpos, kpos, ends):
    r = qpos + lax.broadcasted_iota(jnp.int32, (1, BLK), 1)
    c = kpos + lax.broadcasted_iota(jnp.int32, (BLK, 1), 0)
    return jnp.where((c >= start_of(r, ends)) & (c <= r), SCALE, 0.0)


def attend(q, kv, att, i, j, keep):
    for h in range(2):
        u = nt(q[rows(i), head(h)], kv[rows(j), head(h)])
        w = (u * (1.0 + jnp.tanh(u)) * keep).astype(BF16)
        att[rows(i), head(h)] += nn(w, kv[rows(j), head(h, BLK)])


def block_of(parts, k):
    part, at = ((0, 0), (1, 0), (2, 0), (1, BLK))[k]
    return parts[part][at : at + BLK, :]


def forward_local_body(info, *refs):
    q_in, kv_in = refs[0:3], refs[3:6]
    q, kv, att = refs[6:]
    ends = history_ends(info)
    base = info[8] * GRP
    for k in range(NB):
        at = rows(lax.rem(info[9] + k, NB))
        q[at, :] = block_of(q_in, k)
        kv[at, :] = block_of(kv_in, k)
    att[...] = jnp.zeros_like(att)

    def over_i(i, _):
        qpos = base + i * BLK
        first = jnp.maximum(start_of(qpos, ends) - base, 0) // BLK

        def over_j(j, _):
            attend(q, kv, att, i, j, keep_rows(qpos, base + j * BLK, ends))
            return 0

        return lax.fori_loop(first, i + 1, over_j, 0)

    lax.fori_loop(0, NB, over_i, 0)


def halo_first(i, qpos, prev, ends):
    start = start_of(qpos, ends)
    return jnp.where(start >= prev + GRP, NB, jnp.maximum((start - prev) // BLK, i))


def forward_halo_body(info, *refs):
    q, att_in = refs[0:2]
    gg_in, kv_in, gate_in = refs[2:6], refs[6:9], refs[9:12]
    att, kv, gg, cot, gate, stats = refs[12:18]
    ends = history_ends(info)
    base = info[8] * GRP
    prev = base - GRP
    att[...] = att_in[...]
    for k in range(NB):
        at = rows(lax.rem(info[9] + k, NB))
        kv[at, :] = block_of(kv_in, k)
        gate[at, :] = block_of(gate_in, k)
        gg[at, :] = gg_in[(4 - k) % 4][:, :BLK]
        cot[at, :] = gg_in[(4 - k) % 4][:, BLK:]

    def over_i(i, _):
        qpos = base + i * BLK

        def over_j(j, _):
            attend(q, kv, att, i, j, keep_rows(qpos, prev + j * BLK, ends))
            return 0

        return lax.fori_loop(halo_first(i, qpos, prev, ends), NB, over_j, 0)

    lax.fori_loop(0, NB, over_i, 0)
    a = att[...]
    gn = gg[...].astype(F32) * gate[...].astype(F32)
    mean = jnp.sum(a, axis=1, keepdims=True) / BLK
    cent = a - mean
    m2 = jnp.sum(cent * cent, axis=1, keepdims=True)
    g1 = jnp.sum(gn, axis=1, keepdims=True)
    ga = jnp.sum(gn * cent, axis=1, keepdims=True)
    lane = lax.broadcasted_iota(jnp.int32, (GRP, DH), 1)
    packed = jnp.where(lane == 0, mean, jnp.where(lane == 1, m2, jnp.where(lane == 2, g1, ga)))
    stats[...] = packed.T[:8, :]


def norm_body(info, *refs):
    att, gg, gate = refs[0:3]
    stats, dsig = refs[3:7], refs[7:11]
    gatt, gated, gp, table = refs[11:15]
    parts = [s[...] for s in stats]
    mean = (parts[0][0:1] + parts[1][0:1] + parts[2][0:1] + parts[3][0:1]) * 0.25
    m2 = jnp.zeros_like(mean)
    g1 = jnp.zeros_like(mean)
    ga = jnp.zeros_like(mean)
    for p in parts:
        off = p[0:1] - mean
        m2 = m2 + p[1:2] + BLK * off * off
        g1 = g1 + p[2:3]
        ga = ga + p[3:4] + off * p[2:3]
    inv = lax.rsqrt(m2 / D + 1e-6)
    row = lax.broadcasted_iota(jnp.int32, (DH, GRP), 0)
    cols = jnp.where(row == 0, mean, jnp.where(row == 1, inv, jnp.where(row == 2, g1 / D, ga * inv / D)))
    table[...] = cols.T
    for k in range(NB):
        at = rows(lax.rem(info[9] + k, NB))
        t = table[at, :]
        mean_c, inv_c, g1_c, ga_c = (t[:, n : n + 1] for n in range(4))
        normed = (att[at, :] - mean_c) * inv_c
        g = gate[at, :].astype(F32)
        grad_gated = gg[at, :].astype(F32)
        gatt[at, :] = (inv_c * (grad_gated * g - g1_c - normed * ga_c)).astype(BF16)
        gated[at, :] = (normed * g).astype(BF16)
        gp[at, :] = (grad_gated * normed * dsig[k][:, 0:BLK].astype(F32)).astype(BF16)


def pack(info, acc, send, keep):
    for x in range(4):
        for out, c, kind in ((send, 1 - info[10], BF16), (keep, info[10], F32)):
            at = pl.ds(pl.multiple_of((x * 2 + c) * 128, 128), 128)
            out[x, :, :] = acc[at, :].astype(kind)


def early_weights_body(info, *refs):
    ev, (gp_g, gp_q, send, keep, acc) = refs[0:4], refs[4:9]
    for k in range(NB):
        at = rows(lax.rem(info[9] + k, NB))
        for lanes, gp in ((slice(0, BLK), gp_g), (slice(BLK, 2 * BLK), gp_q)):
            part = tn(ev[k][...], gp[at, :])
            acc[:, lanes] = part if k == 0 else acc[:, lanes] + part
    pack(info, acc, send, keep)


def late_weights_body(info, *refs):
    ev, gp = refs[0:4], refs[4:8]
    send, keep, acc = refs[8:11]
    for k in range(NB):
        part = tn(ev[k][...], gp[k][:, 2 * BLK :])
        acc[...] = part if k == 0 else acc[...] + part
    pack(info, acc, send, keep)


def out_weights_body(info, *refs):
    gated, (cot, send, keep, acc) = refs[0:4], refs[4:8]
    for k in range(NB):
        acc[rows(lax.rem(info[9] + k, NB)), :] = tn(gated[k][...], cot[...])
    pack(info, acc, send, keep)


def add_core_body(info, *refs):
    keep, got, away, own = refs[0:3], refs[3:6], refs[6:9], refs[9]
    for k, g, lanes in zip(keep, got, (slice(0, 512), slice(512, 1024), slice(1024, 1280))):
        for d in (1, 2, 3):
            at = lax.rem(info[11] + d, 4)
            away[d - 1][:, lanes] = (k[at] + g[at].astype(F32)).astype(BF16)
        own[:, lanes] = k[info[11]] + g[info[11]].astype(F32)


def add_x_body(own, got_1, got_2, got_3, total):
    part = own[...] + got_1[...].astype(F32) + got_2[...].astype(F32) + got_3[...].astype(F32)
    total[...] = part.astype(BF16)


def last_sum_body(got, grad_w_in, grad_w_out):
    for z in range(4):
        part = got[z].astype(F32)
        for y in range(1, 4):
            part = part + got[y * 4 + z].astype(F32)
        part = part.astype(BF16)
        for n, to in enumerate((0, 2, 1, 3)):
            at = to * D + z * BLK
            grad_w_in[:, at : at + BLK] = part[:, n * BLK : (n + 1) * BLK]
        grad_w_out[:, z * BLK : (z + 1) * BLK] = part[:, 4 * BLK :]


def silu_parts(u):
    t = jnp.tanh(u)
    a = 1.0 + t
    ut = u * t
    return u + ut, a * ((1.0 + u) - ut)


def key_side(q, g, kv, dkv, dq, i, j, keep):
    half = keep * 0.5
    for h in range(2):
        qi, gi = q[rows(i), head(h)], g[rows(i), head(h)]
        kj, vj = kv[rows(j), head(h)], kv[rows(j), head(h, BLK)]
        silu, slope = silu_parts(nt(kj, qi))
        w = (silu * keep).astype(BF16)
        ds = (nt(vj, gi) * slope * half).astype(BF16)
        dkv[rows(j), head(h, BLK)] += nn(w, gi)
        dkv[rows(j), head(h)] += nn(ds, qi)
        if dq is not None:
            dq[rows(i), head(h)] += tn(ds, kj)


def query_side(q, g, kv, dq, i, j, keep):
    half = keep * 0.5
    for h in range(2):
        kj, vj = kv[rows(j), head(h)], kv[rows(j), head(h, BLK)]
        slope = silu_parts(nt(q[rows(i), head(h)], kj))[1]
        ds = (nt(g[rows(i), head(h)], vj) * slope * half).astype(BF16)
        dq[rows(i), head(h)] += nn(ds, kj)


def backward_local_body(info, *refs):
    q, g, kv, kv_prev = refs[0:4]
    dsig = refs[4:8]
    gp_q, dkv, dq = refs[8:11]
    ends = history_ends(info)
    base = info[8] * GRP
    prev = base - GRP
    dq[...] = jnp.zeros_like(dq)
    dkv[...] = jnp.zeros_like(dkv)

    def over_j(j, _):
        kpos = base + j * BLK
        last = jnp.minimum((end_of(kpos + BLK - 1, ends) - 1 - base) // BLK, NB - 1)

        def over_i(i, _):
            key_side(q, g, kv, dkv, dq, i, j, keep_cols(base + i * BLK, kpos, ends))
            return 0

        return lax.fori_loop(j, last + 1, over_i, 0)

    lax.fori_loop(0, NB, over_j, 0)

    def halo_i(i, _):
        qpos = base + i * BLK

        def halo_j(j, _):
            query_side(q, g, kv_prev, dq, i, j, keep_rows(qpos, prev + j * BLK, ends))
            return 0

        return lax.fori_loop(halo_first(i, qpos, prev, ends), NB, halo_j, 0)

    lax.fori_loop(0, NB, halo_i, 0)
    for k in range(NB):
        at = rows(lax.rem(info[9] + k, NB))
        gp_q[at, :] = (dq[at, :] * dsig[k][:, 2 * BLK : 3 * BLK].astype(F32)).astype(BF16)


def backward_later_body(info, *refs):
    q, g, kv, dkv_in, gp_g, gp_q = refs[0:6]
    dsig, gp = refs[6:10], refs[10:14]
    dkv = refs[14]
    ends = history_ends(info)
    base = info[8] * GRP
    later = base + GRP
    dkv[...] = dkv_in[...]

    def over_j(j, _):
        kpos = base + j * BLK
        end = end_of(kpos + BLK - 1, ends)
        count = jnp.where(end > later, jnp.minimum((end - 1 - later) // BLK, j) + 1, 0)

        def over_i(i, _):
            key_side(q, g, kv, dkv, None, i, j, keep_cols(later + i * BLK, kpos, ends))
            return 0

        return lax.fori_loop(0, count, over_i, 0)

    lax.fori_loop(0, NB, over_j, 0)
    for k in range(NB):
        at = rows(lax.rem(info[9] + k, NB))
        dk = 2.0 * dkv[at, 0:BLK]
        gp[k][:, :BLK] = gp_g[at, :]
        gp[k][:, BLK : 2 * BLK] = gp_q[at, :]
        gp[k][:, 2 * BLK : 3 * BLK] = (dkv[at, BLK:] * dsig[k][:, BLK : 2 * BLK].astype(F32)).astype(BF16)
        gp[k][:, 3 * BLK :] = (dk * dsig[k][:, 3 * BLK :].astype(F32)).astype(BF16)


def input_body(info, *refs):
    gp, (w, cot), outs = refs[0:4], refs[4:6], refs[6:10]
    for k in range(NB):
        total = cot[...].astype(F32) if k == 0 else None
        for n, part in enumerate((0, 2, 1, 3)):
            lanes = pl.ds(pl.multiple_of(part * D + info[9] * BLK, BLK), BLK)
            term = nt(gp[k][:, n * BLK : (n + 1) * BLK], w[:, lanes])
            total = term if total is None else total + term
        outs[k][...] = total.astype(outs[k].dtype)


def add_near_body(own, got_1, got_3, out):
    out[...] = own[...] + got_1[...].astype(F32) + got_3[...].astype(F32)


def add_far_body(near, got_2, out):
    out[...] = (near[...] + got_2[...].astype(F32)).astype(BF16)


def along(x, axis, d):
    return lax.ppermute(x, axis, [(i, (i + d) % 4) for i in range(4)])


def swap(x):
    return lax.ppermute(x, "c", [(0, 1), (1, 0)])


def gather_z(x):
    return [x, along(x, "z", -1), along(x, "z", 2), along(x, "z", 1)]


def exchange(parts, axis):
    return [parts[0]] + [along(parts[d], axis, d) for d in (1, 2, 3)]


def f32(shape):
    return jax.ShapeDtypeStruct(shape, F32)


def bf16(shape):
    return jax.ShapeDtypeStruct(shape, BF16)


def body(events, cotangent, hist, w_in, w_out):
    z = lax.axis_index("z")
    info = jnp.concatenate(
        [hist[0], jnp.stack([lax.axis_index("y"), z, lax.axis_index("c"), lax.axis_index("x")]).astype(jnp.int32)]
    )
    ev, cot = events[0], cotangent[0]
    near = along(ev, "z", -1), along(ev, "z", 1)
    evs = [ev, near[0], None, near[1]]
    kvs, qs, gs, dsigs, kv_prevs = [], [], [], [None] * 4, []
    for blocks in ((0,), (1, 3), (2,)):
        n = len(blocks)
        if blocks == (1, 3):
            ev_far, *near, _ = lax.optimization_barrier((ev, *near, kvs[0]))
            evs = [ev, near[0], along(ev_far, "z", 2), near[1]]
        kv, q, g, *dsig = call(
            project_body,
            (bf16((n * BLK, 2 * BLK)), bf16((n * BLK, BLK)), bf16((n * BLK, BLK))) + (bf16((BLK, 4 * BLK)),) * n,
            n + 1, 1 << 20, 1 << 20,
        )(info, *[evs[b] for b in blocks], w_in)
        kvs.append(kv)
        qs.append(q)
        gs.append(g)
        for b, d in zip(blocks, dsig):
            dsigs[b] = d
        kv_prevs.append(along(kv, "y", 1))
    ggs = call(grad_gated_body, (bf16((BLK, 2 * BLK)),) * 4, 2, 1 << 20, 1 << 20)(info, cot, w_out)
    *ggs, _ = lax.optimization_barrier((*ggs, kvs[1]))
    ggs = exchange(ggs, "z")
    q, kv, att = call(
        forward_local_body, (bf16((GRP, BLK)), bf16((GRP, 2 * BLK)), f32((GRP, BLK))), 6, 5 << 30, 4 << 20
    )(info, *qs, *kvs)
    q_next = along(q, "y", -1)
    att, kv_prev, gg, cot_z, gate, stats = call(
        forward_halo_body,
        (f32((GRP, BLK)), bf16((GRP, 2 * BLK))) + (bf16((GRP, BLK)),) * 3 + (f32((8, GRP)),),
        12, 5 << 30, 4 << 20,
    )(info, q, att, *ggs, *kv_prevs, *gs)
    gatt, gated, gp_g = call(
        norm_body, (bf16((GRP, BLK)),) * 3, 11, 1 << 30, 4 << 20, [pltpu.VMEM((GRP, DH), F32)]
    )(info, att, gg, gate, *gather_z(stats), *dsigs)
    g_next = along(gatt, "y", -1)
    gateds = gather_z(gated)
    gp_q, dkv = call(
        backward_local_body, (bf16((GRP, BLK)), f32((GRP, 2 * BLK))), 8, 1 << 20, 1 << 20,
        [pltpu.VMEM((GRP, BLK), F32)],
    )(info, q, gatt, kv, kv_prev, *dsigs)
    def weights(kernel, cols, operands):
        send, keep = call(
            kernel, (bf16((4, 128, cols)), f32((4, 128, cols))), len(operands), 1 << 20, 1 << 20,
            [pltpu.VMEM((D, cols), F32)],
        )(info, *operands)
        return swap(send), keep

    got_1, keep_1 = weights(early_weights_body, 512, (*evs, gp_g, gp_q))
    q_next, g_next, keep_1 = lax.optimization_barrier((q_next, g_next, keep_1))
    gp = call(
        backward_later_body, (bf16((BLK, 4 * BLK)),) * 4, 10, 5 << 30, 4 << 20, [pltpu.VMEM((GRP, 2 * BLK), F32)]
    )(info, q_next, g_next, kv, dkv, gp_g, gp_q, *dsigs)
    *partial, = call(
        input_body, (f32((BLK, D)),) + (bf16((BLK, D)),) * 3, 6, 1 << 20, 1 << 20
    )(info, *gp, w_in, cot)
    *gp, partial[0] = lax.optimization_barrier((*gp, partial[0]))
    got_2, keep_2 = weights(late_weights_body, 512, (*evs, *gp))
    cot_z, keep_2 = lax.optimization_barrier((cot_z, keep_2))
    partial = exchange(partial, "z")
    got_3, keep_3 = weights(out_weights_body, 256, (*gateds, cot_z))
    *away, own = call(
        add_core_body, (bf16((128, 5 * BLK)),) * 3 + (f32((128, 5 * BLK)),), 6, 1 << 20, 1 << 20
    )(info, keep_1, keep_2, keep_3, got_1, got_2, got_3)
    sums = exchange([own] + away, "x")
    near_rows = call(
        add_near_body, f32((BLK, D)), 3, 40 << 30, 4 << 20, scalars=0
    )(partial[0], partial[1], partial[3])
    own, near_rows = lax.optimization_barrier((own, near_rows))
    total = call(add_x_body, bf16((128, 5 * BLK)), 4, 1 << 20, 1 << 20, scalars=0)(own, *sums[1:])
    _, near_rows = lax.optimization_barrier((total, near_rows))
    grad_events = call(add_far_body, bf16((BLK, D)), 2, 1 << 20, 4 << 20, scalars=0)(near_rows, partial[2])
    got = lax.all_to_all(total.reshape(16, 8, 5 * BLK), ("y", "z"), 0, 0)
    grad_w_in, grad_w_out = call(
        last_sum_body, (bf16((8, 4 * D)), bf16((8, D))), 1, 1 << 20, 1 << 20, scalars=0
    )(got)
    return grad_events[None], grad_w_in, grad_w_out


def solution(mesh):
    axes = ("x", "c", "y", "z")
    split = Mesh(mesh.devices.reshape(4, 2, 4, 4), axes)
    dp, seq = ("x", "c"), ("y", "z")
    return jax.shard_map(
        body,
        mesh=split,
        in_specs=(P(dp, seq, None), P(dp, seq, None), P(dp, None), P(), P()),
        out_specs=(P(dp, seq, None), P(axes, None), P(axes, None)),
        check_vma=False,
    )
```

```python
import jax
import jax.numpy as jnp
from jax import lax
from jax.experimental import pallas as pl
from jax.experimental.pallas import tpu as pltpu
from jax.sharding import Mesh
from jax.sharding import PartitionSpec as P

BLK = 256
NB = 4
DH = 128
GRP = NB * BLK
D = 1024
F32 = jnp.float32
BF16 = jnp.bfloat16
SCALE = 1.0 / 256.0
VMEM = pl.BlockSpec(memory_space=pltpu.VMEM)
SMEM = pl.BlockSpec(memory_space=pltpu.SMEM)


def call(body, outs, n_in, flops, nbytes, scratch=(), scalars=1):
    return pl.pallas_call(
        body,
        out_shape=outs,
        in_specs=[SMEM] * scalars + [VMEM] * n_in,
        out_specs=jax.tree.map(lambda _: VMEM, outs),
        scratch_shapes=scratch,
        compiler_params=pltpu.CompilerParams(vmem_limit_bytes=20 * 1024 * 1024),
        cost_estimate=pl.CostEstimate(flops=flops, bytes_accessed=nbytes, transcendentals=0),
    )


def nt(a, b):
    return lax.dot_general(a, b, (((1,), (1,)), ((), ())), preferred_element_type=F32)


def nn(a, b):
    return lax.dot_general(a, b, (((1,), (0,)), ((), ())), preferred_element_type=F32)


def tn(a, b):
    return lax.dot_general(a, b, (((0,), (0,)), ((), ())), preferred_element_type=F32)


def history_ends(info):
    ends, total = [], jnp.int32(0)
    for k in range(8):
        total = total + info[k]
        ends.append(total)
    return ends


def start_of(pos, ends):
    start = jnp.zeros_like(pos)
    for e in ends:
        start = jnp.where(pos >= e, e, start)
    return start


def end_of(pos, ends):
    end = ends[-1]
    for e in reversed(ends):
        end = jnp.where(e > pos, e, end)
    return end


def rows(i):
    return pl.ds(pl.multiple_of(i * BLK, BLK), BLK)


def head(h, base=0):
    return slice(base + h * DH, base + (h + 1) * DH)


def project_body(info, *refs):
    n = (len(refs) - 4) // 2
    ev, (w, kv, q, g), dsig = refs[:n], refs[n : n + 4], refs[n + 4 :]
    for b in range(n):
        x, at = ev[b][...], slice(b * BLK, (b + 1) * BLK)
        for p in range(4):
            lanes = pl.ds(pl.multiple_of(p * D + info[9] * BLK, BLK), BLK)
            proj = nn(x, w[:, lanes])
            sig = 0.5 + 0.5 * jnp.tanh(0.5 * proj)
            act = (proj * sig).astype(BF16)
            if p == 0:
                g[at, :] = act
            elif p == 1:
                kv[at, BLK:] = act
            elif p == 2:
                q[at, :] = (0.5 * act.astype(F32)).astype(BF16)
            else:
                kv[at, :BLK] = act
            dsig[b][:, p * BLK : (p + 1) * BLK] = (sig * (1.0 + proj * (1.0 - sig))).astype(BF16)


def grad_gated_body(info, cot, w, *outs):
    for d in range(NB):
        owner = lax.rem(info[9] + d, NB)
        outs[d][:, :BLK] = nt(cot[...], w[rows(owner), :]).astype(BF16)
        outs[d][:, BLK:] = cot[:, pl.ds(pl.multiple_of(owner * BLK, BLK), BLK)]


def keep_rows(qpos, kpos, ends):
    r = qpos + lax.broadcasted_iota(jnp.int32, (BLK, 1), 0)
    c = kpos + lax.broadcasted_iota(jnp.int32, (1, BLK), 1)
    return jnp.where((c >= start_of(r, ends)) & (c <= r), SCALE, 0.0)


def keep_cols(qpos, kpos, ends):
    r = qpos + lax.broadcasted_iota(jnp.int32, (1, BLK), 1)
    c = kpos + lax.broadcasted_iota(jnp.int32, (BLK, 1), 0)
    return jnp.where((c >= start_of(r, ends)) & (c <= r), SCALE, 0.0)


def attend(q, kv, att, i, j, keep):
    for h in range(2):
        u = nt(q[rows(i), head(h)], kv[rows(j), head(h)])
        w = (u * (1.0 + jnp.tanh(u)) * keep).astype(BF16)
        att[rows(i), head(h)] += nn(w, kv[rows(j), head(h, BLK)])


def block_of(parts, k):
    part, at = ((0, 0), (1, 0), (2, 0), (1, BLK))[k]
    return parts[part][at : at + BLK, :]


def forward_local_body(info, *refs):
    q_in, kv_in = refs[0:3], refs[3:6]
    q, kv, att = refs[6:]
    ends = history_ends(info)
    base = info[8] * GRP
    for k in range(NB):
        at = rows(lax.rem(info[9] + k, NB))
        q[at, :] = block_of(q_in, k)
        kv[at, :] = block_of(kv_in, k)
    att[...] = jnp.zeros_like(att)

    def over_i(i, _):
        qpos = base + i * BLK
        first = jnp.maximum(start_of(qpos, ends) - base, 0) // BLK

        def over_j(j, _):
            attend(q, kv, att, i, j, keep_rows(qpos, base + j * BLK, ends))
            return 0

        return lax.fori_loop(first, i + 1, over_j, 0)

    lax.fori_loop(0, NB, over_i, 0)


def halo_first(i, qpos, prev, ends):
    start = start_of(qpos, ends)
    return jnp.where(start >= prev + GRP, NB, jnp.maximum((start - prev) // BLK, i))


def forward_halo_body(info, *refs):
    q, att_in = refs[0:2]
    gg_in, kv_in, gate_in = refs[2:6], refs[6:9], refs[9:12]
    att, kv, gg, cot, gate, stats = refs[12:18]
    ends = history_ends(info)
    base = info[8] * GRP
    prev = base - GRP
    att[...] = att_in[...]
    for k in range(NB):
        at = rows(lax.rem(info[9] + k, NB))
        kv[at, :] = block_of(kv_in, k)
        gate[at, :] = block_of(gate_in, k)
        gg[at, :] = gg_in[(4 - k) % 4][:, :BLK]
        cot[at, :] = gg_in[(4 - k) % 4][:, BLK:]

    def over_i(i, _):
        qpos = base + i * BLK

        def over_j(j, _):
            attend(q, kv, att, i, j, keep_rows(qpos, prev + j * BLK, ends))
            return 0

        return lax.fori_loop(halo_first(i, qpos, prev, ends), NB, over_j, 0)

    lax.fori_loop(0, NB, over_i, 0)
    a = att[...]
    gn = gg[...].astype(F32) * gate[...].astype(F32)
    mean = jnp.sum(a, axis=1, keepdims=True) / BLK
    cent = a - mean
    m2 = jnp.sum(cent * cent, axis=1, keepdims=True)
    g1 = jnp.sum(gn, axis=1, keepdims=True)
    ga = jnp.sum(gn * cent, axis=1, keepdims=True)
    lane = lax.broadcasted_iota(jnp.int32, (GRP, DH), 1)
    packed = jnp.where(lane == 0, mean, jnp.where(lane == 1, m2, jnp.where(lane == 2, g1, ga)))
    stats[...] = packed.T[:8, :]


def norm_body(info, *refs):
    att, gg, gate = refs[0:3]
    stats, dsig = refs[3:7], refs[7:11]
    gatt, gated, gp, table = refs[11:15]
    parts = [s[...] for s in stats]
    mean = (parts[0][0:1] + parts[1][0:1] + parts[2][0:1] + parts[3][0:1]) * 0.25
    m2 = jnp.zeros_like(mean)
    g1 = jnp.zeros_like(mean)
    ga = jnp.zeros_like(mean)
    for p in parts:
        off = p[0:1] - mean
        m2 = m2 + p[1:2] + BLK * off * off
        g1 = g1 + p[2:3]
        ga = ga + p[3:4] + off * p[2:3]
    inv = lax.rsqrt(m2 / D + 1e-6)
    row = lax.broadcasted_iota(jnp.int32, (DH, GRP), 0)
    cols = jnp.where(row == 0, mean, jnp.where(row == 1, inv, jnp.where(row == 2, g1 / D, ga * inv / D)))
    table[...] = cols.T
    for k in range(NB):
        at = rows(lax.rem(info[9] + k, NB))
        t = table[at, :]
        mean_c, inv_c, g1_c, ga_c = (t[:, n : n + 1] for n in range(4))
        normed = (att[at, :] - mean_c) * inv_c
        g = gate[at, :].astype(F32)
        grad_gated = gg[at, :].astype(F32)
        gatt[at, :] = (inv_c * (grad_gated * g - g1_c - normed * ga_c)).astype(BF16)
        gated[at, :] = (normed * g).astype(BF16)
        gp[at, :] = (grad_gated * normed * dsig[k][:, 0:BLK].astype(F32)).astype(BF16)


def pack(info, acc, send, keep):
    for x in range(4):
        for out, c, kind in ((send, 1 - info[10], BF16), (keep, info[10], F32)):
            at = pl.ds(pl.multiple_of((x * 2 + c) * 128, 128), 128)
            out[x, :, :] = acc[at, :].astype(kind)


def early_weights_body(info, *refs):
    ev, (gp_g, gp_q, send, keep, acc) = refs[0:4], refs[4:9]
    for k in range(NB):
        at = rows(lax.rem(info[9] + k, NB))
        for lanes, gp in ((slice(0, BLK), gp_g), (slice(BLK, 2 * BLK), gp_q)):
            part = tn(ev[k][...], gp[at, :])
            acc[:, lanes] = part if k == 0 else acc[:, lanes] + part
    pack(info, acc, send, keep)


def late_weights_body(info, *refs):
    ev, gp = refs[0:4], refs[4:8]
    send, keep, acc = refs[8:11]
    for k in range(NB):
        part = tn(ev[k][...], gp[k][:, 2 * BLK :])
        acc[...] = part if k == 0 else acc[...] + part
    pack(info, acc, send, keep)


def out_weights_body(info, *refs):
    gated, (cot, send, keep, acc) = refs[0:4], refs[4:8]
    for k in range(NB):
        acc[rows(lax.rem(info[9] + k, NB)), :] = tn(gated[k][...], cot[...])
    pack(info, acc, send, keep)


def add_core_body(keep_1, keep_2, keep_3, got_1, got_2, got_3, out):
    out[:, :, 0:512] = (keep_1[...] + got_1[...].astype(F32)).astype(BF16)
    out[:, :, 512:1024] = (keep_2[...] + got_2[...].astype(F32)).astype(BF16)
    out[:, :, 1024:] = (keep_3[...] + got_3[...].astype(F32)).astype(BF16)


def add_xy_body(got, total):
    part = got[0].astype(F32)
    for xy in range(1, 16):
        part = part + got[xy].astype(F32)
    total[...] = part.astype(BF16)


def last_body(got, grad_w_in, grad_w_out):
    for z in range(4):
        part = got[z]
        for n, to in enumerate((0, 2, 1, 3)):
            at = to * D + z * BLK
            grad_w_in[:, at : at + BLK] = part[:, n * BLK : (n + 1) * BLK]
        grad_w_out[:, z * BLK : (z + 1) * BLK] = part[:, 4 * BLK :]


def silu_parts(u):
    t = jnp.tanh(u)
    a = 1.0 + t
    ut = u * t
    return u + ut, a * ((1.0 + u) - ut)


def key_side(q, g, kv, dkv, dq, i, j, keep):
    half = keep * 0.5
    for h in range(2):
        qi, gi = q[rows(i), head(h)], g[rows(i), head(h)]
        kj, vj = kv[rows(j), head(h)], kv[rows(j), head(h, BLK)]
        silu, slope = silu_parts(nt(kj, qi))
        w = (silu * keep).astype(BF16)
        ds = (nt(vj, gi) * slope * half).astype(BF16)
        dkv[rows(j), head(h, BLK)] += nn(w, gi)
        dkv[rows(j), head(h)] += nn(ds, qi)
        if dq is not None:
            dq[rows(i), head(h)] += tn(ds, kj)


def query_side(q, g, kv, dq, i, j, keep):
    half = keep * 0.5
    for h in range(2):
        kj, vj = kv[rows(j), head(h)], kv[rows(j), head(h, BLK)]
        slope = silu_parts(nt(q[rows(i), head(h)], kj))[1]
        ds = (nt(g[rows(i), head(h)], vj) * slope * half).astype(BF16)
        dq[rows(i), head(h)] += nn(ds, kj)


def backward_local_body(info, *refs):
    q, g, kv, kv_prev = refs[0:4]
    dsig = refs[4:8]
    gp_q, dkv, dq = refs[8:11]
    ends = history_ends(info)
    base = info[8] * GRP
    prev = base - GRP
    dq[...] = jnp.zeros_like(dq)
    dkv[...] = jnp.zeros_like(dkv)

    def over_j(j, _):
        kpos = base + j * BLK
        last = jnp.minimum((end_of(kpos + BLK - 1, ends) - 1 - base) // BLK, NB - 1)

        def over_i(i, _):
            key_side(q, g, kv, dkv, dq, i, j, keep_cols(base + i * BLK, kpos, ends))
            return 0

        return lax.fori_loop(j, last + 1, over_i, 0)

    lax.fori_loop(0, NB, over_j, 0)

    def halo_i(i, _):
        qpos = base + i * BLK

        def halo_j(j, _):
            query_side(q, g, kv_prev, dq, i, j, keep_rows(qpos, prev + j * BLK, ends))
            return 0

        return lax.fori_loop(halo_first(i, qpos, prev, ends), NB, halo_j, 0)

    lax.fori_loop(0, NB, halo_i, 0)
    for k in range(NB):
        at = rows(lax.rem(info[9] + k, NB))
        gp_q[at, :] = (dq[at, :] * dsig[k][:, 2 * BLK : 3 * BLK].astype(F32)).astype(BF16)


def backward_later_body(info, *refs):
    q, g, kv, dkv_in, gp_g, gp_q = refs[0:6]
    dsig, gp = refs[6:10], refs[10:14]
    dkv = refs[14]
    ends = history_ends(info)
    base = info[8] * GRP
    later = base + GRP
    dkv[...] = dkv_in[...]

    def over_j(j, _):
        kpos = base + j * BLK
        end = end_of(kpos + BLK - 1, ends)
        count = jnp.where(end > later, jnp.minimum((end - 1 - later) // BLK, j) + 1, 0)

        def over_i(i, _):
            key_side(q, g, kv, dkv, None, i, j, keep_cols(later + i * BLK, kpos, ends))
            return 0

        return lax.fori_loop(0, count, over_i, 0)

    lax.fori_loop(0, NB, over_j, 0)
    for k in range(NB):
        at = rows(lax.rem(info[9] + k, NB))
        dk = 2.0 * dkv[at, 0:BLK]
        gp[k][:, :BLK] = gp_g[at, :]
        gp[k][:, BLK : 2 * BLK] = gp_q[at, :]
        gp[k][:, 2 * BLK : 3 * BLK] = (dkv[at, BLK:] * dsig[k][:, BLK : 2 * BLK].astype(F32)).astype(BF16)
        gp[k][:, 3 * BLK :] = (dk * dsig[k][:, 3 * BLK :].astype(F32)).astype(BF16)


def input_body(info, *refs):
    gp, (w, cot), outs = refs[0:4], refs[4:6], refs[6:10]
    for k in range(NB):
        total = cot[...].astype(F32) if k == 0 else None
        for n, part in enumerate((0, 2, 1, 3)):
            lanes = pl.ds(pl.multiple_of(part * D + info[9] * BLK, BLK), BLK)
            term = nt(gp[k][:, n * BLK : (n + 1) * BLK], w[:, lanes])
            total = term if total is None else total + term
        outs[k][...] = total.astype(outs[k].dtype)


def add_rows_body(own, got_1, got_2, got_3, out):
    total = own[...] + got_1[...].astype(F32) + got_2[...].astype(F32) + got_3[...].astype(F32)
    out[...] = total.astype(BF16)


def along(x, axis, d):
    return lax.ppermute(x, axis, [(i, (i + d) % 4) for i in range(4)])


def swap(x):
    return lax.ppermute(x, "c", [(0, 1), (1, 0)])


def gather_z(x):
    return [x, along(x, "z", -1), along(x, "z", 2), along(x, "z", 1)]


def exchange(parts, axis):
    return [parts[0]] + [along(parts[d], axis, d) for d in (1, 2, 3)]


def f32(shape):
    return jax.ShapeDtypeStruct(shape, F32)


def bf16(shape):
    return jax.ShapeDtypeStruct(shape, BF16)


def body(events, cotangent, hist, w_in, w_out):
    z = lax.axis_index("z")
    info = jnp.concatenate(
        [hist[0], jnp.stack([lax.axis_index("y"), z, lax.axis_index("c"), lax.axis_index("x")]).astype(jnp.int32)]
    )
    ev, cot = events[0], cotangent[0]
    near = along(ev, "z", -1), along(ev, "z", 1)
    evs = [ev, near[0], None, near[1]]
    kvs, qs, gs, dsigs, kv_prevs = [], [], [], [None] * 4, []
    for blocks in ((0,), (1, 3), (2,)):
        n = len(blocks)
        if blocks == (1, 3):
            ev_far, *near, _ = lax.optimization_barrier((ev, *near, kvs[0]))
            evs = [ev, near[0], along(ev_far, "z", 2), near[1]]
        kv, q, g, *dsig = call(
            project_body,
            (bf16((n * BLK, 2 * BLK)), bf16((n * BLK, BLK)), bf16((n * BLK, BLK))) + (bf16((BLK, 4 * BLK)),) * n,
            n + 1, 1 << 20, 1 << 20,
        )(info, *[evs[b] for b in blocks], w_in)
        kvs.append(kv)
        qs.append(q)
        gs.append(g)
        for b, d in zip(blocks, dsig):
            dsigs[b] = d
        kv_prevs.append(along(kv, "y", 1))
    ggs = call(grad_gated_body, (bf16((BLK, 2 * BLK)),) * 4, 2, 1 << 20, 1 << 20)(info, cot, w_out)
    *ggs, _ = lax.optimization_barrier((*ggs, kvs[1]))
    ggs = exchange(ggs, "z")
    q, kv, att = call(
        forward_local_body, (bf16((GRP, BLK)), bf16((GRP, 2 * BLK)), f32((GRP, BLK))), 6, 5 << 30, 4 << 20
    )(info, *qs, *kvs)
    q_next = along(q, "y", -1)
    att, kv_prev, gg, cot_z, gate, stats = call(
        forward_halo_body,
        (f32((GRP, BLK)), bf16((GRP, 2 * BLK))) + (bf16((GRP, BLK)),) * 3 + (f32((8, GRP)),),
        12, 5 << 30, 4 << 20,
    )(info, q, att, *ggs, *kv_prevs, *gs)
    gatt, gated, gp_g = call(
        norm_body, (bf16((GRP, BLK)),) * 3, 11, 1 << 30, 4 << 20, [pltpu.VMEM((GRP, DH), F32)]
    )(info, att, gg, gate, *gather_z(stats), *dsigs)
    g_next = along(gatt, "y", -1)
    gateds = gather_z(gated)
    gp_q, dkv = call(
        backward_local_body, (bf16((GRP, BLK)), f32((GRP, 2 * BLK))), 8, 1 << 20, 1 << 20,
        [pltpu.VMEM((GRP, BLK), F32)],
    )(info, q, gatt, kv, kv_prev, *dsigs)
    def weights(kernel, cols, operands):
        send, keep = call(
            kernel, (bf16((4, 128, cols)), f32((4, 128, cols))), len(operands), 1 << 20, 1 << 20,
            [pltpu.VMEM((D, cols), F32)],
        )(info, *operands)
        return swap(send), keep

    got_1, keep_1 = weights(early_weights_body, 512, (*evs, gp_g, gp_q))
    q_next, g_next, keep_1 = lax.optimization_barrier((q_next, g_next, keep_1))
    gp = call(
        backward_later_body, (bf16((BLK, 4 * BLK)),) * 4, 10, 5 << 30, 4 << 20, [pltpu.VMEM((GRP, 2 * BLK), F32)]
    )(info, q_next, g_next, kv, dkv, gp_g, gp_q, *dsigs)
    got_2, keep_2 = weights(late_weights_body, 512, (*evs, *gp))
    *partial, = call(
        input_body, (f32((BLK, D)),) + (bf16((BLK, D)),) * 3, 6, 1 << 20, 1 << 20
    )(info, *gp, w_in, cot)
    cot_z, keep_2, partial[0] = lax.optimization_barrier((cot_z, keep_2, partial[0]))
    partial = exchange(partial, "z")
    got_3, keep_3 = weights(out_weights_body, 256, (*gateds, cot_z))
    mine = call(
        add_core_body, bf16((4, 128, 5 * BLK)), 6, 1 << 20, 1 << 20, scalars=0
    )(keep_1, keep_2, keep_3, got_1, got_2, got_3)
    sums = lax.all_to_all(mine.reshape(16, 32, 5 * BLK), ("x", "y"), 0, 0)
    total = call(add_xy_body, bf16((32, 5 * BLK)), 1, 1 << 20, 1 << 20, scalars=0)(sums)
    _, own_rows = lax.optimization_barrier((total, partial[0]))
    grad_events = call(
        add_rows_body, bf16((BLK, D)), 4, 1 << 20, 4 << 20, scalars=0
    )(own_rows, *partial[1:])
    got = lax.all_to_all(total.reshape(4, 8, 5 * BLK), "z", 0, 0)
    grad_w_in, grad_w_out = call(
        last_body, (bf16((8, 4 * D)), bf16((8, D))), 1, 1 << 20, 1 << 20, scalars=0
    )(got)
    return grad_events[None], grad_w_in, grad_w_out


def solution(mesh):
    axes = ("x", "c", "y", "z")
    split = Mesh(mesh.devices.reshape(4, 2, 4, 4), axes)
    dp, seq = ("x", "c"), ("y", "z")
    return jax.shard_map(
        body,
        mesh=split,
        in_specs=(P(dp, seq, None), P(dp, seq, None), P(dp, None), P(), P()),
        out_specs=(P(dp, seq, None), P(axes, None), P(axes, None)),
        check_vma=False,
    )
```

```python
import jax
import jax.numpy as jnp
from jax import lax
from jax.experimental import pallas as pl
from jax.experimental.pallas import tpu as pltpu
from jax.sharding import Mesh
from jax.sharding import PartitionSpec as P

BLK = 256
NB = 4
DH = 128
GRP = NB * BLK
D = 1024
F32 = jnp.float32
BF16 = jnp.bfloat16
SCALE = 1.0 / 256.0
VMEM = pl.BlockSpec(memory_space=pltpu.VMEM)
SMEM = pl.BlockSpec(memory_space=pltpu.SMEM)


def call(body, outs, n_in, flops, nbytes, scratch=(), scalars=1):
    return pl.pallas_call(
        body,
        out_shape=outs,
        in_specs=[SMEM] * scalars + [VMEM] * n_in,
        out_specs=jax.tree.map(lambda _: VMEM, outs),
        scratch_shapes=scratch,
        compiler_params=pltpu.CompilerParams(vmem_limit_bytes=20 * 1024 * 1024),
        cost_estimate=pl.CostEstimate(flops=flops, bytes_accessed=nbytes, transcendentals=0),
    )


def nt(a, b):
    return lax.dot_general(a, b, (((1,), (1,)), ((), ())), preferred_element_type=F32)


def nn(a, b):
    return lax.dot_general(a, b, (((1,), (0,)), ((), ())), preferred_element_type=F32)


def tn(a, b):
    return lax.dot_general(a, b, (((0,), (0,)), ((), ())), preferred_element_type=F32)


def history_ends(info):
    ends, total = [], jnp.int32(0)
    for k in range(8):
        total = total + info[k]
        ends.append(total)
    return ends


def start_of(pos, ends):
    start = jnp.zeros_like(pos)
    for e in ends:
        start = jnp.where(pos >= e, e, start)
    return start


def end_of(pos, ends):
    end = ends[-1]
    for e in reversed(ends):
        end = jnp.where(e > pos, e, end)
    return end


def rows(i):
    return pl.ds(pl.multiple_of(i * BLK, BLK), BLK)


def head(h, base=0):
    return slice(base + h * DH, base + (h + 1) * DH)


def project_body(info, *refs):
    n = (len(refs) - 4) // 2
    ev, (w, kv, q, g), dsig = refs[:n], refs[n : n + 4], refs[n + 4 :]
    for b in range(n):
        x, at = ev[b][...], slice(b * BLK, (b + 1) * BLK)
        for p in range(4):
            lanes = pl.ds(pl.multiple_of(p * D + info[9] * BLK, BLK), BLK)
            proj = nn(x, w[:, lanes])
            sig = 0.5 + 0.5 * jnp.tanh(0.5 * proj)
            act = (proj * sig).astype(BF16)
            if p == 0:
                g[at, :] = act
            elif p == 1:
                kv[at, BLK:] = act
            elif p == 2:
                q[at, :] = (0.5 * act.astype(F32)).astype(BF16)
            else:
                kv[at, :BLK] = act
            dsig[b][:, p * BLK : (p + 1) * BLK] = (sig * (1.0 + proj * (1.0 - sig))).astype(BF16)


def grad_gated_body(info, cot, w, *outs):
    for d in range(NB):
        owner = lax.rem(info[9] + d, NB)
        outs[d][:, :BLK] = nt(cot[...], w[rows(owner), :]).astype(BF16)
        outs[d][:, BLK:] = cot[:, pl.ds(pl.multiple_of(owner * BLK, BLK), BLK)]


def keep_rows(qpos, kpos, ends):
    r = qpos + lax.broadcasted_iota(jnp.int32, (BLK, 1), 0)
    c = kpos + lax.broadcasted_iota(jnp.int32, (1, BLK), 1)
    return jnp.where((c >= start_of(r, ends)) & (c <= r), SCALE, 0.0)


def keep_cols(qpos, kpos, ends):
    r = qpos + lax.broadcasted_iota(jnp.int32, (1, BLK), 1)
    c = kpos + lax.broadcasted_iota(jnp.int32, (BLK, 1), 0)
    return jnp.where((c >= start_of(r, ends)) & (c <= r), SCALE, 0.0)


def attend(q, kv, att, i, j, keep):
    two = range(2)
    qi = [q[rows(i), head(h)] for h in two]
    kj = [kv[rows(j), head(h)] for h in two]
    vj = [kv[rows(j), head(h, BLK)] for h in two]
    u = [nt(qi[h], kj[h]) for h in two]
    w = [(u[h] * (1.0 + jnp.tanh(u[h])) * keep).astype(BF16) for h in two]
    out = [nn(w[h], vj[h]) for h in two]
    for h in two:
        att[rows(i), head(h)] += out[h]


def block_of(parts, k):
    part, at = ((0, 0), (1, 0), (2, 0), (1, BLK))[k]
    return parts[part][at : at + BLK, :]


def forward_local_body(info, *refs):
    q_in, kv_in = refs[0:3], refs[3:6]
    q, kv, att = refs[6:]
    ends = history_ends(info)
    base = info[8] * GRP
    for k in range(NB):
        at = rows(lax.rem(info[9] + k, NB))
        q[at, :] = block_of(q_in, k)
        kv[at, :] = block_of(kv_in, k)
    att[...] = jnp.zeros_like(att)

    def over_i(i, _):
        qpos = base + i * BLK
        first = jnp.maximum(start_of(qpos, ends) - base, 0) // BLK

        def over_j(j, _):
            attend(q, kv, att, i, j, keep_rows(qpos, base + j * BLK, ends))
            return 0

        return lax.fori_loop(first, i + 1, over_j, 0)

    lax.fori_loop(0, NB, over_i, 0)


def halo_first(i, qpos, prev, ends):
    start = start_of(qpos, ends)
    return jnp.where(start >= prev + GRP, NB, jnp.maximum((start - prev) // BLK, i))


def forward_halo_body(info, *refs):
    q, att_in = refs[0:2]
    gg_in, kv_in, gate_in = refs[2:6], refs[6:9], refs[9:12]
    att, kv, gg, cot, gate, stats = refs[12:18]
    ends = history_ends(info)
    base = info[8] * GRP
    prev = base - GRP
    att[...] = att_in[...]
    for k in range(NB):
        at = rows(lax.rem(info[9] + k, NB))
        kv[at, :] = block_of(kv_in, k)
        gate[at, :] = block_of(gate_in, k)
        gg[at, :] = gg_in[(4 - k) % 4][:, :BLK]
        cot[at, :] = gg_in[(4 - k) % 4][:, BLK:]

    def over_i(i, _):
        qpos = base + i * BLK

        def over_j(j, _):
            attend(q, kv, att, i, j, keep_rows(qpos, prev + j * BLK, ends))
            return 0

        return lax.fori_loop(halo_first(i, qpos, prev, ends), NB, over_j, 0)

    lax.fori_loop(0, NB, over_i, 0)
    a = att[...]
    gn = gg[...].astype(F32) * gate[...].astype(F32)
    mean = jnp.sum(a, axis=1, keepdims=True) / BLK
    cent = a - mean
    m2 = jnp.sum(cent * cent, axis=1, keepdims=True)
    g1 = jnp.sum(gn, axis=1, keepdims=True)
    ga = jnp.sum(gn * cent, axis=1, keepdims=True)
    lane = lax.broadcasted_iota(jnp.int32, (GRP, DH), 1)
    packed = jnp.where(lane == 0, mean, jnp.where(lane == 1, m2, jnp.where(lane == 2, g1, ga)))
    stats[...] = packed.T[:8, :]


def norm_body(info, *refs):
    att, gg, gate = refs[0:3]
    stats, dsig = refs[3:7], refs[7:11]
    gatt, gated, gp, table = refs[11:15]
    parts = [s[...] for s in stats]
    mean = (parts[0][0:1] + parts[1][0:1] + parts[2][0:1] + parts[3][0:1]) * 0.25
    m2 = jnp.zeros_like(mean)
    g1 = jnp.zeros_like(mean)
    ga = jnp.zeros_like(mean)
    for p in parts:
        off = p[0:1] - mean
        m2 = m2 + p[1:2] + BLK * off * off
        g1 = g1 + p[2:3]
        ga = ga + p[3:4] + off * p[2:3]
    inv = lax.rsqrt(m2 / D + 1e-6)
    row = lax.broadcasted_iota(jnp.int32, (DH, GRP), 0)
    cols = jnp.where(row == 0, mean, jnp.where(row == 1, inv, jnp.where(row == 2, g1 / D, ga * inv / D)))
    table[...] = cols.T
    for k in range(NB):
        at = rows(lax.rem(info[9] + k, NB))
        t = table[at, :]
        mean_c, inv_c, g1_c, ga_c = (t[:, n : n + 1] for n in range(4))
        normed = (att[at, :] - mean_c) * inv_c
        g = gate[at, :].astype(F32)
        grad_gated = gg[at, :].astype(F32)
        gatt[at, :] = (inv_c * (grad_gated * g - g1_c - normed * ga_c)).astype(BF16)
        gated[at, :] = (normed * g).astype(BF16)
        gp[at, :] = (grad_gated * normed * dsig[k][:, 0:BLK].astype(F32)).astype(BF16)


def pack(info, acc, send, keep):
    for x in range(4):
        for out, c, kind in ((send, 1 - info[10], BF16), (keep, info[10], F32)):
            at = pl.ds(pl.multiple_of((x * 2 + c) * 128, 128), 128)
            out[x, :, :] = acc[at, :].astype(kind)


def early_weights_body(info, *refs):
    ev, (gp_g, gp_q, send, keep, acc) = refs[0:4], refs[4:9]
    for k in range(NB):
        at = rows(lax.rem(info[9] + k, NB))
        for lanes, gp in ((slice(0, BLK), gp_g), (slice(BLK, 2 * BLK), gp_q)):
            part = tn(ev[k][...], gp[at, :])
            acc[:, lanes] = part if k == 0 else acc[:, lanes] + part
    pack(info, acc, send, keep)


def late_weights_body(info, *refs):
    ev, gp = refs[0:4], refs[4:8]
    send, keep, acc = refs[8:11]
    for k in range(NB):
        part = tn(ev[k][...], gp[k][:, 2 * BLK :])
        acc[...] = part if k == 0 else acc[...] + part
    pack(info, acc, send, keep)


def out_weights_body(info, *refs):
    gated, (cot, send, keep, acc) = refs[0:4], refs[4:8]
    for k in range(NB):
        acc[rows(lax.rem(info[9] + k, NB)), :] = tn(gated[k][...], cot[...])
    pack(info, acc, send, keep)


def add_core_body(keep_1, keep_2, keep_3, got_1, got_2, got_3, out):
    out[:, :, 0:512] = (keep_1[...] + got_1[...].astype(F32)).astype(BF16)
    out[:, :, 512:1024] = (keep_2[...] + got_2[...].astype(F32)).astype(BF16)
    out[:, :, 1024:] = (keep_3[...] + got_3[...].astype(F32)).astype(BF16)


def add_xy_body(got, total):
    part = got[0].astype(F32)
    for xy in range(1, 16):
        part = part + got[xy].astype(F32)
    total[...] = part.astype(BF16)


def last_body(got, grad_w_in, grad_w_out):
    for z in range(4):
        part = got[z]
        for n, to in enumerate((0, 2, 1, 3)):
            at = to * D + z * BLK
            grad_w_in[:, at : at + BLK] = part[:, n * BLK : (n + 1) * BLK]
        grad_w_out[:, z * BLK : (z + 1) * BLK] = part[:, 4 * BLK :]


def silu_parts(u):
    t = jnp.tanh(u)
    a = 1.0 + t
    ut = u * t
    return u + ut, a * ((1.0 + u) - ut)


def key_side(q, g, kv, dkv, dq, i, j, keep):
    two = range(2)
    half = keep * 0.5
    qi = [q[rows(i), head(h)] for h in two]
    gi = [g[rows(i), head(h)] for h in two]
    kj = [kv[rows(j), head(h)] for h in two]
    vj = [kv[rows(j), head(h, BLK)] for h in two]
    u = [nt(kj[h], qi[h]) for h in two]
    dw = [nt(vj[h], gi[h]) for h in two]
    parts = [silu_parts(u[h]) for h in two]
    w = [(parts[h][0] * keep).astype(BF16) for h in two]
    ds = [(dw[h] * parts[h][1] * half).astype(BF16) for h in two]
    dv = [nn(w[h], gi[h]) for h in two]
    dk = [nn(ds[h], qi[h]) for h in two]
    dqi = [tn(ds[h], kj[h]) for h in two] if dq is not None else None
    for h in two:
        dkv[rows(j), head(h, BLK)] += dv[h]
        dkv[rows(j), head(h)] += dk[h]
        if dq is not None:
            dq[rows(i), head(h)] += dqi[h]


def query_side(q, g, kv, dq, i, j, keep):
    two = range(2)
    half = keep * 0.5
    qi = [q[rows(i), head(h)] for h in two]
    gi = [g[rows(i), head(h)] for h in two]
    kj = [kv[rows(j), head(h)] for h in two]
    vj = [kv[rows(j), head(h, BLK)] for h in two]
    slope = [silu_parts(nt(qi[h], kj[h]))[1] for h in two]
    dw = [nt(gi[h], vj[h]) for h in two]
    ds = [(dw[h] * slope[h] * half).astype(BF16) for h in two]
    dqi = [nn(ds[h], kj[h]) for h in two]
    for h in two:
        dq[rows(i), head(h)] += dqi[h]


def backward_local_body(info, *refs):
    q, g, kv, kv_prev = refs[0:4]
    dsig = refs[4:8]
    gp_q, dkv, dq = refs[8:11]
    ends = history_ends(info)
    base = info[8] * GRP
    prev = base - GRP
    dq[...] = jnp.zeros_like(dq)
    dkv[...] = jnp.zeros_like(dkv)

    def over_j(j, _):
        kpos = base + j * BLK
        last = jnp.minimum((end_of(kpos + BLK - 1, ends) - 1 - base) // BLK, NB - 1)

        def over_i(i, _):
            key_side(q, g, kv, dkv, dq, i, j, keep_cols(base + i * BLK, kpos, ends))
            return 0

        return lax.fori_loop(j, last + 1, over_i, 0)

    lax.fori_loop(0, NB, over_j, 0)

    def halo_i(i, _):
        qpos = base + i * BLK

        def halo_j(j, _):
            query_side(q, g, kv_prev, dq, i, j, keep_rows(qpos, prev + j * BLK, ends))
            return 0

        return lax.fori_loop(halo_first(i, qpos, prev, ends), NB, halo_j, 0)

    lax.fori_loop(0, NB, halo_i, 0)
    for k in range(NB):
        at = rows(lax.rem(info[9] + k, NB))
        gp_q[at, :] = (dq[at, :] * dsig[k][:, 2 * BLK : 3 * BLK].astype(F32)).astype(BF16)


def backward_later_body(info, *refs):
    q, g, kv, dkv_in, gp_g, gp_q = refs[0:6]
    dsig, gp = refs[6:10], refs[10:14]
    dkv = refs[14]
    ends = history_ends(info)
    base = info[8] * GRP
    later = base + GRP
    dkv[...] = dkv_in[...]

    def over_j(j, _):
        kpos = base + j * BLK
        end = end_of(kpos + BLK - 1, ends)
        count = jnp.where(end > later, jnp.minimum((end - 1 - later) // BLK, j) + 1, 0)

        def over_i(i, _):
            key_side(q, g, kv, dkv, None, i, j, keep_cols(later + i * BLK, kpos, ends))
            return 0

        return lax.fori_loop(0, count, over_i, 0)

    lax.fori_loop(0, NB, over_j, 0)
    for k in range(NB):
        at = rows(lax.rem(info[9] + k, NB))
        dk = 2.0 * dkv[at, 0:BLK]
        gp[k][:, :BLK] = gp_g[at, :]
        gp[k][:, BLK : 2 * BLK] = gp_q[at, :]
        gp[k][:, 2 * BLK : 3 * BLK] = (dkv[at, BLK:] * dsig[k][:, BLK : 2 * BLK].astype(F32)).astype(BF16)
        gp[k][:, 3 * BLK :] = (dk * dsig[k][:, 3 * BLK :].astype(F32)).astype(BF16)


def input_body(info, *refs):
    gp, (w, cot), outs = refs[0:4], refs[4:6], refs[6:10]
    for k in range(NB):
        total = cot[...].astype(F32) if k == 0 else None
        for n, part in enumerate((0, 2, 1, 3)):
            lanes = pl.ds(pl.multiple_of(part * D + info[9] * BLK, BLK), BLK)
            term = nt(gp[k][:, n * BLK : (n + 1) * BLK], w[:, lanes])
            total = term if total is None else total + term
        outs[k][...] = total.astype(outs[k].dtype)


def add_rows_body(own, got_1, got_2, got_3, out):
    total = own[...] + got_1[...].astype(F32) + got_2[...].astype(F32) + got_3[...].astype(F32)
    out[...] = total.astype(BF16)


def along(x, axis, d):
    return lax.ppermute(x, axis, [(i, (i + d) % 4) for i in range(4)])


def swap(x):
    return lax.ppermute(x, "c", [(0, 1), (1, 0)])


def gather_z(x):
    return [x, along(x, "z", -1), along(x, "z", 2), along(x, "z", 1)]


def exchange(parts, axis):
    return [parts[0]] + [along(parts[d], axis, d) for d in (1, 2, 3)]


def f32(shape):
    return jax.ShapeDtypeStruct(shape, F32)


def bf16(shape):
    return jax.ShapeDtypeStruct(shape, BF16)


def body(events, cotangent, hist, w_in, w_out):
    z = lax.axis_index("z")
    info = jnp.concatenate(
        [hist[0], jnp.stack([lax.axis_index("y"), z, lax.axis_index("c"), lax.axis_index("x")]).astype(jnp.int32)]
    )
    ev, cot = events[0], cotangent[0]
    near = along(ev, "z", -1), along(ev, "z", 1)
    evs = [ev, near[0], None, near[1]]
    kvs, qs, gs, dsigs, kv_prevs = [], [], [], [None] * 4, []
    for blocks in ((0,), (1, 3), (2,)):
        n = len(blocks)
        if blocks == (1, 3):
            ev_far, *near, _ = lax.optimization_barrier((ev, *near, kvs[0]))
            evs = [ev, near[0], along(ev_far, "z", 2), near[1]]
        kv, q, g, *dsig = call(
            project_body,
            (bf16((n * BLK, 2 * BLK)), bf16((n * BLK, BLK)), bf16((n * BLK, BLK))) + (bf16((BLK, 4 * BLK)),) * n,
            n + 1, 1 << 20, 1 << 20,
        )(info, *[evs[b] for b in blocks], w_in)
        kvs.append(kv)
        qs.append(q)
        gs.append(g)
        for b, d in zip(blocks, dsig):
            dsigs[b] = d
        kv_prevs.append(along(kv, "y", 1))
    ggs = call(grad_gated_body, (bf16((BLK, 2 * BLK)),) * 4, 2, 1 << 20, 1 << 20)(info, cot, w_out)
    *ggs, _ = lax.optimization_barrier((*ggs, kvs[1]))
    ggs = exchange(ggs, "z")
    q, kv, att = call(
        forward_local_body, (bf16((GRP, BLK)), bf16((GRP, 2 * BLK)), f32((GRP, BLK))), 6, 5 << 30, 4 << 20
    )(info, *qs, *kvs)
    q_next = along(q, "y", -1)
    att, kv_prev, gg, cot_z, gate, stats = call(
        forward_halo_body,
        (f32((GRP, BLK)), bf16((GRP, 2 * BLK))) + (bf16((GRP, BLK)),) * 3 + (f32((8, GRP)),),
        12, 5 << 30, 4 << 20,
    )(info, q, att, *ggs, *kv_prevs, *gs)
    gatt, gated, gp_g = call(
        norm_body, (bf16((GRP, BLK)),) * 3, 11, 1 << 30, 4 << 20, [pltpu.VMEM((GRP, DH), F32)]
    )(info, att, gg, gate, *gather_z(stats), *dsigs)
    g_next = along(gatt, "y", -1)
    gateds = gather_z(gated)
    gp_q, dkv = call(
        backward_local_body, (bf16((GRP, BLK)), f32((GRP, 2 * BLK))), 8, 1 << 20, 1 << 20,
        [pltpu.VMEM((GRP, BLK), F32)],
    )(info, q, gatt, kv, kv_prev, *dsigs)
    def weights(kernel, cols, operands):
        send, keep = call(
            kernel, (bf16((4, 128, cols)), f32((4, 128, cols))), len(operands), 1 << 20, 1 << 20,
            [pltpu.VMEM((D, cols), F32)],
        )(info, *operands)
        return swap(send), keep

    got_1, keep_1 = weights(early_weights_body, 512, (*evs, gp_g, gp_q))
    q_next, g_next, keep_1 = lax.optimization_barrier((q_next, g_next, keep_1))
    gp = call(
        backward_later_body, (bf16((BLK, 4 * BLK)),) * 4, 10, 5 << 30, 4 << 20, [pltpu.VMEM((GRP, 2 * BLK), F32)]
    )(info, q_next, g_next, kv, dkv, gp_g, gp_q, *dsigs)
    got_2, keep_2 = weights(late_weights_body, 512, (*evs, *gp))
    *partial, = call(
        input_body, (f32((BLK, D)),) + (bf16((BLK, D)),) * 3, 6, 1 << 20, 1 << 20
    )(info, *gp, w_in, cot)
    cot_z, keep_2, partial[0] = lax.optimization_barrier((cot_z, keep_2, partial[0]))
    partial = exchange(partial, "z")
    got_3, keep_3 = weights(out_weights_body, 256, (*gateds, cot_z))
    mine = call(
        add_core_body, bf16((4, 128, 5 * BLK)), 6, 1 << 20, 1 << 20, scalars=0
    )(keep_1, keep_2, keep_3, got_1, got_2, got_3)
    sums = lax.all_to_all(mine.reshape(16, 32, 5 * BLK), ("x", "y"), 0, 0)
    total = call(add_xy_body, bf16((32, 5 * BLK)), 1, 1 << 20, 1 << 20, scalars=0)(sums)
    _, own_rows = lax.optimization_barrier((total, partial[0]))
    grad_events = call(
        add_rows_body, bf16((BLK, D)), 4, 1 << 20, 4 << 20, scalars=0
    )(own_rows, *partial[1:])
    got = lax.all_to_all(total.reshape(4, 8, 5 * BLK), "z", 0, 0)
    grad_w_in, grad_w_out = call(
        last_body, (bf16((8, 4 * D)), bf16((8, D))), 1, 1 << 20, 1 << 20, scalars=0
    )(got)
    return grad_events[None], grad_w_in, grad_w_out


def solution(mesh):
    axes = ("x", "c", "y", "z")
    split = Mesh(mesh.devices.reshape(4, 2, 4, 4), axes)
    dp, seq = ("x", "c"), ("y", "z")
    return jax.shard_map(
        body,
        mesh=split,
        in_specs=(P(dp, seq, None), P(dp, seq, None), P(dp, None), P(), P()),
        out_specs=(P(dp, seq, None), P(axes, None), P(axes, None)),
        check_vma=False,
    )
```

```python
import jax
import jax.numpy as jnp
from jax import lax
from jax.experimental import pallas as pl
from jax.experimental.pallas import tpu as pltpu
from jax.sharding import Mesh
from jax.sharding import PartitionSpec as P

BLK = 256
NB = 4
DH = 128
GRP = NB * BLK
D = 1024
F32 = jnp.float32
BF16 = jnp.bfloat16
SCALE = 1.0 / 256.0
VMEM = pl.BlockSpec(memory_space=pltpu.VMEM)
SMEM = pl.BlockSpec(memory_space=pltpu.SMEM)


def call(body, outs, n_in, flops, nbytes, scratch=(), scalars=1):
    return pl.pallas_call(
        body,
        out_shape=outs,
        in_specs=[SMEM] * scalars + [VMEM] * n_in,
        out_specs=jax.tree.map(lambda _: VMEM, outs),
        scratch_shapes=scratch,
        compiler_params=pltpu.CompilerParams(vmem_limit_bytes=20 * 1024 * 1024),
        cost_estimate=pl.CostEstimate(flops=flops, bytes_accessed=nbytes, transcendentals=0),
    )


def nt(a, b):
    return lax.dot_general(a, b, (((1,), (1,)), ((), ())), preferred_element_type=F32)


def nn(a, b):
    return lax.dot_general(a, b, (((1,), (0,)), ((), ())), preferred_element_type=F32)


def tn(a, b):
    return lax.dot_general(a, b, (((0,), (0,)), ((), ())), preferred_element_type=F32)


def history_ends(info):
    ends, total = [], jnp.int32(0)
    for k in range(8):
        total = total + info[k]
        ends.append(total)
    return ends


def start_of(pos, ends):
    start = jnp.zeros_like(pos)
    for e in ends:
        start = jnp.where(pos >= e, e, start)
    return start


def end_of(pos, ends):
    end = ends[-1]
    for e in reversed(ends):
        end = jnp.where(e > pos, e, end)
    return end


def rows(i):
    return pl.ds(pl.multiple_of(i * BLK, BLK), BLK)


def head(h, base=0):
    return slice(base + h * DH, base + (h + 1) * DH)


def project_body(info, *refs):
    n = (len(refs) - 4) // 2
    ev, (w, kv, q, g), dsig = refs[:n], refs[n : n + 4], refs[n + 4 :]
    for b in range(n):
        x, at = ev[b][...], slice(b * BLK, (b + 1) * BLK)
        for p in range(4):
            lanes = pl.ds(pl.multiple_of(p * D + info[9] * BLK, BLK), BLK)
            proj = nn(x, w[:, lanes])
            sig = 0.5 + 0.5 * jnp.tanh(0.5 * proj)
            act = (proj * sig).astype(BF16)
            if p == 0:
                g[at, :] = act
            elif p == 1:
                kv[at, BLK:] = act
            elif p == 2:
                q[at, :] = (0.5 * act.astype(F32)).astype(BF16)
            else:
                kv[at, :BLK] = act
            dsig[b][:, p * BLK : (p + 1) * BLK] = (sig * (1.0 + proj * (1.0 - sig))).astype(BF16)


def grad_gated_body(info, cot, w, *outs):
    for d in range(NB):
        owner = lax.rem(info[9] + d, NB)
        outs[d][:, :BLK] = nt(cot[...], w[rows(owner), :]).astype(BF16)
        outs[d][:, BLK:] = cot[:, pl.ds(pl.multiple_of(owner * BLK, BLK), BLK)]


def keep_rows(qpos, kpos, ends):
    r = qpos + lax.broadcasted_iota(jnp.int32, (BLK, 1), 0)
    c = kpos + lax.broadcasted_iota(jnp.int32, (1, BLK), 1)
    return jnp.where((c >= start_of(r, ends)) & (c <= r), SCALE, 0.0)


def keep_cols(qpos, kpos, ends):
    r = qpos + lax.broadcasted_iota(jnp.int32, (1, BLK), 1)
    c = kpos + lax.broadcasted_iota(jnp.int32, (BLK, 1), 0)
    return jnp.where((c >= start_of(r, ends)) & (c <= r), SCALE, 0.0)


def attend(q, kv, att, i, j, keep):
    two = range(2)
    qi = [q[rows(i), head(h)] for h in two]
    kj = [kv[rows(j), head(h)] for h in two]
    vj = [kv[rows(j), head(h, BLK)] for h in two]
    u = [nt(qi[h], kj[h]) for h in two]
    w = [(u[h] * (1.0 + jnp.tanh(u[h])) * keep).astype(BF16) for h in two]
    out = [nn(w[h], vj[h]) for h in two]
    for h in two:
        att[rows(i), head(h)] += out[h]


def block_of(parts, k):
    part, at = ((0, 0), (1, 0), (2, 0), (1, BLK))[k]
    return parts[part][at : at + BLK, :]


def forward_local_body(info, *refs):
    q_in, kv_in = refs[0:3], refs[3:6]
    q, kv, att = refs[6:]
    ends = history_ends(info)
    base = info[8] * GRP
    for k in range(NB):
        at = rows(lax.rem(info[9] + k, NB))
        q[at, :] = block_of(q_in, k)
        kv[at, :] = block_of(kv_in, k)
    att[...] = jnp.zeros_like(att)

    def over_i(i, _):
        qpos = base + i * BLK
        first = jnp.maximum(start_of(qpos, ends) - base, 0) // BLK

        def over_j(j, _):
            attend(q, kv, att, i, j, keep_rows(qpos, base + j * BLK, ends))
            return 0

        return lax.fori_loop(first, i + 1, over_j, 0)

    lax.fori_loop(0, NB, over_i, 0)


def halo_first(i, qpos, prev, ends):
    start = start_of(qpos, ends)
    return jnp.where(start >= prev + GRP, NB, jnp.maximum((start - prev) // BLK, i))


def forward_halo_body(info, *refs):
    q, att_in = refs[0:2]
    gg_in, kv_in, gate_in = refs[2:6], refs[6:9], refs[9:12]
    att, kv, gg, cot, gate, stats = refs[12:18]
    ends = history_ends(info)
    base = info[8] * GRP
    prev = base - GRP
    att[...] = att_in[...]
    for k in range(NB):
        at = rows(lax.rem(info[9] + k, NB))
        kv[at, :] = block_of(kv_in, k)
        gate[at, :] = block_of(gate_in, k)
        gg[at, :] = gg_in[(4 - k) % 4][:, :BLK]
        cot[at, :] = gg_in[(4 - k) % 4][:, BLK:]

    def over_i(i, _):
        qpos = base + i * BLK

        def over_j(j, _):
            attend(q, kv, att, i, j, keep_rows(qpos, prev + j * BLK, ends))
            return 0

        return lax.fori_loop(halo_first(i, qpos, prev, ends), NB, over_j, 0)

    lax.fori_loop(0, NB, over_i, 0)
    a = att[...]
    gn = gg[...].astype(F32) * gate[...].astype(F32)
    mean = jnp.sum(a, axis=1, keepdims=True) / BLK
    cent = a - mean
    m2 = jnp.sum(cent * cent, axis=1, keepdims=True)
    g1 = jnp.sum(gn, axis=1, keepdims=True)
    ga = jnp.sum(gn * cent, axis=1, keepdims=True)
    lane = lax.broadcasted_iota(jnp.int32, (GRP, DH), 1)
    packed = jnp.where(lane == 0, mean, jnp.where(lane == 1, m2, jnp.where(lane == 2, g1, ga)))
    stats[...] = packed.T[:8, :]


def norm_body(info, *refs):
    att, gg, gate = refs[0:3]
    stats, dsig = refs[3:7], refs[7:11]
    gatt, gated, gp, table = refs[11:15]
    parts = [s[...] for s in stats]
    mean = (parts[0][0:1] + parts[1][0:1] + parts[2][0:1] + parts[3][0:1]) * 0.25
    m2 = jnp.zeros_like(mean)
    g1 = jnp.zeros_like(mean)
    ga = jnp.zeros_like(mean)
    for p in parts:
        off = p[0:1] - mean
        m2 = m2 + p[1:2] + BLK * off * off
        g1 = g1 + p[2:3]
        ga = ga + p[3:4] + off * p[2:3]
    inv = lax.rsqrt(m2 / D + 1e-6)
    row = lax.broadcasted_iota(jnp.int32, (DH, GRP), 0)
    cols = jnp.where(row == 0, mean, jnp.where(row == 1, inv, jnp.where(row == 2, g1 / D, ga * inv / D)))
    table[...] = cols.T
    for k in range(NB):
        at = rows(lax.rem(info[9] + k, NB))
        t = table[at, :]
        mean_c, inv_c, g1_c, ga_c = (t[:, n : n + 1] for n in range(4))
        normed = (att[at, :] - mean_c) * inv_c
        g = gate[at, :].astype(F32)
        grad_gated = gg[at, :].astype(F32)
        gatt[at, :] = (inv_c * (grad_gated * g - g1_c - normed * ga_c)).astype(BF16)
        gated[at, :] = (normed * g).astype(BF16)
        gp[at, :] = (grad_gated * normed * dsig[k][:, 0:BLK].astype(F32)).astype(BF16)


def pack(info, x, total, lanes, send, keep):
    first = info[10] == 0
    send[x, :, lanes] = jnp.where(first, total[128:], total[:128]).astype(BF16)
    keep[x, :, lanes] = jnp.where(first, total[:128], total[128:])


def early_weights_body(info, *refs):
    ev, (gp_g, gp_q, send, keep) = refs[0:4], refs[4:8]
    for lanes, gp in ((slice(0, BLK), gp_g), (slice(BLK, 2 * BLK), gp_q)):
        for x in range(4):
            part = [
                tn(ev[k][:, x * BLK : (x + 1) * BLK], gp[rows(lax.rem(info[9] + k, NB)), :]) for k in range(NB)
            ]
            pack(info, x, part[0] + part[1] + part[2] + part[3], lanes, send, keep)


def late_weights_body(info, *refs):
    ev, gp = refs[0:4], refs[4:8]
    send, keep = refs[8:10]
    for n in range(2):
        lanes, cols = slice(n * BLK, (n + 1) * BLK), slice((n + 2) * BLK, (n + 3) * BLK)
        for x in range(4):
            part = [tn(ev[k][:, x * BLK : (x + 1) * BLK], gp[k][:, cols]) for k in range(NB)]
            pack(info, x, part[0] + part[1] + part[2] + part[3], lanes, send, keep)


def out_weights_body(info, *refs):
    gated, (cot, send, keep) = refs[0:4], refs[4:7]
    part = [tn(gated[k][...], cot[...]) for k in range(NB)]
    for k in range(NB):
        pack(info, lax.rem(info[9] + k, NB), part[k], slice(0, BLK), send, keep)


def add_core_body(keep_1, keep_2, keep_3, got_1, got_2, got_3, out):
    out[:, :, 0:512] = (keep_1[...] + got_1[...].astype(F32)).astype(BF16)
    out[:, :, 512:1024] = (keep_2[...] + got_2[...].astype(F32)).astype(BF16)
    out[:, :, 1024:] = (keep_3[...] + got_3[...].astype(F32)).astype(BF16)


def add_xy_body(got, total):
    part = got[0].astype(F32)
    for xy in range(1, 16):
        part = part + got[xy].astype(F32)
    total[...] = part.astype(BF16)


def last_body(got, grad_w_in, grad_w_out):
    for z in range(4):
        part = got[z]
        for n, to in enumerate((0, 2, 1, 3)):
            at = to * D + z * BLK
            grad_w_in[:, at : at + BLK] = part[:, n * BLK : (n + 1) * BLK]
        grad_w_out[:, z * BLK : (z + 1) * BLK] = part[:, 4 * BLK :]


def silu_parts(u):
    t = jnp.tanh(u)
    a = 1.0 + t
    ut = u * t
    return u + ut, a * ((1.0 + u) - ut)


def key_side(q, g, kv, dkv, dq, i, j, keep):
    two = range(2)
    half = keep * 0.5
    qi = [q[rows(i), head(h)] for h in two]
    gi = [g[rows(i), head(h)] for h in two]
    kj = [kv[rows(j), head(h)] for h in two]
    vj = [kv[rows(j), head(h, BLK)] for h in two]
    u = [nt(kj[h], qi[h]) for h in two]
    dw = [nt(vj[h], gi[h]) for h in two]
    parts = [silu_parts(u[h]) for h in two]
    w = [(parts[h][0] * keep).astype(BF16) for h in two]
    ds = [(dw[h] * parts[h][1] * half).astype(BF16) for h in two]
    dv = [nn(w[h], gi[h]) for h in two]
    dk = [nn(ds[h], qi[h]) for h in two]
    dqi = [tn(ds[h], kj[h]) for h in two] if dq is not None else None
    for h in two:
        dkv[rows(j), head(h, BLK)] += dv[h]
        dkv[rows(j), head(h)] += dk[h]
        if dq is not None:
            dq[rows(i), head(h)] += dqi[h]


def query_side(q, g, kv, dq, i, j, keep):
    two = range(2)
    half = keep * 0.5
    qi = [q[rows(i), head(h)] for h in two]
    gi = [g[rows(i), head(h)] for h in two]
    kj = [kv[rows(j), head(h)] for h in two]
    vj = [kv[rows(j), head(h, BLK)] for h in two]
    slope = [silu_parts(nt(qi[h], kj[h]))[1] for h in two]
    dw = [nt(gi[h], vj[h]) for h in two]
    ds = [(dw[h] * slope[h] * half).astype(BF16) for h in two]
    dqi = [nn(ds[h], kj[h]) for h in two]
    for h in two:
        dq[rows(i), head(h)] += dqi[h]


def backward_local_body(info, *refs):
    q, g, kv, kv_prev = refs[0:4]
    dsig = refs[4:8]
    gp_q, dkv, dq = refs[8:11]
    ends = history_ends(info)
    base = info[8] * GRP
    prev = base - GRP
    dq[...] = jnp.zeros_like(dq)
    dkv[...] = jnp.zeros_like(dkv)

    def over_j(j, _):
        kpos = base + j * BLK
        last = jnp.minimum((end_of(kpos + BLK - 1, ends) - 1 - base) // BLK, NB - 1)

        def over_i(i, _):
            key_side(q, g, kv, dkv, dq, i, j, keep_cols(base + i * BLK, kpos, ends))
            return 0

        return lax.fori_loop(j, last + 1, over_i, 0)

    lax.fori_loop(0, NB, over_j, 0)

    def halo_i(i, _):
        qpos = base + i * BLK

        def halo_j(j, _):
            query_side(q, g, kv_prev, dq, i, j, keep_rows(qpos, prev + j * BLK, ends))
            return 0

        return lax.fori_loop(halo_first(i, qpos, prev, ends), NB, halo_j, 0)

    lax.fori_loop(0, NB, halo_i, 0)
    for k in range(NB):
        at = rows(lax.rem(info[9] + k, NB))
        gp_q[at, :] = (dq[at, :] * dsig[k][:, 2 * BLK : 3 * BLK].astype(F32)).astype(BF16)


def backward_later_body(info, *refs):
    q, g, kv, dkv_in, gp_g, gp_q = refs[0:6]
    dsig, gp = refs[6:10], refs[10:14]
    dkv = refs[14]
    ends = history_ends(info)
    base = info[8] * GRP
    later = base + GRP
    dkv[...] = dkv_in[...]

    def over_j(j, _):
        kpos = base + j * BLK
        end = end_of(kpos + BLK - 1, ends)
        count = jnp.where(end > later, jnp.minimum((end - 1 - later) // BLK, j) + 1, 0)

        def over_i(i, _):
            key_side(q, g, kv, dkv, None, i, j, keep_cols(later + i * BLK, kpos, ends))
            return 0

        return lax.fori_loop(0, count, over_i, 0)

    lax.fori_loop(0, NB, over_j, 0)
    for k in range(NB):
        at = rows(lax.rem(info[9] + k, NB))
        dk = 2.0 * dkv[at, 0:BLK]
        gp[k][:, :BLK] = gp_g[at, :]
        gp[k][:, BLK : 2 * BLK] = gp_q[at, :]
        gp[k][:, 2 * BLK : 3 * BLK] = (dkv[at, BLK:] * dsig[k][:, BLK : 2 * BLK].astype(F32)).astype(BF16)
        gp[k][:, 3 * BLK :] = (dk * dsig[k][:, 3 * BLK :].astype(F32)).astype(BF16)


def input_body(info, *refs):
    gp, (w, cot), outs = refs[0:4], refs[4:6], refs[6:10]
    for k in range(NB):
        total = cot[...].astype(F32) if k == 0 else None
        for n, part in enumerate((0, 2, 1, 3)):
            lanes = pl.ds(pl.multiple_of(part * D + info[9] * BLK, BLK), BLK)
            term = nt(gp[k][:, n * BLK : (n + 1) * BLK], w[:, lanes])
            total = term if total is None else total + term
        outs[k][...] = total.astype(outs[k].dtype)


def add_rows_body(own, got_1, got_2, got_3, out):
    total = own[...] + got_1[...].astype(F32) + got_2[...].astype(F32) + got_3[...].astype(F32)
    out[...] = total.astype(BF16)


def along(x, axis, d):
    return lax.ppermute(x, axis, [(i, (i + d) % 4) for i in range(4)])


def swap(x):
    return lax.ppermute(x, "c", [(0, 1), (1, 0)])


def gather_z(x):
    return [x, along(x, "z", -1), along(x, "z", 2), along(x, "z", 1)]


def exchange(parts, axis):
    return [parts[0]] + [along(parts[d], axis, d) for d in (1, 2, 3)]


def f32(shape):
    return jax.ShapeDtypeStruct(shape, F32)


def bf16(shape):
    return jax.ShapeDtypeStruct(shape, BF16)


def body(events, cotangent, hist, w_in, w_out):
    z = lax.axis_index("z")
    info = jnp.concatenate(
        [hist[0], jnp.stack([lax.axis_index("y"), z, lax.axis_index("c"), lax.axis_index("x")]).astype(jnp.int32)]
    )
    ev, cot = events[0], cotangent[0]
    near = along(ev, "z", -1), along(ev, "z", 1)
    evs = [ev, near[0], None, near[1]]
    kvs, qs, gs, dsigs, kv_prevs = [], [], [], [None] * 4, []
    for blocks in ((0,), (1, 3), (2,)):
        n = len(blocks)
        if blocks == (1, 3):
            ev_far, *near, _ = lax.optimization_barrier((ev, *near, kvs[0]))
            evs = [ev, near[0], along(ev_far, "z", 2), near[1]]
        kv, q, g, *dsig = call(
            project_body,
            (bf16((n * BLK, 2 * BLK)), bf16((n * BLK, BLK)), bf16((n * BLK, BLK))) + (bf16((BLK, 4 * BLK)),) * n,
            n + 1, 1 << 20, 1 << 20,
        )(info, *[evs[b] for b in blocks], w_in)
        kvs.append(kv)
        qs.append(q)
        gs.append(g)
        for b, d in zip(blocks, dsig):
            dsigs[b] = d
        kv_prevs.append(along(kv, "y", 1))
    ggs = call(grad_gated_body, (bf16((BLK, 2 * BLK)),) * 4, 2, 1 << 20, 1 << 20)(info, cot, w_out)
    *ggs, _ = lax.optimization_barrier((*ggs, kvs[1]))
    ggs = exchange(ggs, "z")
    q, kv, att = call(
        forward_local_body, (bf16((GRP, BLK)), bf16((GRP, 2 * BLK)), f32((GRP, BLK))), 6, 5 << 30, 4 << 20
    )(info, *qs, *kvs)
    q_next = along(q, "y", -1)
    att, kv_prev, gg, cot_z, gate, stats = call(
        forward_halo_body,
        (f32((GRP, BLK)), bf16((GRP, 2 * BLK))) + (bf16((GRP, BLK)),) * 3 + (f32((8, GRP)),),
        12, 5 << 30, 4 << 20,
    )(info, q, att, *ggs, *kv_prevs, *gs)
    gatt, gated, gp_g = call(
        norm_body, (bf16((GRP, BLK)),) * 3, 11, 1 << 30, 4 << 20, [pltpu.VMEM((GRP, DH), F32)]
    )(info, att, gg, gate, *gather_z(stats), *dsigs)
    g_next = along(gatt, "y", -1)
    gateds = gather_z(gated)
    gp_q, dkv = call(
        backward_local_body, (bf16((GRP, BLK)), f32((GRP, 2 * BLK))), 8, 1 << 20, 1 << 20,
        [pltpu.VMEM((GRP, BLK), F32)],
    )(info, q, gatt, kv, kv_prev, *dsigs)
    def weights(kernel, cols, operands):
        send, keep = call(
            kernel, (bf16((4, 128, cols)), f32((4, 128, cols))), len(operands), 1 << 20, 1 << 20
        )(info, *operands)
        return swap(send), keep

    got_1, keep_1 = weights(early_weights_body, 512, (*evs, gp_g, gp_q))
    q_next, g_next, keep_1 = lax.optimization_barrier((q_next, g_next, keep_1))
    gp = call(
        backward_later_body, (bf16((BLK, 4 * BLK)),) * 4, 10, 5 << 30, 4 << 20, [pltpu.VMEM((GRP, 2 * BLK), F32)]
    )(info, q_next, g_next, kv, dkv, gp_g, gp_q, *dsigs)
    got_2, keep_2 = weights(late_weights_body, 512, (*evs, *gp))
    *partial, = call(
        input_body, (f32((BLK, D)),) + (bf16((BLK, D)),) * 3, 6, 1 << 20, 1 << 20
    )(info, *gp, w_in, cot)
    cot_z, keep_2, partial[0] = lax.optimization_barrier((cot_z, keep_2, partial[0]))
    partial = exchange(partial, "z")
    got_3, keep_3 = weights(out_weights_body, 256, (*gateds, cot_z))
    mine = call(
        add_core_body, bf16((4, 128, 5 * BLK)), 6, 1 << 20, 1 << 20, scalars=0
    )(keep_1, keep_2, keep_3, got_1, got_2, got_3)
    sums = lax.all_to_all(mine.reshape(16, 32, 5 * BLK), ("x", "y"), 0, 0)
    total = call(add_xy_body, bf16((32, 5 * BLK)), 1, 1 << 20, 1 << 20, scalars=0)(sums)
    _, own_rows = lax.optimization_barrier((total, partial[0]))
    grad_events = call(
        add_rows_body, bf16((BLK, D)), 4, 1 << 20, 4 << 20, scalars=0
    )(own_rows, *partial[1:])
    got = lax.all_to_all(total.reshape(4, 8, 5 * BLK), "z", 0, 0)
    grad_w_in, grad_w_out = call(
        last_body, (bf16((8, 4 * D)), bf16((8, D))), 1, 1 << 20, 1 << 20, scalars=0
    )(got)
    return grad_events[None], grad_w_in, grad_w_out


def solution(mesh):
    axes = ("x", "c", "y", "z")
    split = Mesh(mesh.devices.reshape(4, 2, 4, 4), axes)
    dp, seq = ("x", "c"), ("y", "z")
    return jax.shard_map(
        body,
        mesh=split,
        in_specs=(P(dp, seq, None), P(dp, seq, None), P(dp, None), P(), P()),
        out_specs=(P(dp, seq, None), P(axes, None), P(axes, None)),
        check_vma=False,
    )
```

```python
import jax
import jax.numpy as jnp
from jax import lax
from jax.experimental import pallas as pl
from jax.experimental.pallas import tpu as pltpu
from jax.sharding import Mesh
from jax.sharding import PartitionSpec as P

BLK = 256
NB = 4
DH = 128
GRP = NB * BLK
D = 1024
F32 = jnp.float32
BF16 = jnp.bfloat16
SCALE = 1.0 / 256.0
VMEM = pl.BlockSpec(memory_space=pltpu.VMEM)
SMEM = pl.BlockSpec(memory_space=pltpu.SMEM)


def call(body, outs, n_in, flops, nbytes, scratch=(), scalars=1):
    return pl.pallas_call(
        body,
        out_shape=outs,
        in_specs=[SMEM] * scalars + [VMEM] * n_in,
        out_specs=jax.tree.map(lambda _: VMEM, outs),
        scratch_shapes=scratch,
        compiler_params=pltpu.CompilerParams(vmem_limit_bytes=20 * 1024 * 1024),
        cost_estimate=pl.CostEstimate(flops=flops, bytes_accessed=nbytes, transcendentals=0),
    )


def nt(a, b):
    return lax.dot_general(a, b, (((1,), (1,)), ((), ())), preferred_element_type=F32)


def nn(a, b):
    return lax.dot_general(a, b, (((1,), (0,)), ((), ())), preferred_element_type=F32)


def tn(a, b):
    return lax.dot_general(a, b, (((0,), (0,)), ((), ())), preferred_element_type=F32)


def history_ends(info):
    ends, total = [], jnp.int32(0)
    for k in range(8):
        total = total + info[k]
        ends.append(total)
    return ends


def start_of(pos, ends):
    start = jnp.zeros_like(pos)
    for e in ends:
        start = jnp.where(pos >= e, e, start)
    return start


def end_of(pos, ends):
    end = ends[-1]
    for e in reversed(ends):
        end = jnp.where(e > pos, e, end)
    return end


def rows(i):
    return pl.ds(pl.multiple_of(i * BLK, BLK), BLK)


def head(h, base=0):
    return slice(base + h * DH, base + (h + 1) * DH)


def project_body(info, *refs):
    n = (len(refs) - 4) // 2
    ev, (w, kv, q, g), dsig = refs[:n], refs[n : n + 4], refs[n + 4 :]
    for b in range(n):
        x, at = ev[b][...], slice(b * BLK, (b + 1) * BLK)
        for p in range(4):
            lanes = pl.ds(pl.multiple_of(p * D + info[9] * BLK, BLK), BLK)
            proj = nn(x, w[:, lanes])
            sig = 0.5 + 0.5 * jnp.tanh(0.5 * proj)
            act = (proj * sig).astype(BF16)
            if p == 0:
                g[at, :] = act
            elif p == 1:
                kv[at, BLK:] = act
            elif p == 2:
                q[at, :] = (0.5 * act.astype(F32)).astype(BF16)
            else:
                kv[at, :BLK] = act
            dsig[b][:, p * BLK : (p + 1) * BLK] = (sig * (1.0 + proj * (1.0 - sig))).astype(BF16)


def grad_gated_body(info, cot, w, *outs):
    for d in range(NB):
        owner = lax.rem(info[9] + d, NB)
        outs[d][:, :BLK] = nt(cot[...], w[rows(owner), :]).astype(BF16)
        outs[d][:, BLK:] = cot[:, pl.ds(pl.multiple_of(owner * BLK, BLK), BLK)]


def keep_rows(qpos, kpos, ends):
    r = qpos + lax.broadcasted_iota(jnp.int32, (BLK, 1), 0)
    c = kpos + lax.broadcasted_iota(jnp.int32, (1, BLK), 1)
    return jnp.where((c >= start_of(r, ends)) & (c <= r), SCALE, 0.0)


def keep_cols(qpos, kpos, ends):
    r = qpos + lax.broadcasted_iota(jnp.int32, (1, BLK), 1)
    c = kpos + lax.broadcasted_iota(jnp.int32, (BLK, 1), 0)
    return jnp.where((c >= start_of(r, ends)) & (c <= r), SCALE, 0.0)


def attend(q, kv, att, i, j, keep):
    two = range(2)
    qi = [q[rows(i), head(h)] for h in two]
    kj = [kv[rows(j), head(h)] for h in two]
    vj = [kv[rows(j), head(h, BLK)] for h in two]
    u = [nt(qi[h], kj[h]) for h in two]
    w = [(u[h] * (1.0 + jnp.tanh(u[h])) * keep).astype(BF16) for h in two]
    out = [nn(w[h], vj[h]) for h in two]
    for h in two:
        att[rows(i), head(h)] += out[h]


def block_of(parts, k):
    part, at = ((0, 0), (1, 0), (2, 0), (1, BLK))[k]
    return parts[part][at : at + BLK, :]


def forward_local_body(info, *refs):
    q_in, kv_in = refs[0:3], refs[3:6]
    q, kv, att = refs[6:]
    ends = history_ends(info)
    base = info[8] * GRP
    for k in range(NB):
        at = rows(lax.rem(info[9] + k, NB))
        q[at, :] = block_of(q_in, k)
        kv[at, :] = block_of(kv_in, k)
    att[...] = jnp.zeros_like(att)

    def over_i(i, _):
        qpos = base + i * BLK
        first = jnp.maximum(start_of(qpos, ends) - base, 0) // BLK

        def over_j(j, _):
            attend(q, kv, att, i, j, keep_rows(qpos, base + j * BLK, ends))
            return 0

        return lax.fori_loop(first, i + 1, over_j, 0)

    lax.fori_loop(0, NB, over_i, 0)


def halo_first(i, qpos, prev, ends):
    start = start_of(qpos, ends)
    return jnp.where(start >= prev + GRP, NB, jnp.maximum((start - prev) // BLK, i))


def forward_halo_body(info, *refs):
    q, att_in = refs[0:2]
    gg_in, kv_in, gate_in = refs[2:6], refs[6:9], refs[9:12]
    att, kv, gg, cot, gate, stats = refs[12:18]
    ends = history_ends(info)
    base = info[8] * GRP
    prev = base - GRP
    att[...] = att_in[...]
    for k in range(NB):
        at = rows(lax.rem(info[9] + k, NB))
        kv[at, :] = block_of(kv_in, k)
        gate[at, :] = block_of(gate_in, k)
        gg[at, :] = gg_in[(4 - k) % 4][:, :BLK]
        cot[at, :] = gg_in[(4 - k) % 4][:, BLK:]

    def over_i(i, _):
        qpos = base + i * BLK

        def over_j(j, _):
            attend(q, kv, att, i, j, keep_rows(qpos, prev + j * BLK, ends))
            return 0

        return lax.fori_loop(halo_first(i, qpos, prev, ends), NB, over_j, 0)

    lax.fori_loop(0, NB, over_i, 0)
    a = att[...]
    gn = gg[...].astype(F32) * gate[...].astype(F32)
    mean = jnp.sum(a, axis=1, keepdims=True) / BLK
    cent = a - mean
    m2 = jnp.sum(cent * cent, axis=1, keepdims=True)
    g1 = jnp.sum(gn, axis=1, keepdims=True)
    ga = jnp.sum(gn * cent, axis=1, keepdims=True)
    lane = lax.broadcasted_iota(jnp.int32, (GRP, DH), 1)
    packed = jnp.where(lane == 0, mean, jnp.where(lane == 1, m2, jnp.where(lane == 2, g1, ga)))
    stats[...] = packed.T[:8, :]


def norm_body(info, *refs):
    att, gg, gate = refs[0:3]
    stats, dsig = refs[3:7], refs[7:11]
    gatt, gated, gp, table = refs[11:15]
    parts = [s[...] for s in stats]
    mean = (parts[0][0:1] + parts[1][0:1] + parts[2][0:1] + parts[3][0:1]) * 0.25
    m2 = jnp.zeros_like(mean)
    g1 = jnp.zeros_like(mean)
    ga = jnp.zeros_like(mean)
    for p in parts:
        off = p[0:1] - mean
        m2 = m2 + p[1:2] + BLK * off * off
        g1 = g1 + p[2:3]
        ga = ga + p[3:4] + off * p[2:3]
    inv = lax.rsqrt(m2 / D + 1e-6)
    row = lax.broadcasted_iota(jnp.int32, (DH, GRP), 0)
    cols = jnp.where(row == 0, mean, jnp.where(row == 1, inv, jnp.where(row == 2, g1 / D, ga * inv / D)))
    table[...] = cols.T
    for k in range(NB):
        at = rows(lax.rem(info[9] + k, NB))
        t = table[at, :]
        mean_c, inv_c, g1_c, ga_c = (t[:, n : n + 1] for n in range(4))
        normed = (att[at, :] - mean_c) * inv_c
        g = gate[at, :].astype(F32)
        grad_gated = gg[at, :].astype(F32)
        gatt[at, :] = (inv_c * (grad_gated * g - g1_c - normed * ga_c)).astype(BF16)
        gated[at, :] = (normed * g).astype(BF16)
        gp[at, :] = (grad_gated * normed * dsig[k][:, 0:BLK].astype(F32)).astype(BF16)


def pack(info, x, total, lanes, send, keep):
    first = info[10] == 0
    send[x, :, lanes] = jnp.where(first, total[128:], total[:128]).astype(BF16)
    keep[x, :, lanes] = jnp.where(first, total[:128], total[128:])


def transpose_body(*refs):
    ev, out = refs[0:4], refs[4]
    for k in range(NB):
        out[:, k * BLK : (k + 1) * BLK] = ev[k][...].T


def early_weights_body(info, et, gp_g, gp_q, send, keep):
    for lanes, gp in ((slice(0, BLK), gp_g), (slice(BLK, 2 * BLK), gp_q)):
        for x in range(4):
            part = [
                nn(et[x * BLK : (x + 1) * BLK, k * BLK : (k + 1) * BLK], gp[rows(lax.rem(info[9] + k, NB)), :])
                for k in range(NB)
            ]
            pack(info, x, part[0] + part[1] + part[2] + part[3], lanes, send, keep)


def late_weights_body(info, *refs):
    et, gp, (send, keep) = refs[0], refs[1:5], refs[5:7]
    for n in range(2):
        lanes, cols = slice(n * BLK, (n + 1) * BLK), slice((n + 2) * BLK, (n + 3) * BLK)
        for x in range(4):
            part = [
                nn(et[x * BLK : (x + 1) * BLK, k * BLK : (k + 1) * BLK], gp[k][:, cols]) for k in range(NB)
            ]
            pack(info, x, part[0] + part[1] + part[2] + part[3], lanes, send, keep)


def out_weights_body(info, *refs):
    gated, (cot, send, keep) = refs[0:4], refs[4:7]
    part = [tn(gated[k][...], cot[...]) for k in range(NB)]
    for k in range(NB):
        pack(info, lax.rem(info[9] + k, NB), part[k], slice(0, BLK), send, keep)


def add_core_body(keep_1, keep_2, keep_3, got_1, got_2, got_3, out):
    out[:, :, 0:512] = (keep_1[...] + got_1[...].astype(F32)).astype(BF16)
    out[:, :, 512:1024] = (keep_2[...] + got_2[...].astype(F32)).astype(BF16)
    out[:, :, 1024:] = (keep_3[...] + got_3[...].astype(F32)).astype(BF16)


def add_xy_body(got, total):
    part = got[0].astype(F32)
    for xy in range(1, 16):
        part = part + got[xy].astype(F32)
    total[...] = part.astype(BF16)


def last_body(got, grad_w_in, grad_w_out):
    for z in range(4):
        part = got[z]
        for n, to in enumerate((0, 2, 1, 3)):
            at = to * D + z * BLK
            grad_w_in[:, at : at + BLK] = part[:, n * BLK : (n + 1) * BLK]
        grad_w_out[:, z * BLK : (z + 1) * BLK] = part[:, 4 * BLK :]


def silu_parts(u):
    t = jnp.tanh(u)
    a = 1.0 + t
    ut = u * t
    return u + ut, a * ((1.0 + u) - ut)


def key_side(q, g, kv, dkv, dq, i, j, keep):
    two = range(2)
    half = keep * 0.5
    qi = [q[rows(i), head(h)] for h in two]
    gi = [g[rows(i), head(h)] for h in two]
    kj = [kv[rows(j), head(h)] for h in two]
    vj = [kv[rows(j), head(h, BLK)] for h in two]
    u = [nt(kj[h], qi[h]) for h in two]
    dw = [nt(vj[h], gi[h]) for h in two]
    parts = [silu_parts(u[h]) for h in two]
    w = [(parts[h][0] * keep).astype(BF16) for h in two]
    ds = [(dw[h] * parts[h][1] * half).astype(BF16) for h in two]
    dv = [nn(w[h], gi[h]) for h in two]
    dk = [nn(ds[h], qi[h]) for h in two]
    dqi = [tn(ds[h], kj[h]) for h in two] if dq is not None else None
    for h in two:
        dkv[rows(j), head(h, BLK)] += dv[h]
        dkv[rows(j), head(h)] += dk[h]
        if dq is not None:
            dq[rows(i), head(h)] += dqi[h]


def query_side(q, g, kv, dq, i, j, keep):
    two = range(2)
    half = keep * 0.5
    qi = [q[rows(i), head(h)] for h in two]
    gi = [g[rows(i), head(h)] for h in two]
    kj = [kv[rows(j), head(h)] for h in two]
    vj = [kv[rows(j), head(h, BLK)] for h in two]
    slope = [silu_parts(nt(qi[h], kj[h]))[1] for h in two]
    dw = [nt(gi[h], vj[h]) for h in two]
    ds = [(dw[h] * slope[h] * half).astype(BF16) for h in two]
    dqi = [nn(ds[h], kj[h]) for h in two]
    for h in two:
        dq[rows(i), head(h)] += dqi[h]


def backward_local_body(info, *refs):
    q, g, kv, kv_prev = refs[0:4]
    dsig = refs[4:8]
    gp_q, dkv, dq = refs[8:11]
    ends = history_ends(info)
    base = info[8] * GRP
    prev = base - GRP
    dq[...] = jnp.zeros_like(dq)
    dkv[...] = jnp.zeros_like(dkv)

    def over_j(j, _):
        kpos = base + j * BLK
        last = jnp.minimum((end_of(kpos + BLK - 1, ends) - 1 - base) // BLK, NB - 1)

        def over_i(i, _):
            key_side(q, g, kv, dkv, dq, i, j, keep_cols(base + i * BLK, kpos, ends))
            return 0

        return lax.fori_loop(j, last + 1, over_i, 0)

    lax.fori_loop(0, NB, over_j, 0)

    def halo_i(i, _):
        qpos = base + i * BLK

        def halo_j(j, _):
            query_side(q, g, kv_prev, dq, i, j, keep_rows(qpos, prev + j * BLK, ends))
            return 0

        return lax.fori_loop(halo_first(i, qpos, prev, ends), NB, halo_j, 0)

    lax.fori_loop(0, NB, halo_i, 0)
    for k in range(NB):
        at = rows(lax.rem(info[9] + k, NB))
        gp_q[at, :] = (dq[at, :] * dsig[k][:, 2 * BLK : 3 * BLK].astype(F32)).astype(BF16)


def backward_later_body(info, *refs):
    q, g, kv, dkv_in, gp_g, gp_q = refs[0:6]
    dsig, gp = refs[6:10], refs[10:14]
    dkv = refs[14]
    ends = history_ends(info)
    base = info[8] * GRP
    later = base + GRP
    dkv[...] = dkv_in[...]

    def over_j(j, _):
        kpos = base + j * BLK
        end = end_of(kpos + BLK - 1, ends)
        count = jnp.where(end > later, jnp.minimum((end - 1 - later) // BLK, j) + 1, 0)

        def over_i(i, _):
            key_side(q, g, kv, dkv, None, i, j, keep_cols(later + i * BLK, kpos, ends))
            return 0

        return lax.fori_loop(0, count, over_i, 0)

    lax.fori_loop(0, NB, over_j, 0)
    for k in range(NB):
        at = rows(lax.rem(info[9] + k, NB))
        dk = 2.0 * dkv[at, 0:BLK]
        gp[k][:, :BLK] = gp_g[at, :]
        gp[k][:, BLK : 2 * BLK] = gp_q[at, :]
        gp[k][:, 2 * BLK : 3 * BLK] = (dkv[at, BLK:] * dsig[k][:, BLK : 2 * BLK].astype(F32)).astype(BF16)
        gp[k][:, 3 * BLK :] = (dk * dsig[k][:, 3 * BLK :].astype(F32)).astype(BF16)


def input_body(info, *refs):
    gp, (w, cot), outs = refs[0:4], refs[4:6], refs[6:10]
    for k in range(NB):
        total = cot[...].astype(F32) if k == 0 else None
        for n, part in enumerate((0, 2, 1, 3)):
            lanes = pl.ds(pl.multiple_of(part * D + info[9] * BLK, BLK), BLK)
            term = nt(gp[k][:, n * BLK : (n + 1) * BLK], w[:, lanes])
            total = term if total is None else total + term
        outs[k][...] = total.astype(outs[k].dtype)


def add_rows_body(own, got_1, got_2, got_3, out):
    total = own[...] + got_1[...].astype(F32) + got_2[...].astype(F32) + got_3[...].astype(F32)
    out[...] = total.astype(BF16)


def along(x, axis, d):
    return lax.ppermute(x, axis, [(i, (i + d) % 4) for i in range(4)])


def swap(x):
    return lax.ppermute(x, "c", [(0, 1), (1, 0)])


def gather_z(x):
    return [x, along(x, "z", -1), along(x, "z", 2), along(x, "z", 1)]


def exchange(parts, axis):
    return [parts[0]] + [along(parts[d], axis, d) for d in (1, 2, 3)]


def f32(shape):
    return jax.ShapeDtypeStruct(shape, F32)


def bf16(shape):
    return jax.ShapeDtypeStruct(shape, BF16)


def body(events, cotangent, hist, w_in, w_out):
    z = lax.axis_index("z")
    info = jnp.concatenate(
        [hist[0], jnp.stack([lax.axis_index("y"), z, lax.axis_index("c"), lax.axis_index("x")]).astype(jnp.int32)]
    )
    ev, cot = events[0], cotangent[0]
    near = along(ev, "z", -1), along(ev, "z", 1)
    evs = [ev, near[0], None, near[1]]
    kvs, qs, gs, dsigs, kv_prevs = [], [], [], [None] * 4, []
    for blocks in ((0,), (1, 3), (2,)):
        n = len(blocks)
        if blocks == (1, 3):
            ev_far, *near, _ = lax.optimization_barrier((ev, *near, kvs[0]))
            evs = [ev, near[0], along(ev_far, "z", 2), near[1]]
        kv, q, g, *dsig = call(
            project_body,
            (bf16((n * BLK, 2 * BLK)), bf16((n * BLK, BLK)), bf16((n * BLK, BLK))) + (bf16((BLK, 4 * BLK)),) * n,
            n + 1, 1 << 20, 1 << 20,
        )(info, *[evs[b] for b in blocks], w_in)
        kvs.append(kv)
        qs.append(q)
        gs.append(g)
        for b, d in zip(blocks, dsig):
            dsigs[b] = d
        kv_prevs.append(along(kv, "y", 1))
    ggs = call(grad_gated_body, (bf16((BLK, 2 * BLK)),) * 4, 2, 1 << 20, 1 << 20)(info, cot, w_out)
    *ggs, _ = lax.optimization_barrier((*ggs, kvs[1]))
    ggs = exchange(ggs, "z")
    q, kv, att = call(
        forward_local_body, (bf16((GRP, BLK)), bf16((GRP, 2 * BLK)), f32((GRP, BLK))), 6, 5 << 30, 4 << 20
    )(info, *qs, *kvs)
    q_next = along(q, "y", -1)
    *evs, att = lax.optimization_barrier((*evs, att))
    et = call(transpose_body, bf16((D, GRP)), 4, 1 << 20, 1 << 20, scalars=0)(*evs)
    att, et = lax.optimization_barrier((att, et))
    att, kv_prev, gg, cot_z, gate, stats = call(
        forward_halo_body,
        (f32((GRP, BLK)), bf16((GRP, 2 * BLK))) + (bf16((GRP, BLK)),) * 3 + (f32((8, GRP)),),
        12, 5 << 30, 4 << 20,
    )(info, q, att, *ggs, *kv_prevs, *gs)
    gatt, gated, gp_g = call(
        norm_body, (bf16((GRP, BLK)),) * 3, 11, 1 << 30, 4 << 20, [pltpu.VMEM((GRP, DH), F32)]
    )(info, att, gg, gate, *gather_z(stats), *dsigs)
    g_next = along(gatt, "y", -1)
    gateds = gather_z(gated)
    gp_q, dkv = call(
        backward_local_body, (bf16((GRP, BLK)), f32((GRP, 2 * BLK))), 8, 1 << 20, 1 << 20,
        [pltpu.VMEM((GRP, BLK), F32)],
    )(info, q, gatt, kv, kv_prev, *dsigs)
    def weights(kernel, cols, operands):
        send, keep = call(
            kernel, (bf16((4, 128, cols)), f32((4, 128, cols))), len(operands), 1 << 20, 1 << 20
        )(info, *operands)
        return swap(send), keep

    got_1, keep_1 = weights(early_weights_body, 512, (et, gp_g, gp_q))
    q_next, g_next, keep_1 = lax.optimization_barrier((q_next, g_next, keep_1))
    gp = call(
        backward_later_body, (bf16((BLK, 4 * BLK)),) * 4, 10, 5 << 30, 4 << 20, [pltpu.VMEM((GRP, 2 * BLK), F32)]
    )(info, q_next, g_next, kv, dkv, gp_g, gp_q, *dsigs)
    got_2, keep_2 = weights(late_weights_body, 512, (et, *gp))
    *partial, = call(
        input_body, (f32((BLK, D)),) + (bf16((BLK, D)),) * 3, 6, 1 << 20, 1 << 20
    )(info, *gp, w_in, cot)
    cot_z, keep_2, partial[0] = lax.optimization_barrier((cot_z, keep_2, partial[0]))
    partial = exchange(partial, "z")
    got_3, keep_3 = weights(out_weights_body, 256, (*gateds, cot_z))
    mine = call(
        add_core_body, bf16((4, 128, 5 * BLK)), 6, 1 << 20, 1 << 20, scalars=0
    )(keep_1, keep_2, keep_3, got_1, got_2, got_3)
    sums = lax.all_to_all(mine.reshape(16, 32, 5 * BLK), ("x", "y"), 0, 0)
    total = call(add_xy_body, bf16((32, 5 * BLK)), 1, 1 << 20, 1 << 20, scalars=0)(sums)
    _, own_rows = lax.optimization_barrier((total, partial[0]))
    grad_events = call(
        add_rows_body, bf16((BLK, D)), 4, 1 << 20, 4 << 20, scalars=0
    )(own_rows, *partial[1:])
    got = lax.all_to_all(total.reshape(4, 8, 5 * BLK), "z", 0, 0)
    grad_w_in, grad_w_out = call(
        last_body, (bf16((8, 4 * D)), bf16((8, D))), 1, 1 << 20, 1 << 20, scalars=0
    )(got)
    return grad_events[None], grad_w_in, grad_w_out


def solution(mesh):
    axes = ("x", "c", "y", "z")
    split = Mesh(mesh.devices.reshape(4, 2, 4, 4), axes)
    dp, seq = ("x", "c"), ("y", "z")
    return jax.shard_map(
        body,
        mesh=split,
        in_specs=(P(dp, seq, None), P(dp, seq, None), P(dp, None), P(), P()),
        out_specs=(P(dp, seq, None), P(axes, None), P(axes, None)),
        check_vma=False,
    )
```

```python
import jax
import jax.numpy as jnp
from jax import lax
from jax.experimental import pallas as pl
from jax.experimental.pallas import tpu as pltpu
from jax.sharding import Mesh
from jax.sharding import PartitionSpec as P

BLK = 256
NB = 4
DH = 128
GRP = NB * BLK
D = 1024
F32 = jnp.float32
BF16 = jnp.bfloat16
SCALE = 1.0 / 256.0
VMEM = pl.BlockSpec(memory_space=pltpu.VMEM)
SMEM = pl.BlockSpec(memory_space=pltpu.SMEM)


def call(body, outs, n_in, flops, nbytes, scratch=(), scalars=1):
    return pl.pallas_call(
        body,
        out_shape=outs,
        in_specs=[SMEM] * scalars + [VMEM] * n_in,
        out_specs=jax.tree.map(lambda _: VMEM, outs),
        scratch_shapes=scratch,
        compiler_params=pltpu.CompilerParams(vmem_limit_bytes=20 * 1024 * 1024),
        cost_estimate=pl.CostEstimate(flops=flops, bytes_accessed=nbytes, transcendentals=0),
    )


def nt(a, b):
    return lax.dot_general(a, b, (((1,), (1,)), ((), ())), preferred_element_type=F32)


def nn(a, b):
    return lax.dot_general(a, b, (((1,), (0,)), ((), ())), preferred_element_type=F32)


def tn(a, b):
    return lax.dot_general(a, b, (((0,), (0,)), ((), ())), preferred_element_type=F32)


def history_ends(info):
    ends, total = [], jnp.int32(0)
    for k in range(8):
        total = total + info[k]
        ends.append(total)
    return ends


def start_of(pos, ends):
    start = jnp.zeros_like(pos)
    for e in ends:
        start = jnp.where(pos >= e, e, start)
    return start


def end_of(pos, ends):
    end = ends[-1]
    for e in reversed(ends):
        end = jnp.where(e > pos, e, end)
    return end


def rows(i):
    return pl.ds(pl.multiple_of(i * BLK, BLK), BLK)


def head(h, base=0):
    return slice(base + h * DH, base + (h + 1) * DH)


def project_body(info, *refs):
    n = (len(refs) - 4) // 2
    ev, (w, kv, q, g), dsig = refs[:n], refs[n : n + 4], refs[n + 4 :]
    for b in range(n):
        x, at = ev[b][...], slice(b * BLK, (b + 1) * BLK)
        for p in range(4):
            lanes = pl.ds(pl.multiple_of(p * D + info[9] * BLK, BLK), BLK)
            proj = nn(x, w[:, lanes])
            sig = 0.5 + 0.5 * jnp.tanh(0.5 * proj)
            act = (proj * sig).astype(BF16)
            if p == 0:
                g[at, :] = act
            elif p == 1:
                kv[at, BLK:] = act
            elif p == 2:
                q[at, :] = (0.5 * act.astype(F32)).astype(BF16)
            else:
                kv[at, :BLK] = act
            dsig[b][:, p * BLK : (p + 1) * BLK] = (sig * (1.0 + proj * (1.0 - sig))).astype(BF16)


def grad_gated_body(info, cot, w, *outs):
    for d in range(NB):
        owner = lax.rem(info[9] + d, NB)
        outs[d][:, :BLK] = nt(cot[...], w[rows(owner), :]).astype(BF16)
        outs[d][:, BLK:] = cot[:, pl.ds(pl.multiple_of(owner * BLK, BLK), BLK)]


def keep_rows(qpos, kpos, ends):
    r = qpos + lax.broadcasted_iota(jnp.int32, (BLK, 1), 0)
    c = kpos + lax.broadcasted_iota(jnp.int32, (1, BLK), 1)
    return jnp.where((c >= start_of(r, ends)) & (c <= r), SCALE, 0.0)


def keep_cols(qpos, kpos, ends):
    r = qpos + lax.broadcasted_iota(jnp.int32, (1, BLK), 1)
    c = kpos + lax.broadcasted_iota(jnp.int32, (BLK, 1), 0)
    return jnp.where((c >= start_of(r, ends)) & (c <= r), SCALE, 0.0)


def attend(q, kv, att, i, j, keep):
    two = range(2)
    qi = [q[rows(i), head(h)] for h in two]
    kj = [kv[rows(j), head(h)] for h in two]
    vj = [kv[rows(j), head(h, BLK)] for h in two]
    u = [nt(qi[h], kj[h]) for h in two]
    w = [(u[h] * (1.0 + jnp.tanh(u[h])) * keep).astype(BF16) for h in two]
    out = [nn(w[h], vj[h]) for h in two]
    for h in two:
        att[rows(i), head(h)] += out[h]


def block_of(parts, k):
    part, at = ((0, 0), (1, 0), (2, 0), (1, BLK))[k]
    return parts[part][at : at + BLK, :]


def forward_local_body(info, *refs):
    q_in, kv_in = refs[0:3], refs[3:6]
    q, kv, att = refs[6:]
    ends = history_ends(info)
    base = info[8] * GRP
    for k in range(NB):
        at = rows(lax.rem(info[9] + k, NB))
        q[at, :] = block_of(q_in, k)
        kv[at, :] = block_of(kv_in, k)
    att[...] = jnp.zeros_like(att)

    def over_i(i, _):
        qpos = base + i * BLK
        first = jnp.maximum(start_of(qpos, ends) - base, 0) // BLK

        def over_j(j, _):
            attend(q, kv, att, i, j, keep_rows(qpos, base + j * BLK, ends))
            return 0

        return lax.fori_loop(first, i + 1, over_j, 0)

    lax.fori_loop(0, NB, over_i, 0)


def halo_first(i, qpos, prev, ends):
    start = start_of(qpos, ends)
    return jnp.where(start >= prev + GRP, NB, jnp.maximum((start - prev) // BLK, i))


def forward_halo_body(info, *refs):
    q, att_in = refs[0:2]
    gg_in, kv_in, gate_in = refs[2:6], refs[6:9], refs[9:12]
    att, kv, gg, cot, gate, stats = refs[12:18]
    ends = history_ends(info)
    base = info[8] * GRP
    prev = base - GRP
    att[...] = att_in[...]
    for k in range(NB):
        at = rows(lax.rem(info[9] + k, NB))
        kv[at, :] = block_of(kv_in, k)
        gate[at, :] = block_of(gate_in, k)
        gg[at, :] = gg_in[(4 - k) % 4][:, :BLK]
        cot[at, :] = gg_in[(4 - k) % 4][:, BLK:]

    def over_i(i, _):
        qpos = base + i * BLK

        def over_j(j, _):
            attend(q, kv, att, i, j, keep_rows(qpos, prev + j * BLK, ends))
            return 0

        return lax.fori_loop(halo_first(i, qpos, prev, ends), NB, over_j, 0)

    lax.fori_loop(0, NB, over_i, 0)
    a = att[...]
    gn = gg[...].astype(F32) * gate[...].astype(F32)
    mean = jnp.sum(a, axis=1, keepdims=True) / BLK
    cent = a - mean
    m2 = jnp.sum(cent * cent, axis=1, keepdims=True)
    g1 = jnp.sum(gn, axis=1, keepdims=True)
    ga = jnp.sum(gn * cent, axis=1, keepdims=True)
    lane = lax.broadcasted_iota(jnp.int32, (GRP, DH), 1)
    packed = jnp.where(lane == 0, mean, jnp.where(lane == 1, m2, jnp.where(lane == 2, g1, ga)))
    stats[...] = packed.T[:8, :]


def norm_body(info, *refs):
    att, gg, gate = refs[0:3]
    stats, dsig = refs[3:7], refs[7:11]
    gatt, gated, gp, table = refs[11:15]
    parts = [s[...] for s in stats]
    mean = (parts[0][0:1] + parts[1][0:1] + parts[2][0:1] + parts[3][0:1]) * 0.25
    m2 = jnp.zeros_like(mean)
    g1 = jnp.zeros_like(mean)
    ga = jnp.zeros_like(mean)
    for p in parts:
        off = p[0:1] - mean
        m2 = m2 + p[1:2] + BLK * off * off
        g1 = g1 + p[2:3]
        ga = ga + p[3:4] + off * p[2:3]
    inv = lax.rsqrt(m2 / D + 1e-6)
    row = lax.broadcasted_iota(jnp.int32, (DH, GRP), 0)
    cols = jnp.where(row == 0, mean, jnp.where(row == 1, inv, jnp.where(row == 2, g1 / D, ga * inv / D)))
    table[...] = cols.T
    for k in range(NB):
        at = rows(lax.rem(info[9] + k, NB))
        t = table[at, :]
        mean_c, inv_c, g1_c, ga_c = (t[:, n : n + 1] for n in range(4))
        normed = (att[at, :] - mean_c) * inv_c
        g = gate[at, :].astype(F32)
        grad_gated = gg[at, :].astype(F32)
        gatt[at, :] = (inv_c * (grad_gated * g - g1_c - normed * ga_c)).astype(BF16)
        gated[at, :] = (normed * g).astype(BF16)
        gp[at, :] = (grad_gated * normed * dsig[k][:, 0:BLK].astype(F32)).astype(BF16)


def pack(info, x, total, lanes, send, keep):
    first = info[10] == 0
    send[x, :, lanes] = jnp.where(first, total[128:], total[:128]).astype(BF16)
    keep[x, :, lanes] = jnp.where(first, total[:128], total[128:])


def early_weights_body(info, *refs):
    ev, (gp_g, gp_q, send, keep) = refs[0:4], refs[4:8]
    for lanes, gp in ((slice(0, BLK), gp_g), (slice(BLK, 2 * BLK), gp_q)):
        for x in range(4):
            part = [
                tn(ev[k][:, x * BLK : (x + 1) * BLK], gp[rows(lax.rem(info[9] + k, NB)), :]) for k in range(NB)
            ]
            pack(info, x, part[0] + part[1] + part[2] + part[3], lanes, send, keep)


def late_weights_body(info, *refs):
    ev, gp = refs[0:4], refs[4:8]
    send, keep = refs[8:10]
    for n in range(2):
        lanes, cols = slice(n * BLK, (n + 1) * BLK), slice((n + 2) * BLK, (n + 3) * BLK)
        for x in range(4):
            part = [tn(ev[k][:, x * BLK : (x + 1) * BLK], gp[k][:, cols]) for k in range(NB)]
            pack(info, x, part[0] + part[1] + part[2] + part[3], lanes, send, keep)


def out_weights_body(info, *refs):
    gated, (cot, send, keep) = refs[0:4], refs[4:7]
    part = [tn(gated[k][...], cot[...]) for k in range(NB)]
    for k in range(NB):
        pack(info, lax.rem(info[9] + k, NB), part[k], slice(0, BLK), send, keep)


def add_core_body(keep_1, keep_2, keep_3, got_1, got_2, got_3, out):
    out[:, :, 0:512] = (keep_1[...] + got_1[...].astype(F32)).astype(BF16)
    out[:, :, 512:1024] = (keep_2[...] + got_2[...].astype(F32)).astype(BF16)
    out[:, :, 1024:] = (keep_3[...] + got_3[...].astype(F32)).astype(BF16)


def add_xy_body(got, total):
    part = got[0].astype(F32)
    for xy in range(1, 16):
        part = part + got[xy].astype(F32)
    total[...] = part.astype(BF16)


def last_body(got, grad_w_in, grad_w_out):
    for z in range(4):
        part = got[z]
        for n, to in enumerate((0, 2, 1, 3)):
            at = to * D + z * BLK
            grad_w_in[:, at : at + BLK] = part[:, n * BLK : (n + 1) * BLK]
        grad_w_out[:, z * BLK : (z + 1) * BLK] = part[:, 4 * BLK :]


def silu_parts(u):
    t = jnp.tanh(u)
    a = 1.0 + t
    ut = u * t
    return u + ut, a * ((1.0 + u) - ut)


def key_side(q, g, kv, dkv, dq, i, j, keep):
    two = range(2)
    half = keep * 0.5
    qi = [q[rows(i), head(h)] for h in two]
    gi = [g[rows(i), head(h)] for h in two]
    kj = [kv[rows(j), head(h)] for h in two]
    vj = [kv[rows(j), head(h, BLK)] for h in two]
    u = [nt(kj[h], qi[h]) for h in two]
    dw = [nt(vj[h], gi[h]) for h in two]
    parts = [silu_parts(u[h]) for h in two]
    w = [(parts[h][0] * keep).astype(BF16) for h in two]
    ds = [(dw[h] * parts[h][1] * half).astype(BF16) for h in two]
    dv = [nn(w[h], gi[h]) for h in two]
    dk = [nn(ds[h], qi[h]) for h in two]
    dqi = [tn(ds[h], kj[h]) for h in two] if dq is not None else None
    for h in two:
        dkv[rows(j), head(h, BLK)] += dv[h]
        dkv[rows(j), head(h)] += dk[h]
        if dq is not None:
            dq[rows(i), head(h)] += dqi[h]


def query_side(q, g, kv, dq, i, j, keep):
    two = range(2)
    half = keep * 0.5
    qi = [q[rows(i), head(h)] for h in two]
    gi = [g[rows(i), head(h)] for h in two]
    kj = [kv[rows(j), head(h)] for h in two]
    vj = [kv[rows(j), head(h, BLK)] for h in two]
    slope = [silu_parts(nt(qi[h], kj[h]))[1] for h in two]
    dw = [nt(gi[h], vj[h]) for h in two]
    ds = [(dw[h] * slope[h] * half).astype(BF16) for h in two]
    dqi = [nn(ds[h], kj[h]) for h in two]
    for h in two:
        dq[rows(i), head(h)] += dqi[h]


def backward_local_body(info, *refs):
    q, g, kv, kv_prev = refs[0:4]
    dsig = refs[4:8]
    gp_q, dkv, dq = refs[8:11]
    ends = history_ends(info)
    base = info[8] * GRP
    prev = base - GRP
    dq[...] = jnp.zeros_like(dq)
    dkv[...] = jnp.zeros_like(dkv)

    def over_j(j, _):
        kpos = base + j * BLK
        last = jnp.minimum((end_of(kpos + BLK - 1, ends) - 1 - base) // BLK, NB - 1)

        def over_i(i, _):
            key_side(q, g, kv, dkv, dq, i, j, keep_cols(base + i * BLK, kpos, ends))
            return 0

        return lax.fori_loop(j, last + 1, over_i, 0)

    lax.fori_loop(0, NB, over_j, 0)

    def halo_i(i, _):
        qpos = base + i * BLK

        def halo_j(j, _):
            query_side(q, g, kv_prev, dq, i, j, keep_rows(qpos, prev + j * BLK, ends))
            return 0

        return lax.fori_loop(halo_first(i, qpos, prev, ends), NB, halo_j, 0)

    lax.fori_loop(0, NB, halo_i, 0)
    for k in range(NB):
        at = rows(lax.rem(info[9] + k, NB))
        gp_q[at, :] = (dq[at, :] * dsig[k][:, 2 * BLK : 3 * BLK].astype(F32)).astype(BF16)


def backward_later_body(info, *refs):
    q, g, kv, dkv_in, gp_g, gp_q = refs[0:6]
    dsig, gp = refs[6:10], refs[10:14]
    dkv = refs[14]
    ends = history_ends(info)
    base = info[8] * GRP
    later = base + GRP
    dkv[...] = dkv_in[...]

    def over_j(j, _):
        kpos = base + j * BLK
        end = end_of(kpos + BLK - 1, ends)
        count = jnp.where(end > later, jnp.minimum((end - 1 - later) // BLK, j) + 1, 0)

        def over_i(i, _):
            key_side(q, g, kv, dkv, None, i, j, keep_cols(later + i * BLK, kpos, ends))
            return 0

        return lax.fori_loop(0, count, over_i, 0)

    lax.fori_loop(0, NB, over_j, 0)
    for k in range(NB):
        at = rows(lax.rem(info[9] + k, NB))
        dk = 2.0 * dkv[at, 0:BLK]
        gp[k][:, :BLK] = gp_g[at, :]
        gp[k][:, BLK : 2 * BLK] = gp_q[at, :]
        gp[k][:, 2 * BLK : 3 * BLK] = (dkv[at, BLK:] * dsig[k][:, BLK : 2 * BLK].astype(F32)).astype(BF16)
        gp[k][:, 3 * BLK :] = (dk * dsig[k][:, 3 * BLK :].astype(F32)).astype(BF16)


def input_body(info, *refs):
    gp, (w, cot), outs = refs[0:4], refs[4:6], refs[6:10]
    for k in range(NB):
        total = cot[...].astype(F32) if k == 0 else None
        for n, part in enumerate((0, 2, 1, 3)):
            lanes = pl.ds(pl.multiple_of(part * D + info[9] * BLK, BLK), BLK)
            term = nt(gp[k][:, n * BLK : (n + 1) * BLK], w[:, lanes])
            total = term if total is None else total + term
        outs[k][...] = total.astype(outs[k].dtype)


def add_rows_body(own, got_1, got_2, got_3, out):
    total = own[...] + got_1[...].astype(F32) + got_2[...].astype(F32) + got_3[...].astype(F32)
    out[...] = total.astype(BF16)


def along(x, axis, d):
    return lax.ppermute(x, axis, [(i, (i + d) % 4) for i in range(4)])


def swap(x):
    return lax.ppermute(x, "c", [(0, 1), (1, 0)])


def gather_z(x):
    return [x, along(x, "z", -1), along(x, "z", 2), along(x, "z", 1)]


def exchange(parts, axis):
    return [parts[0]] + [along(parts[d], axis, d) for d in (1, 2, 3)]


def f32(shape):
    return jax.ShapeDtypeStruct(shape, F32)


def bf16(shape):
    return jax.ShapeDtypeStruct(shape, BF16)


def body(events, cotangent, hist, w_in, w_out):
    z = lax.axis_index("z")
    info = jnp.concatenate(
        [hist[0], jnp.stack([lax.axis_index("y"), z, lax.axis_index("c"), lax.axis_index("x")]).astype(jnp.int32)]
    )
    ev, cot = events[0], cotangent[0]
    near = along(ev, "z", -1), along(ev, "z", 1)
    evs = [ev, near[0], None, near[1]]
    kvs, qs, gs, dsigs, kv_prevs = [], [], [], [None] * 4, []
    for blocks in ((0,), (1, 3), (2,)):
        n = len(blocks)
        if blocks == (1, 3):
            ev_far, *near, _ = lax.optimization_barrier((ev, *near, kvs[0]))
            evs = [ev, near[0], along(ev_far, "z", 2), near[1]]
        kv, q, g, *dsig = call(
            project_body,
            (bf16((n * BLK, 2 * BLK)), bf16((n * BLK, BLK)), bf16((n * BLK, BLK))) + (bf16((BLK, 4 * BLK)),) * n,
            n + 1, 1 << 20, 1 << 20,
        )(info, *[evs[b] for b in blocks], w_in)
        kvs.append(kv)
        qs.append(q)
        gs.append(g)
        for b, d in zip(blocks, dsig):
            dsigs[b] = d
        kv_prevs.append(along(kv, "y", 1))
    ggs = call(grad_gated_body, (bf16((BLK, 2 * BLK)),) * 4, 2, 1 << 20, 1 << 20)(info, cot, w_out)
    *ggs, _ = lax.optimization_barrier((*ggs, kvs[1]))
    ggs = exchange(ggs, "z")
    q, kv, att = call(
        forward_local_body, (bf16((GRP, BLK)), bf16((GRP, 2 * BLK)), f32((GRP, BLK))), 6, 5 << 30, 4 << 20
    )(info, *qs, *kvs)
    q_next = along(q, "y", -1)
    att, kv_prev, gg, cot_z, gate, stats = call(
        forward_halo_body,
        (f32((GRP, BLK)), bf16((GRP, 2 * BLK))) + (bf16((GRP, BLK)),) * 3 + (f32((8, GRP)),),
        12, 5 << 30, 4 << 20,
    )(info, q, att, *ggs, *kv_prevs, *gs)
    gatt, gated, gp_g = call(
        norm_body, (bf16((GRP, BLK)),) * 3, 11, 1 << 30, 4 << 20, [pltpu.VMEM((GRP, DH), F32)]
    )(info, att, gg, gate, *gather_z(stats), *dsigs)
    g_next = along(gatt, "y", -1)
    gateds = gather_z(gated)
    gp_q, dkv = call(
        backward_local_body, (bf16((GRP, BLK)), f32((GRP, 2 * BLK))), 8, 1 << 20, 1 << 20,
        [pltpu.VMEM((GRP, BLK), F32)],
    )(info, q, gatt, kv, kv_prev, *dsigs)
    def weights(kernel, cols, operands):
        send, keep = call(
            kernel, (bf16((4, 128, cols)), f32((4, 128, cols))), len(operands), 1 << 20, 1 << 20
        )(info, *operands)
        return swap(send), keep

    got_1, keep_1 = weights(early_weights_body, 512, (*evs, gp_g, gp_q))
    q_next, g_next, keep_1 = lax.optimization_barrier((q_next, g_next, keep_1))
    gp = call(
        backward_later_body, (bf16((BLK, 4 * BLK)),) * 4, 10, 5 << 30, 4 << 20, [pltpu.VMEM((GRP, 2 * BLK), F32)]
    )(info, q_next, g_next, kv, dkv, gp_g, gp_q, *dsigs)
    got_2, keep_2 = weights(late_weights_body, 512, (*evs, *gp))
    *partial, = call(
        input_body, (f32((BLK, D)),) + (bf16((BLK, D)),) * 3, 6, 1 << 20, 1 << 20
    )(info, *gp, w_in, cot)
    cot_z, keep_2, partial[0] = lax.optimization_barrier((cot_z, keep_2, partial[0]))
    partial = exchange(partial, "z")
    got_3, keep_3 = weights(out_weights_body, 256, (*gateds, cot_z))
    mine = call(
        add_core_body, bf16((4, 128, 5 * BLK)), 6, 1 << 20, 1 << 20, scalars=0
    )(keep_1, keep_2, keep_3, got_1, got_2, got_3)
    sums = lax.all_to_all(mine.reshape(16, 32, 5 * BLK), ("x", "y"), 0, 0)
    total = call(add_xy_body, bf16((32, 5 * BLK)), 1, 1 << 20, 1 << 20, scalars=0)(sums)
    _, own_rows = lax.optimization_barrier((total, partial[0]))
    block = pl.BlockSpec((BLK // 4, D), lambda i: (i, 0))
    grad_events = pl.pallas_call(
        add_rows_body,
        grid=(4,),
        out_shape=bf16((BLK, D)),
        in_specs=[block] * 4,
        out_specs=block,
        compiler_params=pltpu.CompilerParams(vmem_limit_bytes=20 * 1024 * 1024),
        cost_estimate=pl.CostEstimate(flops=1 << 20, bytes_accessed=4 << 20, transcendentals=0),
    )(own_rows, *partial[1:])
    got = lax.all_to_all(total.reshape(4, 8, 5 * BLK), "z", 0, 0)
    grad_w_in, grad_w_out = call(
        last_body, (bf16((8, 4 * D)), bf16((8, D))), 1, 1 << 20, 1 << 20, scalars=0
    )(got)
    return grad_events[None], grad_w_in, grad_w_out


def solution(mesh):
    axes = ("x", "c", "y", "z")
    split = Mesh(mesh.devices.reshape(4, 2, 4, 4), axes)
    dp, seq = ("x", "c"), ("y", "z")
    return jax.shard_map(
        body,
        mesh=split,
        in_specs=(P(dp, seq, None), P(dp, seq, None), P(dp, None), P(), P()),
        out_specs=(P(dp, seq, None), P(axes, None), P(axes, None)),
        check_vma=False,
    )
```
